32 devices in a mesh: dp: 16 (over z, y, x), tensor: 2 (over core).
Axes of the slice: x: 2, y: 2, z: 4, core: 2. Of those that a mesh axis runs over, the one named last changes fastest.
Arguments:
- inputs: bfloat16 [40960, 512], P(('dp', 'tensor')), may hold values from -6 to 6
- cotangent: bfloat16 [40960, 512], P(('dp', 'tensor')), may hold values from -6 to 6
- timesteps: int32 [160], P('dp'), may hold values from 0 to 999
- item_scale: float32 [160], P('dp'), may hold values from 0.5 to 2
- qkv_weight: float32 [2, 512, 3, 512], P(None, 'dp', None, 'tensor'), may hold values from -0.25 to 0.25
- qkv_first: float32 [2, 512, 3, 512], P(None, 'dp', None, 'tensor'), may hold values from -256 to 256
- qkv_second: float32 [2, 512, 3, 512], P(None, 'dp', None, 'tensor'), may hold values from 819.2 to 13107.2
- out_weight: float32 [2, 512, 512], P(None, 'tensor', 'dp'), may hold values from -1 to 1
- out_first: float32 [2, 512, 512], P(None, 'tensor', 'dp'), may hold values from -256 to 256
- out_second: float32 [2, 512, 512], P(None, 'tensor', 'dp'), may hold values from 819.2 to 13107.2
- up_weight: float32 [2, 512, 2048], P(None, 'dp', 'tensor'), may hold values from -0.25 to 0.25
- up_first: float32 [2, 512, 2048], P(None, 'dp', 'tensor'), may hold values from -384 to 384
- up_second: float32 [2, 512, 2048], P(None, 'dp', 'tensor'), may hold values from 1843.2 to 29491.2
- up_bias: float32 [2, 16, 128], P(None, 'tensor', 'dp'), may hold values from -3 to 3
- bias_first: float32 [2, 16, 128], P(None, 'tensor', 'dp'), may hold values from -384 to 384
- bias_second: float32 [2, 16, 128], P(None, 'tensor', 'dp'), may hold values from 1843.2 to 29491.2
- down_weight: float32 [2, 2048, 512], P(None, 'tensor', 'dp'), may hold values from -0.125 to 0.125
- down_first: float32 [2, 2048, 512], P(None, 'tensor', 'dp'), may hold values from -512 to 512
- down_second: float32 [2, 2048, 512], P(None, 'tensor', 'dp'), may hold values from 3276.8 to 52428.8
- norm_params: float32 [2, 5, 512], P(None, None, ('dp', 'tensor')), may hold values from -1.2 to 1.4, as said below
- norm_first: float32 [2, 5, 512], P(None, None, ('dp', 'tensor')), may hold values from -1280 to 1280
- norm_second: float32 [2, 5, 512], P(None, None, ('dp', 'tensor')), may hold values from 20480 to 327680
- time_weight: float32 [2, 512, 512], P(None, ('dp', 'tensor')), may hold values from -0.25 to 0.25
- time_first: float32 [2, 512, 512], P(None, ('dp', 'tensor')), may hold values from -896 to 896
- time_second: float32 [2, 512, 512], P(None, ('dp', 'tensor')), may hold values from 10035.2 to 160563.2
Outputs:
- activations: bfloat16 [40960, 512], P(('dp', 'tensor'))
- input_grad: bfloat16 [40960, 512], P(('dp', 'tensor'))
- new_qkv_weight: float32 [2, 512, 3, 512], P(None, 'dp', None, 'tensor')
- new_qkv_first: float32 [2, 512, 3, 512], P(None, 'dp', None, 'tensor')
- new_qkv_second: float32 [2, 512, 2, 512], P(None, 'dp', None, 'tensor')
- new_value_second: float32 [2, 512, 512], P(None, 'dp', 'tensor')
- new_out_weight: float32 [2, 512, 512], P(None, 'tensor', 'dp')
- new_out_first: float32 [2, 512, 512], P(None, 'tensor', 'dp')
- new_out_second: float32 [2, 512, 512], P(None, 'tensor', 'dp')
- new_up_weight: float32 [2, 512, 2048], P(None, 'dp', 'tensor')
- new_up_first: float32 [2, 512, 2048], P(None, 'dp', 'tensor')
- new_up_second: float32 [2, 512, 2048], P(None, 'dp', 'tensor')
- new_up_bias: float32 [2, 16, 128], P(None, 'tensor', 'dp')
- new_bias_first: float32 [2, 16, 128], P(None, 'tensor', 'dp')
- new_bias_second: float32 [2, 16, 128], P(None, 'tensor', 'dp')
- new_down_weight: float32 [2, 2048, 512], P(None, 'tensor', 'dp')
- new_down_first: float32 [2, 2048, 512], P(None, 'tensor', 'dp')
- new_down_second: float32 [2, 2048, 512], P(None, 'tensor', 'dp')
- new_norm_params: float32 [2, 5, 512], P(None, None, ('dp', 'tensor'))
- new_norm_first: float32 [2, 5, 512], P(None, None, ('dp', 'tensor'))
- new_norm_second: float32 [2, 5, 512], P(None, None, ('dp', 'tensor'))
- new_time_weight: float32 [2, 512, 512], P(None, ('dp', 'tensor'))
- new_time_first: float32 [2, 512, 512], P(None, ('dp', 'tensor'))
- new_time_second: float32 [2, 512, 512], P(None, ('dp', 'tensor'))
The draws below stay inside these ranges and needn't reach their ends.
Inputs may be any that keep to these rules, and one draw needn't show every extreme that they name: `norm_params`: rows 0 and 2 of each layer are gains, rows 1, 3 and 4 shifts and a bias.
All inputs are finite; a program needn't handle non-finite values.
Results may differ from the reference program's by a relative error of at most 0.018.
Values may be sent and summed in bfloat16 or wider, within the bound.
A program may use at most 256 MiB of HBM per device.

```python
import math
import jax
import jax.numpy as jnp
from jax import lax

D = 512
HEADS = 8
HEAD_DIM = 64
FF = 2048
TE = 512
LENGTH = 256
LAYERS = 2
STEP = 8
TSTEPS = 1000
BIAS_ROW = 128
ITEMS = 160
TOKENS = 40960


def draw_norm_params(key, part):
    key = jax.random.fold_in(key, 11)
    gain_key, shift_key = jax.random.split(key)
    gains = jax.random.uniform(gain_key, (LAYERS, 5, D), jnp.float32, 0.6, 1.4)
    shifts = jnp.clip(0.3 * jax.random.normal(shift_key, (LAYERS, 5, D), jnp.float32), -1.2, 1.2)
    row_ids = jnp.arange(5)
    is_gain = (row_ids == 0) | (row_ids == 2)
    return jnp.where(is_gain[None, :, None], gains, shifts)


def plant(result, key, low, top_value):
    dims = result.shape
    place = [jax.random.randint(jax.random.fold_in(key, axis), (), 0, dims[axis]) for axis in range(len(dims))]
    result = result.at[tuple(place)].set(low)
    longest = dims.index(max(dims))
    place[longest] = (place[longest] + 1) % dims[longest]
    return result.at[tuple(place)].set(top_value)


def block_levels(stream_key, extent, cuts, low, top_value):
    level = 1.0
    for position, parts in cuts:
        steps = jax.random.uniform(jax.random.fold_in(jax.random.fold_in(stream_key, 6), position), (parts,), jnp.float32, low / len(cuts), top_value / len(cuts))
        level = level * jnp.repeat(jnp.exp(steps), extent[position] // parts).reshape((-1,) + (1,) * (len(extent) - 1 - position))
    return level


def noise(own_key, extent, deviation, limit, shards=(), kind=jnp.bfloat16):
    level = block_levels(own_key, extent, shards, -0.22, 0.18) if shards else 1.0
    values = jax.random.normal(own_key, extent, jnp.float32) * deviation * level
    return jnp.minimum(jnp.maximum(values, -limit), limit).astype(kind)


def setup_inputs(seed: int = 0) -> dict:
    keys = jax.random.split(jax.random.key(seed), 26)
    inputs = noise(keys[0], (TOKENS, D), 1.0, 6.0, ((0, 32),))
    cotangent = noise(keys[1], (TOKENS, D), 1.0, 6.0, ((0, 32),))
    timesteps = plant(jax.random.randint(keys[2], (ITEMS,), 0, TSTEPS), jax.random.fold_in(keys[2], 1), 0, TSTEPS - 1).astype(jnp.int32)
    item_scale = jnp.clip(jnp.exp(math.log(2.0) - 1.3862944 * jax.random.uniform(keys[3], (ITEMS,), jnp.float32) ** block_levels(keys[3], (ITEMS,), ((0, 16),), -0.2, 0.2)), 0.5, 2.0)
    qkv_weight = noise(keys[4], (LAYERS, D, 3, D), D ** -0.5, 0.25, ((1, 16), (3, 2)), jnp.float32)
    qkv_first = noise(keys[5], (LAYERS, D, 3, D), (0.2 * TOKENS ** 0.5), 256.0, ((1, 16), (3, 2)), jnp.float32)
    qkv_second = jnp.clip(jnp.exp(math.log(13107.2) - 2.7725887 * jax.random.uniform(keys[6], (LAYERS, D, 3, D), jnp.float32) ** block_levels(keys[6], (LAYERS, D, 3, D), ((1, 16), (3, 2)), -0.2, 0.2)), 819.2, 13107.2)
    out_weight = noise(keys[7], (LAYERS, D, D), (D // 16) ** -0.5, 1.0, ((1, 2), (2, 16)), jnp.float32)
    out_first = noise(keys[8], (LAYERS, D, D), (0.2 * TOKENS ** 0.5), 256.0, ((1, 2), (2, 16)), jnp.float32)
    out_second = jnp.clip(jnp.exp(math.log(13107.2) - 2.7725887 * jax.random.uniform(keys[9], (LAYERS, D, D), jnp.float32) ** block_levels(keys[9], (LAYERS, D, D), ((1, 2), (2, 16)), -0.2, 0.2)), 819.2, 13107.2)
    up_weight = noise(keys[10], (LAYERS, D, FF), D ** -0.5, 0.25, ((1, 16), (2, 2)), jnp.float32)
    up_first = noise(keys[11], (LAYERS, D, FF), (0.3 * TOKENS ** 0.5), 384.0, ((1, 16), (2, 2)), jnp.float32)
    up_second = jnp.clip(jnp.exp(math.log(29491.2) - 2.7725887 * jax.random.uniform(keys[12], (LAYERS, D, FF), jnp.float32) ** block_levels(keys[12], (LAYERS, D, FF), ((1, 16), (2, 2)), -0.2, 0.2)), 1843.2, 29491.2)
    up_bias = noise(keys[13], (LAYERS, FF // BIAS_ROW, BIAS_ROW), 0.5, 3.0, ((1, 2), (2, 16)), jnp.float32)
    bias_first = noise(keys[14], (LAYERS, FF // BIAS_ROW, BIAS_ROW), (0.3 * TOKENS ** 0.5), 384.0, ((1, 2), (2, 16)), jnp.float32)
    bias_second = jnp.clip(jnp.exp(math.log(29491.2) - 2.7725887 * jax.random.uniform(keys[15], (LAYERS, FF // BIAS_ROW, BIAS_ROW), jnp.float32) ** block_levels(keys[15], (LAYERS, FF // BIAS_ROW, BIAS_ROW), ((1, 2), (2, 16)), -0.2, 0.2)), 1843.2, 29491.2)
    down_weight = noise(keys[16], (LAYERS, FF, D), FF ** -0.5, 0.125, ((1, 2), (2, 16)), jnp.float32)
    down_first = noise(keys[17], (LAYERS, FF, D), (0.4 * TOKENS ** 0.5), 512.0, ((1, 2), (2, 16)), jnp.float32)
    down_second = jnp.clip(jnp.exp(math.log(52428.8) - 2.7725887 * jax.random.uniform(keys[18], (LAYERS, FF, D), jnp.float32) ** block_levels(keys[18], (LAYERS, FF, D), ((1, 2), (2, 16)), -0.2, 0.2)), 3276.8, 52428.8)
    norm_params = draw_norm_params(jax.random.fold_in(keys[25], 71), 0)
    norm_first = noise(keys[20], (LAYERS, 5, D), (TOKENS ** 0.5), 1280.0, ((2, 32),), jnp.float32)
    norm_second = jnp.clip(jnp.exp(math.log(327680.0) - 2.7725887 * jax.random.uniform(keys[21], (LAYERS, 5, D), jnp.float32) ** block_levels(keys[21], (LAYERS, 5, D), ((2, 32),), -0.2, 0.2)), 20480.0, 327680.0)
    time_weight = noise(keys[22], (LAYERS, TE, D), TE ** -0.5, 0.25, ((1, 32),), jnp.float32)
    time_first = noise(keys[23], (LAYERS, TE, D), (0.7 * TOKENS ** 0.5), 896.0, ((1, 32),), jnp.float32)
    time_second = jnp.clip(jnp.exp(math.log(160563.2) - 2.7725887 * jax.random.uniform(keys[24], (LAYERS, TE, D), jnp.float32) ** block_levels(keys[24], (LAYERS, TE, D), ((1, 32),), -0.2, 0.2)), 10035.2, 160563.2)
    return dict(inputs=inputs, cotangent=cotangent, timesteps=timesteps, item_scale=item_scale, qkv_weight=qkv_weight, qkv_first=qkv_first, qkv_second=qkv_second, out_weight=out_weight, out_first=out_first, out_second=out_second, up_weight=up_weight, up_first=up_first, up_second=up_second, up_bias=up_bias, bias_first=bias_first, bias_second=bias_second, down_weight=down_weight, down_first=down_first, down_second=down_second, norm_params=norm_params, norm_first=norm_first, norm_second=norm_second, time_weight=time_weight, time_first=time_first, time_second=time_second)


@jax.custom_vjp
def low(v):
    return lax.optimization_barrier(v.astype(jnp.bfloat16)).astype(jnp.float32)

@jax.custom_vjp
def low_back(v):
    return v

def low_keep(v):
    return (low(v), None)

def low_pass(kept, grad):
    return (grad,)

def back_keep(v):
    return (v, None)

def back_low(kept, grad):
    return (low(grad),)
low.defvjp(low_keep, low_pass)
low_back.defvjp(back_keep, back_low)
highest = lax.Precision.HIGHEST
beta_first = 0.5
beta_second = 0.5
learn_rate = 0.1
norm_rate = 0.4
weight_decay = 0.01
adam_eps = 1e-08
norm_eps = 1e-05

def matmul_high(left, right):
    return jnp.dot(left, right, precision=highest, preferred_element_type=jnp.float32)

def layer_norm(values, gain, shift):
    center = values - lax.optimization_barrier(jnp.mean(values, -1, keepdims=True))
    spread = lax.optimization_barrier(jnp.mean(center * center, -1, keepdims=True))
    return center * lax.rsqrt(spread + norm_eps) * gain + shift

def time_features(steps_in):
    half_width = TE // 2
    frequency = jnp.exp(-math.log(10000.0) / half_width * jnp.arange(half_width).astype(jnp.float32))
    angles = steps_in.astype(jnp.float32)[:, None] * frequency[None, :]
    return jnp.concatenate([jnp.sin(angles), jnp.cos(angles)], 1)

def gelu_exact(values):
    return jax.nn.gelu(values, approximate=False)

def attend_block(block):
    query_mat, key_mat, value_mat = block
    scores = jnp.einsum('snhd,smhd->shnm', query_mat, key_mat, precision=highest) * HEAD_DIM ** (-0.5)
    scores = low_back(scores)
    attn_probs = low(jax.nn.softmax(scores, axis=-1))
    return jnp.einsum('shnm,smhd->snhd', attn_probs, value_mat, precision=highest)

def forward(weights, stream, time_feats):
    qkv_w, out_w, up_w, up_b, down_w, norms, time_w = weights
    items_all = stream.shape[0] // LENGTH
    group_size = math.gcd(items_all, max(1, 4096 // LENGTH))
    group_count = items_all // group_size
    for layer_index in range(LAYERS):
        shift_rows = matmul_high(time_feats, time_w[layer_index])
        stream = (stream.reshape(items_all, LENGTH, D) + shift_rows[:, None, :]).reshape(items_all * LENGTH, D)
        normed = low(layer_norm(stream, norms[layer_index, 0], norms[layer_index, 1]))
        proj_w = low(qkv_w[layer_index])
        shaped = []
        for slot_index in range(3):
            projected = low(low_back(matmul_high(normed, proj_w[:, slot_index, :])))
            shaped.append(projected.reshape(group_count, group_size, LENGTH, HEADS, HEAD_DIM))
        mixed = lax.map(jax.checkpoint(attend_block), (shaped[0], shaped[1], shaped[2]))
        mixed = low(low_back(mixed.reshape(items_all * LENGTH, D)))
        stream = stream + low_back(matmul_high(mixed, low(out_w[layer_index])))
        normed_ffn = low(layer_norm(stream, norms[layer_index, 2], norms[layer_index, 3]))
        pre_act = low_back(matmul_high(normed_ffn, low(up_w[layer_index])) + low(up_b[layer_index]).reshape(FF))
        hidden = low(gelu_exact(pre_act))
        stream = stream + low_back(matmul_high(hidden, low(down_w[layer_index]))) + norms[layer_index, 4]
    return stream

def adamw(weight, gradient, first_moment, second_moment, rate):
    first_new = beta_first * first_moment + (1.0 - beta_first) * gradient
    second_new = beta_second * second_moment + (1.0 - beta_second) * gradient * gradient
    first_corr = first_new / (1.0 - beta_first ** STEP)
    second_corr = second_new / (1.0 - beta_second ** STEP)
    weight_new = weight - rate * (first_corr / (jnp.sqrt(second_corr) + adam_eps) + weight_decay * weight)
    return [weight_new, first_new, second_new]

def reference(inputs, cotangent, timesteps, item_scale, qkv_weight, qkv_first, qkv_second, out_weight, out_first, out_second, up_weight, up_first, up_second, up_bias, bias_first, bias_second, down_weight, down_first, down_second, norm_params, norm_first, norm_second, time_weight, time_first, time_second):
    time_feats = time_features(timesteps)
    params = (qkv_weight, out_weight, up_weight, up_bias, down_weight, norm_params, time_weight)
    start_rows = inputs.astype(jnp.float32)
    final, pull = jax.vjp(lambda weights, stream: forward(weights, stream, time_feats), params, start_rows)
    start_grad = (cotangent.astype(jnp.float32).reshape(ITEMS, LENGTH, D) * item_scale[:, None, None]).reshape(TOKENS, D)
    grads, grad_rows = pull(start_grad)
    firsts = (qkv_first, out_first, up_first, bias_first, down_first, norm_first, time_first)
    seconds = (qkv_second, out_second, up_second, bias_second, down_second, norm_second, time_second)
    rates = (learn_rate, learn_rate, learn_rate, learn_rate, learn_rate, norm_rate, learn_rate)
    updated = []
    for kind_index in range(7):
        updated.extend(adamw(params[kind_index], grads[kind_index], firsts[kind_index], seconds[kind_index], rates[kind_index]))
    return (final.astype(jnp.bfloat16), grad_rows.astype(jnp.bfloat16), updated[0], updated[1], updated[2][:, :, :2], updated[2][:, :, 2], updated[3], updated[4], updated[5], updated[6], updated[7], updated[8], updated[9], updated[10], updated[11], updated[12], updated[13], updated[14], updated[15], updated[16], updated[17], updated[18], updated[19], updated[20])
```

```python
import functools
import math

import jax
import jax.numpy as jnp
import numpy as np
from jax import lax
from jax.experimental import pallas as pl
from jax.experimental.pallas import tpu as pltpu
from jax.sharding import PartitionSpec as P

HEAD_DIM = 64
LENGTH = 256
LAYERS = 2
STEP = 8
GROUPS = 16
MESH = pl.DeviceIdType.MESH
F32 = jnp.float32
BF16 = jnp.bfloat16

beta_first = 0.5
beta_second = 0.5
learn_rate = 0.1
norm_rate = 0.4
weight_decay = 0.01
adam_eps = 1e-08
norm_eps = 1e-05


def nn(a, b):
    return lax.dot_general(a, b, (((1,), (0,)), ((), ())), preferred_element_type=F32)


def nt(a, b):
    return lax.dot_general(a, b, (((1,), (1,)), ((), ())), preferred_element_type=F32)


def tn(a, b):
    return lax.dot_general(a, b, (((0,), (0,)), ((), ())), preferred_element_type=F32)


def normalize(values):
    center = values - jnp.mean(values, -1, keepdims=True)
    inverse = lax.rsqrt(jnp.mean(center * center, -1, keepdims=True) + norm_eps)
    return center * inverse, inverse


def fold_rows(values):
    rows, cols = values.shape
    return jnp.sum(values.reshape(rows // 8, 8, cols), 0)


def gelu_and_slope(x):
    size = jnp.abs(x)
    denom = 1.0 + (0.3275911 / math.sqrt(2.0)) * size
    t = pl.reciprocal(denom, approx=True)
    t = t * (2.0 - denom * t)
    bell = jnp.exp(x * x * -0.5)
    poly = 0.5 * 1.061405429
    poly = poly * t + 0.5 * -1.453152027
    poly = poly * t + 0.5 * 1.421413741
    poly = poly * t + 0.5 * -0.284496736
    poly = poly * t + 0.5 * 0.254829592
    tail = poly * t * bell
    below = jnp.where(x >= 0.0, 1.0 - tail, tail)
    return x * below, below + x * bell * (1.0 / math.sqrt(2.0 * math.pi))


class Place:
    def __init__(self, rep):
        dp = lax.axis_index("dp")
        self.rep = rep
        self.copy = dp % rep
        self.group = dp // rep
        self.t = lax.axis_index("tensor")
        self.z = self.group // 4
        self.yx = self.group % 4
        x, y = self.yx % 2, self.yx // 2
        self.yx_x = self.yx + 1 - 2 * x
        self.yx_y = self.yx + 2 - 4 * y
        self.yx_d = 3 - self.yx
        self.cols = pl.ds(pl.multiple_of(self.t * 256, 256), 256)
        self.other_cols = pl.ds(pl.multiple_of((1 - self.t) * 256, 256), 256)

    def device(self, z, yx, t):
        return ((z * 4 + yx) * self.rep + self.copy, t)

    def z_ahead(self, k):
        return (self.z + k) % 4

    @property
    def partners(self):
        return [self.device(self.z_ahead(k), self.yx, self.t) for k in (1, 2, 3)] + [
            self.device(self.z, self.yx_x, self.t),
            self.device(self.z, self.yx_y, self.t),
            self.device(self.z, self.yx, 1 - self.t),
        ]

    def greet(self):
        barrier = pltpu.get_barrier_semaphore()
        for partner in self.partners:
            pl.semaphore_signal(barrier, inc=1, device_id=partner, device_id_type=MESH)
        pl.semaphore_wait(barrier, len(self.partners))


class Gather:
    def __init__(self, place, view, core_view, send, recv):
        self.place, self.view, self.core_view, self.send, self.recv = place, view, core_view, send, recv
        self.copies = {}

    def start(self, slot, ref, device):
        copy = pltpu.make_async_remote_copy(
            src_ref=ref, dst_ref=ref, send_sem=self.send.at[slot], recv_sem=self.recv.at[slot],
            device_id=device, device_id_type=MESH,
        )
        copy.start()
        self.copies[slot] = copy

    def step(self, number):
        p = self.place
        if number == 0:
            for k in (1, 2, 3):
                self.start(k - 1, self.view(p.z, p.yx), p.device(p.z_ahead(k), p.yx, p.t))
        elif number == 1:
            for slot in (0, 1, 2):
                self.copies[slot].wait_recv()
            column = self.view(slice(None), p.yx)
            self.start(3, column, p.device(p.z, p.yx_x, p.t))
            self.start(4, column, p.device(p.z, p.yx_y, p.t))
        elif number == 2:
            self.copies[3].wait_recv()
            self.start(5, self.view(pl.ds(0, 2), p.yx_x), p.device(p.z, p.yx_y, p.t))
            self.copies[4].wait_recv()
            self.start(6, self.view(pl.ds(2, 2), p.yx_y), p.device(p.z, p.yx_x, p.t))
        elif number == 3:
            self.copies[5].wait_recv()
            self.copies[6].wait_recv()
            self.start(7, self.core_view(), p.device(p.z, p.yx, 1 - p.t))
        elif number == 4:
            self.copies[7].wait_recv()

    def finish(self):
        for copy in self.copies.values():
            copy.wait_send()


GATHER_PIECES = 10
GATHER_GROUPS = ((0, 3), (3, 1), (4, 4), (8, 4))


def forward_kernel(
    rep,
    steps_ref, freq_ref, x_ref, qkv_ref, out_ref, up_ref, down_ref, time_ref, norm_ref, bias_ref,
    w_out, small_out, feats_out, entry_out, middle_out, qkv_out, probs_out, attn_out, hidden_out, slope_out, act_out,
    w, tw, nb, norms, bias, shifts, stream, attn, send, recv, keep_sem,
):
    place = Place(rep)
    z, yx, t = place.z, place.yx, place.t
    items = stream.shape[0] // LENGTH

    for layer in range(LAYERS):
        for slot in range(3):
            w[layer, slot, z, yx, :, place.cols] = qkv_ref[layer, slot].astype(BF16)
        w[layer, 3, z, yx, :, place.cols] = out_ref[layer].astype(BF16)
        for part in range(4):
            own = slice(part * 256, (part + 1) * 256)
            w[layer, 4 + part, z, yx, :, place.cols] = up_ref[layer, :, own].astype(BF16)
            w[layer, 8 + part, z, yx, :, place.cols] = down_ref[layer, :, own].astype(BF16)
        tw[layer, z, yx, t] = time_ref[layer].astype(BF16)
    nb[z, yx, t, 0:16] = norm_ref[...]
    nb[z, yx, t, 16:32] = bias_ref[...]
    place.greet()

    pieces = [
        Gather(place, lambda a, b: nb.at[a, b, t], lambda: nb.at[:, :, t], send.at[0], recv.at[0]),
        Gather(place, lambda a, b: tw.at[:, a, b, t], lambda: tw.at[:, :, :, t], send.at[1], recv.at[1]),
    ]
    for layer in range(LAYERS):
        for first, count in GATHER_GROUPS:
            span = w.at[layer, pl.ds(first, count)]
            number = len(pieces)
            pieces.append(
                Gather(
                    place,
                    lambda a, b, span=span: span.at[:, a, b, :, place.cols],
                    lambda span=span: span.at[:, :, :, :, place.cols],
                    send.at[number],
                    recv.at[number],
                )
            )
    for piece in pieces:
        piece.step(0)
    events = []
    for turn in range(len(pieces) + 3):
        for number in (1, 2, 3, 4):
            index = turn - (number - 1)
            if 0 <= index < len(pieces):
                events.append((index, number))
    position = [0]

    def run_until(index):
        while position[0] < len(events):
            piece, number = events[position[0]]
            pieces[piece].step(number)
            position[0] += 1
            if (piece, number) == (index, 4):
                break

    rows = lax.broadcasted_iota(jnp.int32, (8, 256), 0)
    angles = jnp.zeros((8, 256), F32)
    for item in range(items):
        step_value = steps_ref[t * items + item].astype(F32)
        angles = jnp.where(rows == item, step_value * freq_ref[0:1, :], angles)
    live = rows < items
    feats = jnp.concatenate(
        [jnp.where(live, jnp.sin(angles), 0.0), jnp.where(live, jnp.cos(angles), 0.0)], 1
    )
    feats_out[...] = feats
    feats_high = feats.astype(BF16)
    feats_low = (feats - feats_high.astype(F32)).astype(BF16)

    run_until(2)
    for zz in range(4):
        total = jnp.zeros((16, 128), F32)
        for part in range(8):
            total = total + nb[zz, part // 2, part % 2, 0:16]
        norms[:, zz * 128 : (zz + 1) * 128] = total
    for core in range(2):
        total = jnp.zeros((16, 128), F32)
        for part in range(16):
            total = total + nb[part // 4, part % 4, core, 16:32]
        total = total.astype(BF16).astype(F32)
        for layer in range(LAYERS):
            for part in range(4):
                for half in range(2):
                    row = layer * 8 + part * 2 + half
                    col = core * 256 + half * 128
                    bias[layer * 4 + part : layer * 4 + part + 1, col : col + 128] = total[row : row + 1]
    small_out[...] = norms[...]
    for layer in range(LAYERS):
        table = tw[layer].reshape(512, 512)
        shifts[layer * 8 : (layer + 1) * 8] = nn(feats_high, table) + nn(feats_low, table)

    lane = lax.broadcasted_iota(jnp.int32, (1, 128), 1)
    even = lane < HEAD_DIM
    even_mask = jnp.where(even, 1.0, 0.0).astype(BF16)
    odd_mask = jnp.where(even, 0.0, 1.0).astype(BF16)

    def attention_phase(layer):
        def body(*refs):
            if layer == 0:
                x_blk, *refs = refs
            entry_blk, qkv_blk, probs_blk, attn_blk = refs
            item = pl.program_id(0)
            here = pl.ds(pl.multiple_of(item * LENGTH, LENGTH), LENGTH)
            start = x_blk[...].astype(F32) if layer == 0 else stream[here]
            entry = start + shifts[pl.ds(layer * 8 + item, 1)]
            entry_blk[...] = entry
            stream[here] = entry
            hat, _ = normalize(entry)
            normed = (hat * norms[layer * 5 : layer * 5 + 1] + norms[layer * 5 + 1 : layer * 5 + 2]).astype(BF16)
            for slot in range(3):
                projected = nn(normed, w[layer, slot].reshape(512, 512)).astype(BF16)
                if slot == 0:
                    projected = projected * jnp.asarray(HEAD_DIM**-0.5, BF16)
                qkv_blk[:, slot * 512 : (slot + 1) * 512] = projected
            for pair in range(4):
                span = slice(pair * 128, (pair + 1) * 128)
                query = qkv_blk[:, span]
                key = qkv_blk[:, 512 + pair * 128 : 512 + (pair + 1) * 128]
                value = qkv_blk[:, 1024 + pair * 128 : 1024 + (pair + 1) * 128]
                mixed = []
                for side, mask in enumerate((even_mask, odd_mask)):
                    scores = nt(query * mask, key)
                    weight = jnp.exp(scores - jnp.max(scores, -1, keepdims=True))
                    probs = (weight * (1.0 / jnp.sum(weight, -1, keepdims=True))).astype(BF16)
                    probs_blk[0, pair * 2 + side] = probs
                    mixed.append(nn(probs, value))
                joined = jnp.where(even, mixed[0], mixed[1]).astype(BF16)
                attn_blk[:, span] = joined
                attn[here, span] = joined

        wide = lambda cols: pl.BlockSpec((LENGTH, cols), lambda i: (i, 0))
        pipeline = pltpu.emit_pipeline(
            body,
            grid=(items,),
            in_specs=[wide(512)] if layer == 0 else [],
            out_specs=[wide(512), wide(1536), pl.BlockSpec((1, 8, 256, 256), lambda i: (i, 0, 0, 0)), wide(512)],
        )
        ins = [x_ref] if layer == 0 else []
        pipeline(*ins, entry_out.at[layer], qkv_out.at[layer], probs_out.at[layer], attn_out.at[layer])

    def feed_phase(layer):
        def body(*refs):
            middle_blk, hidden_blk, slope_blk, *rest = refs
            item = pl.program_id(0)
            here = pl.ds(pl.multiple_of(item * LENGTH, LENGTH), LENGTH)
            middle = stream[here] + nt(attn[here], w[layer, 3].reshape(512, 512))
            middle_blk[...] = middle
            hat, _ = normalize(middle)
            normed = (hat * norms[layer * 5 + 2 : layer * 5 + 3] + norms[layer * 5 + 3 : layer * 5 + 4]).astype(BF16)
            total = middle + norms[layer * 5 + 4 : layer * 5 + 5]
            for part in range(4):
                row = layer * 4 + part
                span = slice(part * 512, (part + 1) * 512)
                pre = nn(normed, w[layer, 4 + part].reshape(512, 512)) + bias[row : row + 1]
                hidden, slope = gelu_and_slope(pre)
                hidden = hidden.astype(BF16)
                hidden_blk[:, span] = hidden
                slope_blk[:, span] = slope.astype(BF16)
                total = total + nt(hidden, w[layer, 8 + part].reshape(512, 512))
            if layer == LAYERS - 1:
                rest[0][...] = total.astype(BF16)
            else:
                stream[here] = total

        wide = lambda cols: pl.BlockSpec((LENGTH, cols), lambda i: (i, 0))
        last = layer == LAYERS - 1
        pipeline = pltpu.emit_pipeline(
            body,
            grid=(items,),
            in_specs=[],
            out_specs=[wide(512), wide(2048), wide(2048)] + ([wide(512)] if last else []),
        )
        pipeline(middle_out.at[layer], hidden_out.at[layer], slope_out.at[layer], *([act_out] if last else []))

    keeps = []
    for layer in range(LAYERS):
        run_until(2 + layer * 4)
        with jax.named_scope("attention"):
            attention_phase(layer)
        run_until(5 + layer * 4)
        keep = pltpu.make_async_copy(w.at[layer], w_out.at[layer], keep_sem.at[layer])
        keep.start()
        keeps.append(keep)
        with jax.named_scope("feed"):
            feed_phase(layer)
    for piece in pieces:
        piece.finish()
    for keep in keeps:
        keep.wait()


def forward_call(rep, rows, steps, freq, x, qkv, out, up, down, time, norm, bias):
    items = rows // LENGTH
    hbm = pl.BlockSpec(memory_space=pl.ANY)
    vmem = pl.BlockSpec(memory_space=pltpu.VMEM)
    smem = pl.BlockSpec(memory_space=pltpu.SMEM)
    shape = jax.ShapeDtypeStruct
    return pl.pallas_call(
        functools.partial(forward_kernel, rep),
        name="forward",
        in_specs=[smem, vmem, hbm] + [vmem] * 7,
        out_shape=[
            shape((LAYERS, 12, 4, 4, 32, 512), BF16),
            shape((16, 512), F32),
            shape((8, 512), F32),
            shape((LAYERS, rows, 512), F32),
            shape((LAYERS, rows, 512), F32),
            shape((LAYERS, rows, 1536), BF16),
            shape((LAYERS, items, 8, 256, 256), BF16),
            shape((LAYERS, rows, 512), BF16),
            shape((LAYERS, rows, 2048), BF16),
            shape((LAYERS, rows, 2048), BF16),
            shape((rows, 512), BF16),
        ],
        out_specs=[hbm, vmem, vmem] + [hbm] * 8,
        scratch_shapes=[
            pltpu.VMEM((LAYERS, 12, 4, 4, 32, 512), BF16),
            pltpu.VMEM((LAYERS, 4, 4, 2, 16, 512), BF16),
            pltpu.VMEM((4, 4, 2, 32, 128), F32),
            pltpu.VMEM((16, 512), F32),
            pltpu.VMEM((8, 512), F32),
            pltpu.VMEM((16, 512), F32),
            pltpu.VMEM((rows, 512), F32),
            pltpu.VMEM((rows, 512), BF16),
            pltpu.SemaphoreType.DMA((GATHER_PIECES, 8)),
            pltpu.SemaphoreType.DMA((GATHER_PIECES, 8)),
            pltpu.SemaphoreType.DMA((LAYERS,)),
        ],
        compiler_params=pltpu.CompilerParams(collective_id=1, has_side_effects=True, vmem_limit_bytes=56 << 20),
    )(steps, freq, x, qkv, out, up, down, time, norm, bias)


class Scatter:
    def __init__(self, place, grads, received, total, groups, send, recv):
        self.place, self.grads, self.received, self.total = place, grads, received, total
        self.first, self.count = groups
        self.span = pl.ds(*groups)
        self.send, self.recv = send, recv
        self.copies = {}

    def start(self, slot, src, dst, device):
        copy = pltpu.make_async_remote_copy(
            src_ref=src, dst_ref=dst, send_sem=self.send.at[slot], recv_sem=self.recv.at[slot],
            device_id=device, device_id_type=MESH,
        )
        copy.start()
        self.copies[slot] = copy

    def add(self, where, terms):
        def one(group, carry):
            ref = self.grads.at[(group,) + where]
            value = ref[...].astype(F32)
            for term in terms:
                value = value + term[group].astype(F32)
            ref[...] = value.astype(BF16)
            return carry

        lax.fori_loop(self.first, self.first + self.count, one, 0)

    def step(self, number):
        p, span = self.place, self.span
        core, diag_y, diag_x, col_x, col_y, along = self.received
        every = slice(None)
        if number == 0:
            self.start(0, self.grads.at[span, :, :, :, p.other_cols], core.at[span], p.device(p.z, p.yx, 1 - p.t))
        elif number == 1:
            self.copies[0].wait_recv()
            self.add((every, every, every, p.cols), [core])
            low = self.grads.at[span, pl.ds(0, 2), p.yx_d, :, p.cols]
            high = self.grads.at[span, pl.ds(2, 2), p.yx_d, :, p.cols]
            self.start(1, low, diag_y.at[span], p.device(p.z, p.yx_y, p.t))
            self.start(2, high, diag_x.at[span], p.device(p.z, p.yx_x, p.t))
        elif number == 2:
            self.copies[1].wait_recv()
            self.add((pl.ds(0, 2), p.yx_x, every, p.cols), [diag_y])
            self.start(3, self.grads.at[span, :, p.yx_x, :, p.cols], col_x.at[span], p.device(p.z, p.yx_x, p.t))
            self.copies[2].wait_recv()
            self.add((pl.ds(2, 2), p.yx_y, every, p.cols), [diag_x])
            self.start(4, self.grads.at[span, :, p.yx_y, :, p.cols], col_y.at[span], p.device(p.z, p.yx_y, p.t))
        elif number == 3:
            self.copies[3].wait_recv()
            self.copies[4].wait_recv()
            self.add((every, p.yx, every, p.cols), [col_x, col_y])
            for k in (1, 2, 3):
                there = p.z_ahead(k)
                self.start(
                    4 + k, self.grads.at[span, there, p.yx, :, p.cols], along.at[k - 1, span],
                    p.device(there, p.yx, p.t),
                )
        elif number == 4:
            for k in (1, 2, 3):
                self.copies[4 + k].wait_recv()

            def one(group, carry):
                value = self.grads[group, p.z, p.yx, :, p.cols].astype(F32)
                for k in range(3):
                    value = value + along[k, group].astype(F32)
                self.total[group] = value
                return carry

            lax.fori_loop(self.first, self.first + self.count, one, 0)

    def finish(self):
        for copy in self.copies.values():
            copy.wait_send()


class SmallSum:
    def __init__(self, place, sums, received, total, send, recv):
        self.place, self.sums, self.received, self.total = place, sums, received, total
        self.send, self.recv = send, recv
        self.copies = {}

    def start(self, slot, stage, device):
        copy = pltpu.make_async_remote_copy(
            src_ref=self.sums.at[stage], dst_ref=self.received.at[slot], send_sem=self.send.at[slot],
            recv_sem=self.recv.at[slot], device_id=device, device_id_type=MESH,
        )
        copy.start()
        self.copies[slot] = copy

    def step(self, number):
        p = self.place
        if number > 0:
            slots = (0,) if number == 1 else (1,) if number == 2 else (2,) if number == 3 else (3, 4, 5)
            value = self.sums[number - 1]
            for slot in slots:
                self.copies[slot].wait_recv()
                value = value + self.received[slot]
            if number < 4:
                self.sums[number] = value
            else:
                self.total[...] = value
        if number == 0:
            self.start(0, 0, p.device(p.z, p.yx, 1 - p.t))
        elif number == 1:
            self.start(1, 1, p.device(p.z, p.yx_x, p.t))
        elif number == 2:
            self.start(2, 2, p.device(p.z, p.yx_y, p.t))
        elif number == 3:
            for k in (1, 2, 3):
                self.start(2 + k, 3, p.device(p.z_ahead(k), p.yx, p.t))

    def finish(self):
        for copy in self.copies.values():
            copy.wait_send()


GRAD_GROUPS = 13
SCATTER_PIECES = ((4, 4), (8, 4), (3, 1), (0, 3), (12, 1))


def backward_kernel(
    rep,
    scale_ref, small_ref, feats_ref, cot_ref, w_in, entry_in, middle_in, qkv_in, probs_in, attn_in, hidden_in, slope_in,
    grad_out, total_out, sums_out, time_out,
    w, gx, dattn, du, hidden, attn, n1t, n2t, gdt, got, dqkv, grads, item_grad, acc, acc_bias,
    r_core, r_dy, r_dx, r_x, r_y, r_z, sums, r_sums, r_time,
    w_sem, in_sem, send, recv, small_send, small_recv, time_send, time_recv,
):
    place = Place(rep)
    t = place.t
    rows = gx.shape[0]
    items = rows // LENGTH
    wide = lambda cols: pl.BlockSpec((LENGTH, cols), lambda i: (i, 0))
    lane = lax.broadcasted_iota(jnp.int32, (1, 128), 1)
    even = lane < HEAD_DIM
    even_mask = jnp.where(even, 1.0, 0.0).astype(BF16)
    odd_mask = jnp.where(even, 0.0, 1.0).astype(BF16)

    def load_weights(layer):
        copies = []
        for number, (first, count) in enumerate(((3, 9), (0, 3))):
            copy = pltpu.make_async_copy(
                w_in.at[layer, pl.ds(first, count)], w.at[pl.ds(first, count)], w_sem.at[layer, number]
            )
            copies.append(copy)
        return copies

    def load_stash(layer):
        return [
            pltpu.make_async_copy(hidden_in.at[layer], hidden, in_sem.at[layer, 0]),
            pltpu.make_async_copy(attn_in.at[layer], attn, in_sem.at[layer, 1]),
        ]

    def norm_back(hat, inverse, dy, layer, row, here):
        acc[row] += fold_rows(dy * hat)
        acc[row + 1] += fold_rows(dy)
        scaled = dy * small_ref[layer * 5 + row : layer * 5 + row + 1]
        mean = jnp.mean(scaled, -1, keepdims=True)
        along = jnp.mean(scaled * hat, -1, keepdims=True)
        return inverse * (scaled - mean - hat * along)

    def feed_phase(layer):
        last = layer == LAYERS - 1

        def body(*refs):
            middle_blk, slope_blk, *rest = refs
            item = pl.program_id(0)
            here = pl.ds(pl.multiple_of(item * LENGTH, LENGTH), LENGTH)
            if last:
                grad = rest[0][...].astype(F32) * scale_ref[t * items + item]
            else:
                grad = gx[here]
            acc[4] += fold_rows(grad)
            low = grad.astype(BF16)
            gdt[:, here] = low.T
            back = jnp.zeros((LENGTH, 512), F32)
            for part in range(4):
                span = slice(part * 512, (part + 1) * 512)
                dh = nn(low, w[8 + part].reshape(512, 512))
                pre_grad = (dh * slope_blk[:, span].astype(F32)).astype(BF16)
                du[here, span] = pre_grad
                acc_bias[part] += fold_rows(pre_grad.astype(F32))
                back = back + nt(pre_grad, w[4 + part].reshape(512, 512))
            hat, inverse = normalize(middle_blk[...])
            normed = hat * small_ref[layer * 5 + 2 : layer * 5 + 3] + small_ref[layer * 5 + 3 : layer * 5 + 4]
            n2t[:, here] = normed.astype(BF16).T
            grad = grad + norm_back(hat, inverse, back, layer, 2, here)
            gx[here] = grad
            low = grad.astype(BF16)
            got[:, here] = low.T
            dattn[here] = nn(low, w[3].reshape(512, 512)).astype(BF16)

        pipeline = pltpu.emit_pipeline(
            body, grid=(items,), in_specs=[wide(512), wide(2048)] + ([wide(512)] if last else [])
        )
        pipeline(middle_in.at[layer], slope_in.at[layer], *([cot_ref] if last else []))

    def attention_phase(layer):
        def body(*refs):
            entry_blk, qkv_blk, probs_blk, *rest = refs
            item = pl.program_id(0)
            here = pl.ds(pl.multiple_of(item * LENGTH, LENGTH), LENGTH)
            for pair in range(4):
                span = slice(pair * 128, (pair + 1) * 128)
                query = qkv_blk[:, span]
                key = qkv_blk[:, 512 + pair * 128 : 512 + (pair + 1) * 128]
                value = qkv_blk[:, 1024 + pair * 128 : 1024 + (pair + 1) * 128]
                back = dattn[here, span]
                found = []
                for side, mask in enumerate((even_mask, odd_mask)):
                    probs = probs_blk[0, pair * 2 + side]
                    dprobs = nt(back * mask, value)
                    wide_probs = probs.astype(F32)
                    delta = jnp.sum(wide_probs * dprobs, -1, keepdims=True)
                    dscores = (wide_probs * (dprobs - delta)).astype(BF16)
                    found.append((nn(dscores, key), tn(dscores, query), tn(probs, back)))
                dq, dk, dv = [jnp.where(even, found[0][i], found[1][i]) for i in range(3)]
                dqkv[here, span] = (dq * HEAD_DIM**-0.5).astype(BF16)
                dqkv[here, 512 + pair * 128 : 512 + (pair + 1) * 128] = dk.astype(BF16)
                dqkv[here, 1024 + pair * 128 : 1024 + (pair + 1) * 128] = dv.astype(BF16)
            back = jnp.zeros((LENGTH, 512), F32)
            for slot in range(3):
                back = back + nt(dqkv[here, slot * 512 : (slot + 1) * 512], w[slot].reshape(512, 512))
            hat, inverse = normalize(entry_blk[...])
            normed = hat * small_ref[layer * 5 : layer * 5 + 1] + small_ref[layer * 5 + 1 : layer * 5 + 2]
            n1t[:, here] = normed.astype(BF16).T
            grad = gx[here] + norm_back(hat, inverse, back, layer, 0, here)
            item_grad[pl.ds(item, 1)] = jnp.sum(grad, 0, keepdims=True)
            if layer == 0:
                rest[0][...] = grad.astype(BF16)
            else:
                gx[here] = grad

        pipeline = pltpu.emit_pipeline(
            body,
            grid=(items,),
            in_specs=[wide(512), wide(1536), pl.BlockSpec((1, 8, 256, 256), lambda i: (i, 0, 0, 0))],
            out_specs=[wide(512)] if layer == 0 else [],
        )
        pipeline(entry_in.at[layer], qkv_in.at[layer], probs_in.at[layer], *([grad_out] if layer == 0 else []))

    def weight_grad(left, right, first, count):
        def one(part, carry):
            span = pl.ds(pl.multiple_of(part * 512, 512), 512)
            grads[first + part] = nn(left[...], right[:, span]).astype(BF16).reshape(4, 4, 32, 512)
            return carry

        lax.fori_loop(0, count, one, 0)

    scatters, smalls = [], []
    for layer in range(LAYERS):
        received = [r.at[layer] for r in (r_core, r_dy, r_dx, r_x, r_y, r_z)]
        scatters.append(
            [
                Scatter(place, grads, received, total_out.at[layer], groups, send.at[layer, i], recv.at[layer, i])
                for i, groups in enumerate(SCATTER_PIECES)
            ]
        )
        smalls.append(
            SmallSum(place, sums.at[layer], r_sums.at[layer], sums_out.at[layer], small_send.at[layer], small_recv.at[layer])
        )

    order = [LAYERS - 1 - i for i in range(LAYERS)]
    weights = {order[0]: load_weights(order[0])}
    stash = {order[0]: load_stash(order[0])}
    for copy in weights[order[0]] + stash[order[0]]:
        copy.start()
    item_grad[...] = jnp.zeros(item_grad.shape, F32)
    place.greet()

    for turn, layer in enumerate(order):
        acc[...] = jnp.zeros(acc.shape, F32)
        acc_bias[...] = jnp.zeros(acc_bias.shape, F32)
        weights[layer][0].wait()
        with jax.named_scope("feed_back"):
            feed_phase(layer)
        stash[layer][0].wait()
        stash[layer][1].wait()
        weights[layer][1].wait()
        if turn > 0:
            for piece in scatters[order[turn - 1]]:
                piece.finish()
        with jax.named_scope("feed_grads"):
            weight_grad(n2t, du, 4, 4)
            scatters[layer][0].step(0)
            weight_grad(gdt, hidden, 8, 4)
            scatters[layer][1].step(0)
            weight_grad(got, attn, 3, 1)
            scatters[layer][2].step(0)
        with jax.named_scope("attention_back"):
            attention_phase(layer)
        if turn + 1 < LAYERS:
            after = order[turn + 1]
            weights[after] = load_weights(after)
            stash[after] = load_stash(after)
            for copy in weights[after] + stash[after]:
                copy.start()
        with jax.named_scope("attention_grads"):
            weight_grad(n1t, dqkv, 0, 3)
            scatters[layer][3].step(0)
            spread = lax.dot_general(
                feats_ref[...], item_grad[...], (((0,), (0,)), ((), ())),
                precision=lax.Precision.HIGHEST, preferred_element_type=F32,
            )
            grads[12] = spread.astype(BF16).reshape(4, 4, 32, 512)
            scatters[layer][4].step(0)
            for row in range(5):
                sums[layer, 0, row : row + 1] = jnp.sum(acc[row], 0, keepdims=True)
            for part in range(4):
                sums[layer, 0, 5 + part : 6 + part] = jnp.sum(acc_bias[part], 0, keepdims=True)
            sums[layer, 0, 9:16] = jnp.zeros((7, 512), F32)
            smalls[layer].step(0)
        with jax.named_scope("scatter"):
            for number in (1, 2, 3, 4):
                for piece in scatters[layer]:
                    piece.step(number)
                smalls[layer].step(number)

    swaps = []
    for layer in range(LAYERS):
        swap = pltpu.make_async_remote_copy(
            src_ref=total_out.at[layer, 12, pl.ds(pl.multiple_of((1 - t) * 16, 16), 16)],
            dst_ref=r_time.at[layer], send_sem=time_send.at[layer], recv_sem=time_recv.at[layer],
            device_id=place.device(place.z, place.yx, 1 - t), device_id_type=MESH,
        )
        swap.start()
        swaps.append(swap)
    for layer in range(LAYERS):
        swaps[layer].wait()
        time_out[layer, :, place.cols] = total_out[layer, 12, pl.ds(pl.multiple_of(t * 16, 16), 16)]
        time_out[layer, :, place.other_cols] = r_time[layer]
    for piece in scatters[order[-1]]:
        piece.finish()
    for piece in smalls:
        piece.finish()


def backward_call(rep, rows, scale, small, feats, cot, w, entry, middle, qkv, probs, attn, hidden, slope):
    items = rows // LENGTH
    hbm = pl.BlockSpec(memory_space=pl.ANY)
    vmem = pl.BlockSpec(memory_space=pltpu.VMEM)
    smem = pl.BlockSpec(memory_space=pltpu.SMEM)
    shape = jax.ShapeDtypeStruct
    pieces = len(SCATTER_PIECES)
    dma = pltpu.SemaphoreType.DMA
    return pl.pallas_call(
        functools.partial(backward_kernel, rep),
        name="backward",
        in_specs=[smem, vmem, vmem] + [hbm] * 9,
        out_shape=[
            shape((rows, 512), BF16),
            shape((LAYERS, GRAD_GROUPS, 32, 256), F32),
            shape((LAYERS, 16, 512), F32),
            shape((LAYERS, 16, 512), F32),
        ],
        out_specs=[hbm, vmem, vmem, vmem],
        scratch_shapes=[
            pltpu.VMEM((12, 4, 4, 32, 512), BF16),
            pltpu.VMEM((rows, 512), F32),
            pltpu.VMEM((rows, 512), BF16),
            pltpu.VMEM((rows, 2048), BF16),
            pltpu.VMEM((rows, 2048), BF16),
            pltpu.VMEM((rows, 512), BF16),
            pltpu.VMEM((512, rows), BF16),
            pltpu.VMEM((512, rows), BF16),
            pltpu.VMEM((512, rows), BF16),
            pltpu.VMEM((512, rows), BF16),
            pltpu.VMEM((rows, 1536), BF16),
            pltpu.VMEM((GRAD_GROUPS, 4, 4, 32, 512), BF16),
            pltpu.VMEM((8, 512), F32),
            pltpu.VMEM((5, 8, 512), F32),
            pltpu.VMEM((4, 8, 512), F32),
            pltpu.VMEM((LAYERS, GRAD_GROUPS, 4, 4, 32, 256), BF16),
            pltpu.VMEM((LAYERS, GRAD_GROUPS, 2, 32, 256), BF16),
            pltpu.VMEM((LAYERS, GRAD_GROUPS, 2, 32, 256), BF16),
            pltpu.VMEM((LAYERS, GRAD_GROUPS, 4, 32, 256), BF16),
            pltpu.VMEM((LAYERS, GRAD_GROUPS, 4, 32, 256), BF16),
            pltpu.VMEM((LAYERS, 3, GRAD_GROUPS, 32, 256), BF16),
            pltpu.VMEM((LAYERS, 4, 16, 512), F32),
            pltpu.VMEM((LAYERS, 6, 16, 512), F32),
            pltpu.VMEM((LAYERS, 16, 256), F32),
            dma((LAYERS, 2)),
            dma((LAYERS, 2)),
            dma((LAYERS, pieces, 8)),
            dma((LAYERS, pieces, 8)),
            dma((LAYERS, 6)),
            dma((LAYERS, 6)),
            dma((LAYERS,)),
            dma((LAYERS,)),
        ],
        compiler_params=pltpu.CompilerParams(collective_id=2, has_side_effects=True, vmem_limit_bytes=62 << 20),
    )(scale, small, feats, cot, w, entry, middle, qkv, probs, attn, hidden, slope)


def adamw(weight, gradient, first_moment, second_moment, rate):
    first_new = beta_first * first_moment + (1.0 - beta_first) * gradient
    second_new = beta_second * second_moment + (1.0 - beta_second) * gradient * gradient
    first_corr = first_new / (1.0 - beta_first**STEP)
    second_corr = second_new / (1.0 - beta_second**STEP)
    weight_new = weight - rate * (first_corr / (jnp.sqrt(second_corr) + adam_eps) + weight_decay * weight)
    return (weight_new, first_new, second_new)


def per_device(
    rep,
    inputs, cotangent, timesteps, item_scale,
    qkv_weight, qkv_first, qkv_second,
    out_weight, out_first, out_second,
    up_weight, up_first, up_second,
    up_bias, bias_first, bias_second,
    down_weight, down_first, down_second,
    norm_params, norm_first, norm_second,
    time_weight, time_first, time_second,
):
    rows = inputs.shape[0]
    dp, t = lax.axis_index("dp"), lax.axis_index("tensor")
    group = dp // rep
    qkv, out, up, down, bias = qkv_weight, out_weight, up_weight, down_weight, up_bias
    norm, time = norm_params, time_weight
    teams = None
    if rep > 1:
        size = GROUPS * rep
        teams = [[g * rep + j for j in range(rep)] for g in range(GROUPS)]
        pairs = [[g * rep * 2 + j for j in range(rep * 2)] for g in range(GROUPS)]
        join = lambda v, axis: lax.all_gather(v, "dp", axis=axis, axis_index_groups=teams, tiled=True)
        join_both = lambda v, axis: lax.all_gather(
            v, ("dp", "tensor"), axis=axis, axis_index_groups=pairs, tiled=True
        )
        qkv, out, up, down, bias = join(qkv, 1), join(out, 2), join(up, 1), join(down, 2), join(bias, 2)
        norm, time = join_both(norm, 2), join_both(time, 1)
        norm = lax.dynamic_slice_in_dim(norm, t * 16, 16, 2)
        time = lax.dynamic_slice_in_dim(time, t * 16, 16, 1)

    lane = lax.broadcasted_iota(jnp.int32, (16, 128), 1)
    spot = (group % 4) * 2 + t
    norm_rows = jnp.pad(norm.reshape(10, 16), ((0, 6), (0, 0)))
    norm_block = jnp.where(lane // 16 == spot, jnp.tile(norm_rows, (1, 8)), 0.0)
    bias_block = jnp.where(lane // 8 == group, jnp.tile(bias.reshape(16, 8), (1, 16)), 0.0)
    half_width = 256
    freq = np.exp(-math.log(10000.0) / half_width * np.arange(half_width)).astype(np.float32)
    freq = jnp.asarray(np.broadcast_to(freq, (8, half_width)))

    w, small, feats, entry, middle, qkv_rows, probs, attn, hidden, slope, activations = forward_call(
        rep, rows, timesteps, freq, inputs,
        jnp.transpose(qkv, (0, 2, 1, 3)), jnp.swapaxes(out, 1, 2), up, jnp.swapaxes(down, 1, 2),
        time, norm_block, bias_block,
    )
    input_grad, total, sums, time_grad = backward_call(
        rep, rows, item_scale, small, feats, cotangent, w, entry, middle, qkv_rows, probs, attn, hidden, slope
    )

    qkv_grad = jnp.transpose(total[:, 0:3], (0, 2, 1, 3))
    out_grad = jnp.swapaxes(total[:, 3], 1, 2)
    up_grad = jnp.transpose(total[:, 4:8], (0, 2, 1, 3)).reshape(LAYERS, 32, 1024)
    down_grad = jnp.swapaxes(jnp.transpose(total[:, 8:12], (0, 2, 1, 3)).reshape(LAYERS, 32, 1024), 1, 2)
    norm_sum = sums[:, 0:5]
    bias_sum = sums[:, 5:9].reshape(LAYERS, 4, 2, 2, 128)
    if rep > 1:
        part = lambda v, axis: lax.psum_scatter(
            v, "dp", scatter_dimension=axis, axis_index_groups=teams, tiled=True
        )
        qkv_grad, out_grad, up_grad, down_grad = part(qkv_grad, 1), part(out_grad, 2), part(up_grad, 1), part(down_grad, 2)
        whole = lambda v: lax.psum(v, "dp", axis_index_groups=teams)
        norm_sum, bias_sum = whole(norm_sum), whole(bias_sum)
        time_grad = lax.all_gather(whole(time_grad), "tensor", axis=1, tiled=True)
        width = time_weight.shape[1]
        time_grad = lax.dynamic_slice_in_dim(time_grad, ((dp % rep) * 2 + t) * width, width, 1)
    width = norm_params.shape[2]
    norm_grad = lax.dynamic_slice_in_dim(norm_sum, (dp * 2 + t) * width, width, 2)
    bias_sum = lax.dynamic_index_in_dim(bias_sum, t, 2, keepdims=False).reshape(LAYERS, 8, 128)
    width = up_bias.shape[2]
    bias_grad = lax.dynamic_slice_in_dim(bias_sum, dp * width, width, 2)

    new_qkv = adamw(qkv_weight, qkv_grad, qkv_first, qkv_second, learn_rate)
    new_out = adamw(out_weight, out_grad, out_first, out_second, learn_rate)
    new_up = adamw(up_weight, up_grad, up_first, up_second, learn_rate)
    new_bias = adamw(up_bias, bias_grad, bias_first, bias_second, learn_rate)
    new_down = adamw(down_weight, down_grad, down_first, down_second, learn_rate)
    new_norm = adamw(norm_params, norm_grad, norm_first, norm_second, norm_rate)
    new_time = adamw(time_weight, time_grad, time_first, time_second, learn_rate)
    return (
        activations, input_grad,
        new_qkv[0], new_qkv[1], new_qkv[2][:, :, :2], new_qkv[2][:, :, 2],
        *new_out, *new_up, *new_bias, *new_down, *new_norm, *new_time,
    )


def solution(mesh):
    rep = mesh.shape["dp"] // GROUPS
    shard = P(None, "dp", None, "tensor")
    rows = P(("dp", "tensor"), None)
    trans = P(None, "tensor", "dp")
    flat = P(None, "dp", "tensor")
    norm = P(None, None, ("dp", "tensor"))
    time = P(None, ("dp", "tensor"), None)
    return jax.shard_map(
        functools.partial(per_device, rep),
        mesh=mesh,
        in_specs=(rows, rows, P("dp"), P("dp")) + (shard,) * 3 + (trans,) * 3 + (flat,) * 3 + (trans,) * 6 + (norm,) * 3 + (time,) * 3,
        out_specs=(rows, rows, shard, shard, shard, flat) + (trans,) * 3 + (flat,) * 3 + (trans,) * 6 + (norm,) * 3 + (time,) * 3,
        check_vma=False,
    )
```

```python
import functools
import math

import jax
import jax.numpy as jnp
import numpy as np
from jax import lax
from jax.experimental import pallas as pl
from jax.experimental.pallas import tpu as pltpu
from jax.sharding import PartitionSpec as P

HEAD_DIM = 64
LENGTH = 256
LAYERS = 2
STEP = 8
GROUPS = 16
MESH = pl.DeviceIdType.MESH
LAG = 2
F32 = jnp.float32
BF16 = jnp.bfloat16

beta_first = 0.5
beta_second = 0.5
learn_rate = 0.1
norm_rate = 0.4
weight_decay = 0.01
adam_eps = 1e-08
norm_eps = 1e-05


def nn(a, b):
    return lax.dot_general(a, b, (((1,), (0,)), ((), ())), preferred_element_type=F32)


def nt(a, b):
    return lax.dot_general(a, b, (((1,), (1,)), ((), ())), preferred_element_type=F32)


def tn(a, b):
    return lax.dot_general(a, b, (((0,), (0,)), ((), ())), preferred_element_type=F32)


def normalize(values):
    center = values - jnp.mean(values, -1, keepdims=True)
    inverse = lax.rsqrt(jnp.mean(center * center, -1, keepdims=True) + norm_eps)
    return center * inverse, inverse


def fold_rows(values):
    rows, cols = values.shape
    return jnp.sum(values.reshape(rows // 8, 8, cols), 0)


def gelu_and_slope(x):
    size = jnp.abs(x)
    denom = 1.0 + (0.3275911 / math.sqrt(2.0)) * size
    t = pl.reciprocal(denom, approx=True)
    t = t * (2.0 - denom * t)
    bell = jnp.exp(x * x * -0.5)
    poly = 0.5 * 1.061405429
    poly = poly * t + 0.5 * -1.453152027
    poly = poly * t + 0.5 * 1.421413741
    poly = poly * t + 0.5 * -0.284496736
    poly = poly * t + 0.5 * 0.254829592
    tail = poly * t * bell
    below = jnp.where(x >= 0.0, 1.0 - tail, tail)
    return x * below, below + x * bell * (1.0 / math.sqrt(2.0 * math.pi))


class Place:
    def __init__(self, rep):
        dp = lax.axis_index("dp")
        self.rep = rep
        self.copy = dp % rep
        self.group = dp // rep
        self.t = lax.axis_index("tensor")
        self.z = self.group // 4
        self.yx = self.group % 4
        x, y = self.yx % 2, self.yx // 2
        self.yx_x = self.yx + 1 - 2 * x
        self.yx_y = self.yx + 2 - 4 * y
        self.yx_d = 3 - self.yx
        self.cols = pl.ds(pl.multiple_of(self.t * 256, 256), 256)
        self.other_cols = pl.ds(pl.multiple_of((1 - self.t) * 256, 256), 256)

    def device(self, z, yx, t):
        return ((z * 4 + yx) * self.rep + self.copy, t)

    def z_ahead(self, k):
        return (self.z + k) % 4

    @property
    def partners(self):
        return [self.device(self.z_ahead(k), self.yx, self.t) for k in (1, 2, 3)] + [
            self.device(self.z, self.yx_x, self.t),
            self.device(self.z, self.yx_y, self.t),
            self.device(self.z, self.yx, 1 - self.t),
        ]

    def greet(self):
        barrier = pltpu.get_barrier_semaphore()
        for partner in self.partners:
            pl.semaphore_signal(barrier, inc=1, device_id=partner, device_id_type=MESH)
        pl.semaphore_wait(barrier, len(self.partners))


class Exchange:
    def start(self, slot):
        self.copy(slot).start()

    def arrived(self, *slots):
        for slot in slots:
            self.copy(slot).wait_recv()

    def finish(self):
        for slot in range(self.slots):
            self.copy(slot).wait_send()

    def remote(self, slot, src, dst, device):
        return pltpu.make_async_remote_copy(
            src_ref=src, dst_ref=dst, send_sem=self.send.at[slot], recv_sem=self.recv.at[slot],
            device_id=device, device_id_type=MESH,
        )


class Gather(Exchange):
    slots = 8

    def __init__(self, place, view, core_view, send, recv):
        self.place, self.view, self.core_view, self.send, self.recv = place, view, core_view, send, recv

    def copy(self, slot):
        p = self.place
        if slot < 3:
            ref, device = self.view(p.z, p.yx), p.device(p.z_ahead(slot + 1), p.yx, p.t)
        elif slot < 5:
            ref, device = self.view(slice(None), p.yx), p.device(p.z, p.yx_x if slot == 3 else p.yx_y, p.t)
        elif slot == 5:
            ref, device = self.view(pl.ds(0, 2), p.yx_x), p.device(p.z, p.yx_y, p.t)
        elif slot == 6:
            ref, device = self.view(pl.ds(2, 2), p.yx_y), p.device(p.z, p.yx_x, p.t)
        else:
            ref, device = self.core_view(), p.device(p.z, p.yx, 1 - p.t)
        return self.remote(slot, ref, ref, device)

    def step(self, number):
        if number == 0:
            for slot in (0, 1, 2):
                self.start(slot)
        elif number == 1:
            self.arrived(0, 1, 2)
            self.start(3)
            self.start(4)
        elif number == 2:
            self.arrived(3)
            self.start(5)
            self.arrived(4)
            self.start(6)
        elif number == 3:
            self.arrived(5, 6)
            self.start(7)
        elif number == 4:
            self.arrived(7)


def play(events):
    for piece, number in events:
        piece.step(number)


def stagger(pieces, numbers, lag=1):
    events = []
    for turn in range(len(pieces) + lag * (len(numbers) - 1)):
        for place, number in enumerate(numbers):
            if 0 <= turn - lag * place < len(pieces):
                events.append((pieces[turn - lag * place], number))
    return events


def share(events, counts):
    runs = []
    for count in counts:
        runs.append(events[:count])
        events = events[count:]
    return runs + [events]


def each_item(body, agenda, items, in_specs, out_specs, refs):
    def whole(*blocks):
        item = pl.program_id(0)
        for number, events in enumerate(agenda[:-1]):
            if events:
                pl.when(item == number)(functools.partial(play, events))
        body(item, *blocks)

    pltpu.emit_pipeline(whole, grid=(items,), in_specs=in_specs, out_specs=out_specs)(*refs)
    play(agenda[-1])


GATHER_PIECES = 12


def weight(ref, group):
    return jnp.concatenate([ref[group, 0].reshape(512, 256), ref[group, 1].reshape(512, 256)], 1)


def forward_kernel(
    rep,
    steps_ref, freq_ref, x_ref, qkv_ref, out_ref, up_ref, down_ref, time_ref, norm_ref, bias_ref,
    w_out, small_out, feats_out, entry_out, middle_out, qkv_out, probs_out, attn_out, hidden_out, slope_out, act_out,
    w, tw, nb, norms, bias, shifts, stream, attn, send, recv, keep_sem,
):
    place = Place(rep)
    z, yx, t = place.z, place.yx, place.t
    items = stream.shape[0] // LENGTH

    for layer in range(LAYERS):
        for slot in range(3):
            w[layer, slot, t, z, yx] = qkv_ref[layer, slot].astype(BF16)
        w[layer, 3, t, z, yx] = out_ref[layer].astype(BF16)
        for part in range(4):
            own = slice(part * 256, (part + 1) * 256)
            w[layer, 4 + part, t, z, yx] = up_ref[layer, :, own].astype(BF16)
            w[layer, 8 + part, t, z, yx] = down_ref[layer, :, own].astype(BF16)
        tw[layer, t, z, yx] = time_ref[layer].astype(BF16)
    nb[0, t, z, yx] = norm_ref[...]
    nb[1, t, z, yx] = bias_ref[...]
    place.greet()

    pieces = []

    def piece(ref, *lead):
        number = len(pieces)
        pieces.append(
            Gather(
                place,
                lambda a, b: ref.at[(*lead, t, a, b)],
                lambda: ref.at[(*lead, t)],
                send.at[number],
                recv.at[number],
            )
        )
        return pieces[-1]

    norm_piece = piece(nb, 0)
    time_pieces, layer_pieces = [], []
    for layer in range(LAYERS):
        time_pieces.append(piece(tw, layer))
        layer_pieces.append([piece(w, layer, pl.ds(first, count)) for first, count in ((0, 3), (3, 1), (4, 4), (8, 4))])
        if layer == 0:
            bias_piece = piece(nb, 1)
    opening = [norm_piece, time_pieces[0], layer_pieces[0][0]]
    rest = [layer_pieces[0][1], bias_piece] + layer_pieces[0][2:] + [time_pieces[1]] + layer_pieces[1]
    for entry in opening + rest:
        entry.step(0)
    for number in (1, 2, 3):
        for entry in opening:
            entry.step(number)
    events = stagger(rest, (1, 2, 3, 4), LAG)

    def until(entry):
        last = events.index((entry, 4)) + 1
        first, events[:] = events[:last], events[last:]
        return first

    rows = lax.broadcasted_iota(jnp.int32, (8, 256), 0)
    angles = jnp.zeros((8, 256), F32)
    for item in range(items):
        step_value = steps_ref[t * items + item].astype(F32)
        angles = jnp.where(rows == item, step_value * freq_ref[0:1, :], angles)
    live = rows < items
    feats = jnp.concatenate(
        [jnp.where(live, jnp.sin(angles), 0.0), jnp.where(live, jnp.cos(angles), 0.0)], 1
    )
    feats_out[...] = feats
    feats_high = feats.astype(BF16)
    feats_low = (feats - feats_high.astype(F32)).astype(BF16)

    for entry in opening:
        entry.step(4)
    for zz in range(4):
        total = jnp.zeros((16, 128), F32)
        for part in range(8):
            total = total + nb[0, part % 2, zz, part // 2]
        norms[:, zz * 128 : (zz + 1) * 128] = total
    small_out[...] = norms[...]

    def spread_times(layer):
        table = [tw[layer, core].reshape(GROUPS, 16, 512) for core in range(2)]
        table = jnp.concatenate([table[0][:, None], table[1][:, None]], 1).reshape(512, 512)
        shifts[layer * 8 : (layer + 1) * 8] = nn(feats_high, table) + nn(feats_low, table)

    def spread_bias():
        for core in range(2):
            total = jnp.zeros((16, 128), F32)
            for part in range(16):
                total = total + nb[1, core, part // 4, part % 4]
            total = total.astype(BF16).astype(F32)
            for layer in range(LAYERS):
                for part in range(4):
                    for half in range(2):
                        row = layer * 8 + part * 2 + half
                        col = core * 256 + half * 128
                        bias[layer * 4 + part : layer * 4 + part + 1, col : col + 128] = total[row : row + 1]

    lane = lax.broadcasted_iota(jnp.int32, (1, 128), 1)
    even = lane < HEAD_DIM
    even_mask = jnp.where(even, 1.0, 0.0).astype(BF16)
    odd_mask = jnp.where(even, 0.0, 1.0).astype(BF16)

    def attention_phase(layer, agenda):
        def body(item, *refs):
            if layer == 0:
                x_blk, *refs = refs
            entry_blk, qkv_blk, probs_blk, attn_blk = refs
            here = pl.ds(pl.multiple_of(item * LENGTH, LENGTH), LENGTH)
            start = x_blk[...].astype(F32) if layer == 0 else stream[here]
            entry = start + shifts[pl.ds(layer * 8 + item, 1)]
            entry_blk[...] = entry
            stream[here] = entry
            hat, _ = normalize(entry)
            normed = (hat * norms[layer * 5 : layer * 5 + 1] + norms[layer * 5 + 1 : layer * 5 + 2]).astype(BF16)
            for slot in range(3):
                projected = nn(normed, weight(w.at[layer], slot)).astype(BF16)
                if slot == 0:
                    projected = projected * jnp.asarray(HEAD_DIM**-0.5, BF16)
                qkv_blk[:, slot * 512 : (slot + 1) * 512] = projected
            for pair in range(4):
                span = slice(pair * 128, (pair + 1) * 128)
                query = qkv_blk[:, span]
                key = qkv_blk[:, 512 + pair * 128 : 512 + (pair + 1) * 128]
                value = qkv_blk[:, 1024 + pair * 128 : 1024 + (pair + 1) * 128]
                mixed = []
                for side, mask in enumerate((even_mask, odd_mask)):
                    scores = nt(query * mask, key)
                    raised = jnp.exp(scores - jnp.max(scores, -1, keepdims=True))
                    probs = (raised * (1.0 / jnp.sum(raised, -1, keepdims=True))).astype(BF16)
                    probs_blk[0, pair * 2 + side] = probs
                    mixed.append(nn(probs, value))
                joined = jnp.where(even, mixed[0], mixed[1]).astype(BF16)
                attn_blk[:, span] = joined
                attn[here, span] = joined

        wide = lambda cols: pl.BlockSpec((LENGTH, cols), lambda i: (i, 0))
        each_item(
            body, agenda, items,
            [wide(512)] if layer == 0 else [],
            [wide(512), wide(1536), pl.BlockSpec((1, 8, 256, 256), lambda i: (i, 0, 0, 0)), wide(512)],
            ([x_ref] if layer == 0 else [])
            + [entry_out.at[layer], qkv_out.at[layer], probs_out.at[layer], attn_out.at[layer]],
        )

    def feed_phase(layer, agenda):
        def body(item, middle_blk, hidden_blk, slope_blk, *rest):
            here = pl.ds(pl.multiple_of(item * LENGTH, LENGTH), LENGTH)
            middle = stream[here] + nt(attn[here], weight(w.at[layer], 3))
            middle_blk[...] = middle
            hat, _ = normalize(middle)
            normed = (hat * norms[layer * 5 + 2 : layer * 5 + 3] + norms[layer * 5 + 3 : layer * 5 + 4]).astype(BF16)
            total = middle + norms[layer * 5 + 4 : layer * 5 + 5]
            for part in range(4):
                row = layer * 4 + part
                span = slice(part * 512, (part + 1) * 512)
                pre = nn(normed, weight(w.at[layer], 4 + part)) + bias[row : row + 1]
                hidden, slope = gelu_and_slope(pre)
                hidden = hidden.astype(BF16)
                hidden_blk[:, span] = hidden
                slope_blk[:, span] = slope.astype(BF16)
                total = total + nt(hidden, weight(w.at[layer], 8 + part))
            if layer == LAYERS - 1:
                rest[0][...] = total.astype(BF16)
            else:
                stream[here] = total

        wide = lambda cols: pl.BlockSpec((LENGTH, cols), lambda i: (i, 0))
        last = layer == LAYERS - 1
        each_item(
            body, agenda, items, [],
            [wide(512), wide(2048), wide(2048)] + ([wide(512)] if last else []),
            [middle_out.at[layer], hidden_out.at[layer], slope_out.at[layer]] + ([act_out] if last else []),
        )

    spread_times(0)
    keeps = []
    for layer in range(LAYERS):
        qkv_piece, out_piece, up_piece, down_piece = layer_pieces[layer]
        if layer > 0:
            spread_times(layer)
        attention_phase(layer, share(until(down_piece), AGENDA[layer][0]))
        if layer == 0:
            spread_bias()
        keep = pltpu.make_async_copy(w.at[layer], w_out.at[layer], keep_sem.at[layer])
        keep.start()
        keeps.append(keep)
        feed_phase(layer, share(until(layer_pieces[1][0]) if layer == 0 else [], AGENDA[layer][1]))
    for entry in pieces:
        entry.finish()
    for keep in keeps:
        keep.wait()


AGENDA = (((1, 2, 2, 3, 3), (2, 3, 3, 3, 3)), ((2, 3, 3, 3, 3), ()))


def forward_call(rep, rows, steps, freq, x, qkv, out, up, down, time, norm, bias):
    items = rows // LENGTH
    hbm = pl.BlockSpec(memory_space=pl.ANY)
    vmem = pl.BlockSpec(memory_space=pltpu.VMEM)
    smem = pl.BlockSpec(memory_space=pltpu.SMEM)
    shape = jax.ShapeDtypeStruct
    return pl.pallas_call(
        functools.partial(forward_kernel, rep),
        name="forward",
        in_specs=[smem, vmem, hbm] + [vmem] * 7,
        out_shape=[
            shape((LAYERS, 12, 2, 4, 4, 32, 256), BF16),
            shape((16, 512), F32),
            shape((8, 512), F32),
            shape((LAYERS, rows, 512), F32),
            shape((LAYERS, rows, 512), F32),
            shape((LAYERS, rows, 1536), BF16),
            shape((LAYERS, items, 8, 256, 256), BF16),
            shape((LAYERS, rows, 512), BF16),
            shape((LAYERS, rows, 2048), BF16),
            shape((LAYERS, rows, 2048), BF16),
            shape((rows, 512), BF16),
        ],
        out_specs=[hbm, vmem, vmem] + [hbm] * 8,
        scratch_shapes=[
            pltpu.VMEM((LAYERS, 12, 2, 4, 4, 32, 256), BF16),
            pltpu.VMEM((LAYERS, 2, 4, 4, 16, 512), BF16),
            pltpu.VMEM((2, 2, 4, 4, 16, 128), F32),
            pltpu.VMEM((16, 512), F32),
            pltpu.VMEM((8, 512), F32),
            pltpu.VMEM((16, 512), F32),
            pltpu.VMEM((rows, 512), F32),
            pltpu.VMEM((rows, 512), BF16),
            pltpu.SemaphoreType.DMA((GATHER_PIECES, 8)),
            pltpu.SemaphoreType.DMA((GATHER_PIECES, 8)),
            pltpu.SemaphoreType.DMA((LAYERS,)),
        ],
        compiler_params=pltpu.CompilerParams(collective_id=1, has_side_effects=True, vmem_limit_bytes=56 << 20),
    )(steps, freq, x, qkv, out, up, down, time, norm, bias)


class Scatter(Exchange):
    slots = 10

    def __init__(self, place, grads, received, total, groups, send, recv):
        self.place, self.grads, self.received, self.total = place, grads, received, total
        self.first, self.count = groups
        self.span = pl.ds(*groups)
        self.send, self.recv = send, recv

    def copy(self, slot):
        p, span = self.place, self.span
        core, diag_y, diag_x, col_x, col_y, along = self.received
        low, high = pl.ds(0, 2), pl.ds(2, 2)
        to_x, to_y = p.device(p.z, p.yx_x, p.t), p.device(p.z, p.yx_y, p.t)
        if slot == 0:
            src, dst, device = self.grads.at[span, 1 - p.t], core.at[span], p.device(p.z, p.yx, 1 - p.t)
        elif slot == 1:
            src, dst, device = self.grads.at[span, p.t, low, p.yx_d], diag_y.at[span], to_y
        elif slot == 2:
            src, dst, device = self.grads.at[span, p.t, high, p.yx_d], diag_x.at[span], to_x
        elif slot == 3:
            src, dst, device = self.grads.at[span, p.t, low, p.yx_x], col_x.at[span, low], to_x
        elif slot == 4:
            src, dst, device = self.grads.at[span, p.t, high, p.yx_y], col_y.at[span, high], to_y
        elif slot == 5:
            src, dst, device = self.grads.at[span, p.t, high, p.yx_x], col_x.at[span, high], to_x
        elif slot == 6:
            src, dst, device = self.grads.at[span, p.t, low, p.yx_y], col_y.at[span, low], to_y
        else:
            there = p.z_ahead(slot - 6)
            src, dst, device = self.grads.at[span, p.t, there, p.yx], along.at[slot - 7, span], p.device(there, p.yx, p.t)
        return self.remote(slot, src, dst, device)

    def add(self, where, terms):
        def one(group, carry):
            ref = self.grads.at[(group, self.place.t) + where]
            value = ref[...].astype(F32)
            for term in terms:
                value = value + term[group].astype(F32)
            ref[...] = value.astype(BF16)
            return carry

        lax.fori_loop(self.first, self.first + self.count, one, 0)

    def step(self, number):
        p = self.place
        core, diag_y, diag_x, col_x, col_y, along = self.received
        every = slice(None)
        if number == 0:
            self.start(0)
        elif number == 1:
            self.arrived(0)
            self.add((every, every), [core])
            for slot in (1, 2, 5, 6):
                self.start(slot)
        elif number == 2:
            self.arrived(1)
            self.add((pl.ds(0, 2), p.yx_x), [diag_y])
            self.start(3)
            self.arrived(2)
            self.add((pl.ds(2, 2), p.yx_y), [diag_x])
            self.start(4)
        elif number == 3:
            self.arrived(3, 4, 5, 6)
            self.add((every, p.yx), [col_x, col_y])
            for slot in (7, 8, 9):
                self.start(slot)
        elif number == 4:
            self.arrived(7, 8, 9)

            def one(group, carry):
                value = self.grads[group, p.t, p.z, p.yx].astype(F32)
                for k in range(3):
                    value = value + along[k, group].astype(F32)
                self.total[group] = value
                return carry

            lax.fori_loop(self.first, self.first + self.count, one, 0)


class SmallSum(Exchange):
    slots = 6

    def __init__(self, place, sums, received, total, send, recv):
        self.place, self.sums, self.received, self.total = place, sums, received, total
        self.send, self.recv = send, recv

    def copy(self, slot):
        p = self.place
        if slot == 0:
            device = p.device(p.z, p.yx, 1 - p.t)
        elif slot < 3:
            device = p.device(p.z, p.yx_x if slot == 1 else p.yx_y, p.t)
        else:
            device = p.device(p.z_ahead(slot - 2), p.yx, p.t)
        return self.remote(slot, self.sums.at[min(slot, 3)], self.received.at[slot], device)

    def step(self, number):
        if number > 0:
            slots = (3, 4, 5) if number == 4 else (number - 1,)
            value = self.sums[number - 1]
            self.arrived(*slots)
            for slot in slots:
                value = value + self.received[slot]
            if number < 4:
                self.sums[number] = value
            else:
                self.total[...] = value
        if number < 3:
            self.start(number)
        elif number == 3:
            for slot in (3, 4, 5):
                self.start(slot)


GRAD_GROUPS = 13
SCATTER_PIECES = ((4, 2), (6, 2), (8, 2), (10, 2), (3, 1), (0, 1), (1, 1), (2, 1), (12, 1))
BACK_AGENDA = ((3, 3, 3, 3, 3), (4, 4, 4, 4, 4))


def backward_kernel(
    rep,
    scale_ref, small_ref, feats_ref, cot_ref, w_in, entry_in, middle_in, qkv_in, probs_in, attn_in, hidden_in, slope_in,
    grad_out, total_out, sums_out, time_out,
    w, gx, dattn, du, hidden, attn, n1t, n2t, gdt, got, dqkv, grads, item_grad, acc, acc_bias,
    r_core, r_dy, r_dx, r_x, r_y, r_z, sums, r_sums, r_time,
    w_sem, in_sem, send, recv, small_send, small_recv, time_send, time_recv,
):
    place = Place(rep)
    t = place.t
    rows = gx.shape[0]
    items = rows // LENGTH
    wide = lambda cols: pl.BlockSpec((LENGTH, cols), lambda i: (i, 0))
    lane = lax.broadcasted_iota(jnp.int32, (1, 128), 1)
    even = lane < HEAD_DIM
    even_mask = jnp.where(even, 1.0, 0.0).astype(BF16)
    odd_mask = jnp.where(even, 0.0, 1.0).astype(BF16)

    def load_weights(layer):
        copies = []
        for number, (first, count) in enumerate(((3, 9), (0, 3))):
            copy = pltpu.make_async_copy(
                w_in.at[layer, pl.ds(first, count)], w.at[pl.ds(first, count)], w_sem.at[layer, number]
            )
            copies.append(copy)
        return copies

    def load_stash(layer):
        return [
            pltpu.make_async_copy(hidden_in.at[layer], hidden, in_sem.at[layer, 0]),
            pltpu.make_async_copy(attn_in.at[layer], attn, in_sem.at[layer, 1]),
        ]

    def norm_back(hat, inverse, dy, layer, row, here):
        acc[row] += fold_rows(dy * hat)
        acc[row + 1] += fold_rows(dy)
        scaled = dy * small_ref[layer * 5 + row : layer * 5 + row + 1]
        mean = jnp.mean(scaled, -1, keepdims=True)
        along = jnp.mean(scaled * hat, -1, keepdims=True)
        return inverse * (scaled - mean - hat * along)

    def feed_phase(layer, agenda):
        last = layer == LAYERS - 1

        def body(item, middle_blk, slope_blk, *rest):
            here = pl.ds(pl.multiple_of(item * LENGTH, LENGTH), LENGTH)
            if last:
                grad = rest[0][...].astype(F32) * scale_ref[t * items + item]
            else:
                grad = gx[here]
            acc[4] += fold_rows(grad)
            low = grad.astype(BF16)
            gdt[:, here] = low.T
            back = jnp.zeros((LENGTH, 512), F32)
            for part in range(4):
                span = slice(part * 512, (part + 1) * 512)
                dh = nn(low, weight(w, 8 + part))
                pre_grad = (dh * slope_blk[:, span].astype(F32)).astype(BF16)
                du[here, span] = pre_grad
                acc_bias[part] += fold_rows(pre_grad.astype(F32))
                back = back + nt(pre_grad, weight(w, 4 + part))
            hat, inverse = normalize(middle_blk[...])
            normed = hat * small_ref[layer * 5 + 2 : layer * 5 + 3] + small_ref[layer * 5 + 3 : layer * 5 + 4]
            n2t[:, here] = normed.astype(BF16).T
            grad = grad + norm_back(hat, inverse, back, layer, 2, here)
            gx[here] = grad
            low = grad.astype(BF16)
            got[:, here] = low.T
            dattn[here] = nn(low, weight(w, 3)).astype(BF16)

        each_item(
            body, agenda, items, [wide(512), wide(2048)] + ([wide(512)] if last else []), [],
            [middle_in.at[layer], slope_in.at[layer]] + ([cot_ref] if last else []),
        )

    def attention_phase(layer, agenda):
        def body(item, entry_blk, qkv_blk, probs_blk, *rest):
            here = pl.ds(pl.multiple_of(item * LENGTH, LENGTH), LENGTH)
            for pair in range(4):
                span = slice(pair * 128, (pair + 1) * 128)
                query = qkv_blk[:, span]
                key = qkv_blk[:, 512 + pair * 128 : 512 + (pair + 1) * 128]
                value = qkv_blk[:, 1024 + pair * 128 : 1024 + (pair + 1) * 128]
                back = dattn[here, span]
                found = []
                for side, mask in enumerate((even_mask, odd_mask)):
                    probs = probs_blk[0, pair * 2 + side]
                    dprobs = nt(back * mask, value)
                    wide_probs = probs.astype(F32)
                    delta = jnp.sum(wide_probs * dprobs, -1, keepdims=True)
                    dscores = (wide_probs * (dprobs - delta)).astype(BF16)
                    found.append((nn(dscores, key), tn(dscores, query), tn(probs, back)))
                dq, dk, dv = [jnp.where(even, found[0][i], found[1][i]) for i in range(3)]
                dqkv[here, span] = (dq * HEAD_DIM**-0.5).astype(BF16)
                dqkv[here, 512 + pair * 128 : 512 + (pair + 1) * 128] = dk.astype(BF16)
                dqkv[here, 1024 + pair * 128 : 1024 + (pair + 1) * 128] = dv.astype(BF16)
            back = jnp.zeros((LENGTH, 512), F32)
            for slot in range(3):
                back = back + nt(dqkv[here, slot * 512 : (slot + 1) * 512], weight(w, slot))
            hat, inverse = normalize(entry_blk[...])
            normed = hat * small_ref[layer * 5 : layer * 5 + 1] + small_ref[layer * 5 + 1 : layer * 5 + 2]
            n1t[:, here] = normed.astype(BF16).T
            grad = gx[here] + norm_back(hat, inverse, back, layer, 0, here)
            item_grad[pl.ds(item, 1)] = jnp.sum(grad, 0, keepdims=True)
            if layer == 0:
                rest[0][...] = grad.astype(BF16)
            else:
                gx[here] = grad

        each_item(
            body, agenda, items,
            [wide(512), wide(1536), pl.BlockSpec((1, 8, 256, 256), lambda i: (i, 0, 0, 0))],
            [wide(512)] if layer == 0 else [],
            [entry_in.at[layer], qkv_in.at[layer], probs_in.at[layer]] + ([grad_out] if layer == 0 else []),
        )

    def keep_grad(group, value):
        for half in range(2):
            grads[group, half] = value[:, half * 256 : (half + 1) * 256].astype(BF16).reshape(4, 4, 32, 256)

    def weight_grad(left, right, first, offset, count):
        def one(part, carry):
            span = pl.ds(pl.multiple_of((offset + part) * 512, 512), 512)
            keep_grad(first + part, nn(left[...], right[:, span]))
            return carry

        lax.fori_loop(0, count, one, 0)

    scatters, smalls = [], []
    for layer in range(LAYERS):
        received = [r.at[layer] for r in (r_core, r_dy, r_dx, r_x, r_y, r_z)]
        scatters.append(
            [
                Scatter(place, grads, received, total_out.at[layer], groups, send.at[layer, i], recv.at[layer, i])
                for i, groups in enumerate(SCATTER_PIECES)
            ]
        )
        smalls.append(
            SmallSum(place, sums.at[layer], r_sums.at[layer], sums_out.at[layer], small_send.at[layer], small_recv.at[layer])
        )

    order = [LAYERS - 1 - i for i in range(LAYERS)]
    weights = {order[0]: load_weights(order[0])}
    stash = {order[0]: load_stash(order[0])}
    for copy in weights[order[0]] + stash[order[0]]:
        copy.start()
    item_grad[...] = jnp.zeros(item_grad.shape, F32)
    place.greet()

    pending = []
    for turn, layer in enumerate(order):
        feed_pieces, late_pieces = scatters[layer][:5], scatters[layer][5:]
        acc[...] = jnp.zeros(acc.shape, F32)
        acc_bias[...] = jnp.zeros(acc_bias.shape, F32)
        weights[layer][0].wait()
        with jax.named_scope("feed_back"):
            feed_phase(layer, share(pending, BACK_AGENDA[1]))
        stash[layer][0].wait()
        stash[layer][1].wait()
        weights[layer][1].wait()
        if turn > 0:
            for piece in scatters[order[turn - 1]]:
                piece.finish()
        with jax.named_scope("feed_grads"):
            made = ((n2t, du, 4, 0), (n2t, du, 6, 2), (gdt, hidden, 8, 0), (gdt, hidden, 10, 2), (got, attn, 3, 0))
            pending = stagger(feed_pieces, (0, 1, 2, 3, 4), LAG)
            for piece, (left, right, first, part) in zip(feed_pieces, made):
                weight_grad(left, right, first, part, piece.count)
                ready = pending.index((piece, 0)) + 1
                play(pending[:ready])
                pending = pending[ready:]
        with jax.named_scope("attention_back"):
            attention_phase(layer, share(pending, BACK_AGENDA[0]))
        if turn + 1 < LAYERS:
            after = order[turn + 1]
            weights[after] = load_weights(after)
            stash[after] = load_stash(after)
            for copy in weights[after] + stash[after]:
                copy.start()
        with jax.named_scope("attention_grads"):
            spread = lax.dot_general(
                feats_ref[...], item_grad[...], (((0,), (0,)), ((), ())),
                precision=lax.Precision.HIGHEST, preferred_element_type=F32,
            )
            keep_grad(12, spread)
            for row in range(5):
                sums[layer, 0, row : row + 1] = jnp.sum(acc[row], 0, keepdims=True)
            for part in range(4):
                sums[layer, 0, 5 + part : 6 + part] = jnp.sum(acc_bias[part], 0, keepdims=True)
            sums[layer, 0, 9:16] = jnp.zeros((7, 512), F32)
            late_pieces = [late_pieces[3], smalls[layer]] + late_pieces[:3]
            pending = stagger(late_pieces, (0, 1, 2, 3, 4), LAG)
            for slot in range(3):
                weight_grad(n1t, dqkv, slot, slot, 1)
                ready = pending.index((late_pieces[2 + slot], 0)) + 1
                play(pending[:ready])
                pending = pending[ready:]
    with jax.named_scope("scatter"):
        play(pending)

    swaps = []
    for layer in range(LAYERS):
        swap = pltpu.make_async_remote_copy(
            src_ref=total_out.at[layer, 12, pl.ds(pl.multiple_of((1 - t) * 16, 16), 16)],
            dst_ref=r_time.at[layer], send_sem=time_send.at[layer], recv_sem=time_recv.at[layer],
            device_id=place.device(place.z, place.yx, 1 - t), device_id_type=MESH,
        )
        swap.start()
        swaps.append(swap)
    for layer in range(LAYERS):
        swaps[layer].wait()
        time_out[layer, :, place.cols] = total_out[layer, 12, pl.ds(pl.multiple_of(t * 16, 16), 16)]
        time_out[layer, :, place.other_cols] = r_time[layer]
    for piece in scatters[order[-1]]:
        piece.finish()
    for piece in smalls:
        piece.finish()


def backward_call(rep, rows, scale, small, feats, cot, w, entry, middle, qkv, probs, attn, hidden, slope):
    items = rows // LENGTH
    hbm = pl.BlockSpec(memory_space=pl.ANY)
    vmem = pl.BlockSpec(memory_space=pltpu.VMEM)
    smem = pl.BlockSpec(memory_space=pltpu.SMEM)
    shape = jax.ShapeDtypeStruct
    pieces = len(SCATTER_PIECES)
    dma = pltpu.SemaphoreType.DMA
    return pl.pallas_call(
        functools.partial(backward_kernel, rep),
        name="backward",
        in_specs=[smem, vmem, vmem] + [hbm] * 9,
        out_shape=[
            shape((rows, 512), BF16),
            shape((LAYERS, GRAD_GROUPS, 32, 256), F32),
            shape((LAYERS, 16, 512), F32),
            shape((LAYERS, 16, 512), F32),
        ],
        out_specs=[hbm, vmem, vmem, vmem],
        scratch_shapes=[
            pltpu.VMEM((12, 2, 4, 4, 32, 256), BF16),
            pltpu.VMEM((rows, 512), F32),
            pltpu.VMEM((rows, 512), BF16),
            pltpu.VMEM((rows, 2048), BF16),
            pltpu.VMEM((rows, 2048), BF16),
            pltpu.VMEM((rows, 512), BF16),
            pltpu.VMEM((512, rows), BF16),
            pltpu.VMEM((512, rows), BF16),
            pltpu.VMEM((512, rows), BF16),
            pltpu.VMEM((512, rows), BF16),
            pltpu.VMEM((rows, 1536), BF16),
            pltpu.VMEM((GRAD_GROUPS, 2, 4, 4, 32, 256), BF16),
            pltpu.VMEM((8, 512), F32),
            pltpu.VMEM((5, 8, 512), F32),
            pltpu.VMEM((4, 8, 512), F32),
            pltpu.VMEM((LAYERS, GRAD_GROUPS, 4, 4, 32, 256), BF16),
            pltpu.VMEM((LAYERS, GRAD_GROUPS, 2, 32, 256), BF16),
            pltpu.VMEM((LAYERS, GRAD_GROUPS, 2, 32, 256), BF16),
            pltpu.VMEM((LAYERS, GRAD_GROUPS, 4, 32, 256), BF16),
            pltpu.VMEM((LAYERS, GRAD_GROUPS, 4, 32, 256), BF16),
            pltpu.VMEM((LAYERS, 3, GRAD_GROUPS, 32, 256), BF16),
            pltpu.VMEM((LAYERS, 4, 16, 512), F32),
            pltpu.VMEM((LAYERS, 6, 16, 512), F32),
            pltpu.VMEM((LAYERS, 16, 256), F32),
            dma((LAYERS, 2)),
            dma((LAYERS, 2)),
            dma((LAYERS, pieces, 10)),
            dma((LAYERS, pieces, 10)),
            dma((LAYERS, 6)),
            dma((LAYERS, 6)),
            dma((LAYERS,)),
            dma((LAYERS,)),
        ],
        compiler_params=pltpu.CompilerParams(collective_id=2, has_side_effects=True, vmem_limit_bytes=62 << 20),
    )(scale, small, feats, cot, w, entry, middle, qkv, probs, attn, hidden, slope)


def adamw(weight, gradient, first_moment, second_moment, rate):
    first_new = beta_first * first_moment + (1.0 - beta_first) * gradient
    second_new = beta_second * second_moment + (1.0 - beta_second) * gradient * gradient
    first_corr = first_new * (1.0 / (1.0 - beta_first**STEP))
    second_corr = second_new * (1.0 / (1.0 - beta_second**STEP))
    weight_new = weight - rate * (first_corr / (jnp.sqrt(second_corr) + adam_eps) + weight_decay * weight)
    return (weight_new, first_new, second_new)


def update_kernel(total, sums, time_grad, *refs):
    ins, outs, (row,) = refs[:21], refs[21:43], refs[43:]
    qkv, out, up, bias, down, norm, time = [ins[i * 3 : i * 3 + 3] for i in range(7)]
    qkv_new, key_second, value_second = outs[0:2], outs[2], outs[3]
    out_new, up_new, bias_new, down_new, norm_new, time_new = [outs[4 + i * 3 : 7 + i * 3] for i in range(6)]
    dp, t = lax.axis_index("dp"), lax.axis_index("tensor")

    def one(old, new, where, gradient, rate):
        values = adamw(old[0][where], gradient, old[1][where], old[2][where], rate)
        for ref, value in zip(new, values):
            ref[where] = value
        return values

    for layer in range(LAYERS):
        for slot in range(3):
            values = adamw(qkv[0][layer, slot], total[layer, slot], qkv[1][layer, slot], qkv[2][layer, slot], learn_rate)
            for ref, value in zip(qkv_new, values):
                ref[layer, slot] = value
            if slot < 2:
                key_second[layer, :, slot] = values[2]
            else:
                value_second[layer] = values[2]
        one(out, out_new, (layer,), total[layer, 3], learn_rate)
        for part in range(4):
            where = (layer, slice(None), slice(part * 256, (part + 1) * 256))
            one(up, up_new, where, total[layer, 4 + part], learn_rate)
            one(down, down_new, where, total[layer, 8 + part], learn_rate)
        one(time, time_new, (layer,), time_grad[layer], learn_rate)

        width = norm[0].shape[2]
        start = (dp * 2 + t) * width
        tile = sums[layer, :, pl.ds(pl.multiple_of(start // 128 * 128, 128), 128)]
        mine = pltpu.roll(tile, (128 - start % 128) % 128, 1)[0:5, 0:width]
        one(norm, norm_new, (slice(None), layer), mine, norm_rate)
        for part in range(4):
            for half in range(2):
                span = pl.ds(pl.multiple_of(t * 256 + half * 128, 128), 128)
                row[part * 2 + half : part * 2 + half + 1] = sums[layer, 5 + part : 6 + part, span]
        width = bias[0].shape[2]
        mine = pltpu.roll(row[...], (128 - dp * width) % 128, 1)[:, 0:width]
        one(bias, bias_new, (layer,), mine, learn_rate)


def update_call(total, sums, time_grad, states):
    flat = [array for state in states for array in state]
    like = lambda array: jax.ShapeDtypeStruct(array.shape, F32)
    rows = states[0][0].shape[2]
    shapes = [like(array) for array in flat]
    shapes[2:3] = [
        jax.ShapeDtypeStruct((LAYERS, rows, 2, 256), F32),
        jax.ShapeDtypeStruct((LAYERS, rows, 256), F32),
    ]
    vmem = pl.BlockSpec(memory_space=pltpu.VMEM)
    return pl.pallas_call(
        update_kernel,
        name="update",
        in_specs=[vmem] * 24,
        out_shape=shapes,
        out_specs=[vmem] * 22,
        scratch_shapes=[pltpu.VMEM((8, 128), F32)],
        compiler_params=pltpu.CompilerParams(vmem_limit_bytes=48 << 20),
    )(total, sums, time_grad, *flat)


def per_device(
    rep,
    inputs, cotangent, timesteps, item_scale,
    qkv_weight, qkv_first, qkv_second,
    out_weight, out_first, out_second,
    up_weight, up_first, up_second,
    up_bias, bias_first, bias_second,
    down_weight, down_first, down_second,
    norm_params, norm_first, norm_second,
    time_weight, time_first, time_second,
):
    rows = inputs.shape[0]
    dp, t = lax.axis_index("dp"), lax.axis_index("tensor")
    group = dp // rep
    qkv, out, up, down, bias = qkv_weight, out_weight, up_weight, down_weight, up_bias
    norm, time = norm_params, time_weight
    teams = None
    if rep > 1:
        size = GROUPS * rep
        teams = [[g * rep + j for j in range(rep)] for g in range(GROUPS)]
        pairs = [[g * rep * 2 + j for j in range(rep * 2)] for g in range(GROUPS)]
        join = lambda v, axis: lax.all_gather(v, "dp", axis=axis, axis_index_groups=teams, tiled=True)
        join_both = lambda v, axis: lax.all_gather(
            v, ("dp", "tensor"), axis=axis, axis_index_groups=pairs, tiled=True
        )
        qkv, out, up, down, bias = join(qkv, 1), join(out, 2), join(up, 1), join(down, 2), join(bias, 2)
        norm, time = join_both(norm, 2), join_both(time, 1)
        norm = lax.dynamic_slice_in_dim(norm, t * 16, 16, 2)
        time = lax.dynamic_slice_in_dim(time, t * 16, 16, 1)

    lane = lax.broadcasted_iota(jnp.int32, (16, 128), 1)
    spot = (group % 4) * 2 + t
    norm_rows = jnp.pad(norm.reshape(10, 16), ((0, 6), (0, 0)))
    norm_block = jnp.where(lane // 16 == spot, jnp.tile(norm_rows, (1, 8)), 0.0)
    bias_block = jnp.where(lane // 8 == group, jnp.tile(bias.reshape(16, 8), (1, 16)), 0.0)
    half_width = 256
    freq = np.exp(-math.log(10000.0) / half_width * np.arange(half_width)).astype(np.float32)
    freq = jnp.asarray(np.broadcast_to(freq, (8, half_width)))

    w, small, feats, entry, middle, qkv_rows, probs, attn, hidden, slope, activations = forward_call(
        rep, rows, timesteps, freq, inputs,
        jnp.transpose(qkv, (0, 2, 1, 3)), jnp.swapaxes(out, 1, 2), up, jnp.swapaxes(down, 1, 2),
        time, norm_block, bias_block,
    )
    input_grad, total, sums, time_grad = backward_call(
        rep, rows, item_scale, small, feats, cotangent, w, entry, middle, qkv_rows, probs, attn, hidden, slope
    )

    if rep > 1:
        total = lax.psum_scatter(total, "dp", scatter_dimension=2, axis_index_groups=teams, tiled=True)
        sums, time_grad = lax.psum((sums, time_grad), "dp", axis_index_groups=teams)
        time_grad = lax.all_gather(time_grad, "tensor", axis=1, tiled=True)
        width = time_weight.shape[1]
        time_grad = lax.dynamic_slice_in_dim(time_grad, ((dp % rep) * 2 + t) * width, width, 1)

    slots = lambda *arrays: [jnp.transpose(v, (0, 2, 1, 3)) for v in arrays]
    flip = lambda *arrays: [jnp.swapaxes(v, 1, 2) for v in arrays]
    front = lambda *arrays: [jnp.swapaxes(v, 0, 1) for v in arrays]
    new = update_call(
        total, sums, time_grad,
        [
            slots(qkv_weight, qkv_first, qkv_second),
            flip(out_weight, out_first, out_second),
            [up_weight, up_first, up_second],
            [up_bias, bias_first, bias_second],
            flip(down_weight, down_first, down_second),
            front(norm_params, norm_first, norm_second),
            [time_weight, time_first, time_second],
        ],
    )
    return (
        activations, input_grad,
        *slots(*new[0:2]), new[2], new[3],
        *flip(*new[4:7]), *new[7:10], *new[10:13], *flip(*new[13:16]), *front(*new[16:19]), *new[19:22],
    )


def solution(mesh):
    rep = mesh.shape["dp"] // GROUPS
    shard = P(None, "dp", None, "tensor")
    rows = P(("dp", "tensor"), None)
    trans = P(None, "tensor", "dp")
    flat = P(None, "dp", "tensor")
    norm = P(None, None, ("dp", "tensor"))
    time = P(None, ("dp", "tensor"), None)
    return jax.shard_map(
        functools.partial(per_device, rep),
        mesh=mesh,
        in_specs=(rows, rows, P("dp"), P("dp")) + (shard,) * 3 + (trans,) * 3 + (flat,) * 3 + (trans,) * 6 + (norm,) * 3 + (time,) * 3,
        out_specs=(rows, rows, shard, shard, shard, flat) + (trans,) * 3 + (flat,) * 3 + (trans,) * 6 + (norm,) * 3 + (time,) * 3,
        check_vma=False,
    )
```

```python
import functools
import math

import jax
import jax.numpy as jnp
from jax import lax
from jax.experimental import pallas as pl
from jax.experimental.pallas import tpu as pltpu
from jax.sharding import PartitionSpec as P

HEAD_DIM = 64
LENGTH = 256
LAYERS = 2
STEP = 8
GROUPS = 16
MESH = pl.DeviceIdType.MESH
F32 = jnp.float32
BF16 = jnp.bfloat16

beta_first = 0.5
beta_second = 0.5
learn_rate = 0.1
norm_rate = 0.4
weight_decay = 0.01
adam_eps = 1e-08
norm_eps = 1e-05


def nn(a, b):
    return lax.dot_general(a, b, (((1,), (0,)), ((), ())), preferred_element_type=F32)


def nt(a, b):
    return lax.dot_general(a, b, (((1,), (1,)), ((), ())), preferred_element_type=F32)


def tn(a, b):
    return lax.dot_general(a, b, (((0,), (0,)), ((), ())), preferred_element_type=F32)


def normalize(values):
    center = values - jnp.mean(values, -1, keepdims=True)
    inverse = lax.rsqrt(jnp.mean(center * center, -1, keepdims=True) + norm_eps)
    return center * inverse, inverse


def fold_rows(values):
    rows, cols = values.shape
    return jnp.sum(values.reshape(rows // 8, 8, cols), 0)


def gelu_and_slope(x):
    below = 0.5 + 0.5 * lax.erf(x * math.sqrt(0.5))
    return x * below, below + x * (jnp.exp(x * x * -0.5) * (1.0 / math.sqrt(2.0 * math.pi)))


class Place:
    def __init__(self, rep):
        dp = lax.axis_index("dp")
        self.rep = rep
        self.copy = dp % rep
        self.group = dp // rep
        self.t = lax.axis_index("tensor")
        self.z = self.group // 4
        self.yx = self.group % 4
        x, y = self.yx % 2, self.yx // 2
        self.yx_x = self.yx + 1 - 2 * x
        self.yx_y = self.yx + 2 - 4 * y
        self.yx_d = 3 - self.yx
        self.cols = pl.ds(pl.multiple_of(self.t * 256, 256), 256)
        self.other_cols = pl.ds(pl.multiple_of((1 - self.t) * 256, 256), 256)

    def device(self, z, yx, t):
        return ((z * 4 + yx) * self.rep + self.copy, t)

    def z_ahead(self, k):
        return (self.z + k) % 4

    @property
    def partners(self):
        return [self.device(self.z_ahead(k), self.yx, self.t) for k in (1, 2, 3)] + [
            self.device(self.z, self.yx_x, self.t),
            self.device(self.z, self.yx_y, self.t),
            self.device(self.z, self.yx, 1 - self.t),
        ]

    def greet(self):
        barrier = pltpu.get_barrier_semaphore()
        for partner in self.partners:
            pl.semaphore_signal(barrier, inc=1, device_id=partner, device_id_type=MESH)
        pl.semaphore_wait(barrier, len(self.partners))


class Exchange:
    def start(self, slot):
        self.copy(slot).start()

    def arrived(self, *slots):
        for slot in slots:
            self.copy(slot).wait_recv()

    def finish(self):
        for slot in range(self.slots):
            self.copy(slot).wait_send()

    def remote(self, slot, src, dst, device):
        return pltpu.make_async_remote_copy(
            src_ref=src, dst_ref=dst, send_sem=self.send.at[slot], recv_sem=self.recv.at[slot],
            device_id=device, device_id_type=MESH,
        )


class Gather(Exchange):
    slots = 8

    def __init__(self, place, view, core_view, send, recv):
        self.place, self.view, self.core_view, self.send, self.recv = place, view, core_view, send, recv

    def copy(self, slot):
        p = self.place
        if slot < 3:
            ref, device = self.view(p.z, p.yx), p.device(p.z_ahead(slot + 1), p.yx, p.t)
        elif slot < 5:
            ref, device = self.view(slice(None), p.yx), p.device(p.z, p.yx_x if slot == 3 else p.yx_y, p.t)
        elif slot == 5:
            ref, device = self.view(pl.ds(0, 2), p.yx_x), p.device(p.z, p.yx_y, p.t)
        elif slot == 6:
            ref, device = self.view(pl.ds(2, 2), p.yx_y), p.device(p.z, p.yx_x, p.t)
        else:
            ref, device = self.core_view(), p.device(p.z, p.yx, 1 - p.t)
        return self.remote(slot, ref, ref, device)

    def step(self, number):
        if number == 0:
            for slot in (0, 1, 2):
                self.start(slot)
        elif number == 1:
            self.arrived(0, 1, 2)
            self.start(3)
            self.start(4)
        elif number == 2:
            self.arrived(3)
            self.start(5)
            self.arrived(4)
            self.start(6)
        elif number == 3:
            self.arrived(5, 6)
            self.start(7)
        elif number == 4:
            self.arrived(7)


def play(events):
    for piece, number in events:
        piece.step(number)


class Timeline:
    def __init__(self):
        self.now = 0.0
        self.queue = []
        self.links = 0.0
        self.along = 0.0
        self.count = 0

    def push(self, piece, dues):
        for number, due in enumerate(dues, 1):
            turn = self.count + (number - 1) * LAG
            self.queue.append((turn, number if FIRST else -number, due, number, piece))
        self.queue.sort(key=lambda event: event[:2])
        self.count += 1

    def gather(self, piece, unit):
        self.along += 4 * unit
        arrived = self.along + WAIT
        begun = max(self.links, arrived)
        self.links = begun + 6 * unit
        columns, diagonal = begun + 4 * unit + WAIT, begun + 8 * unit + WAIT
        self.push(piece, [max(arrived, begun - LEAD), columns, diagonal, diagonal + 1.6 * unit + WAIT])

    def scatter(self, piece, unit):
        added = self.now + 1.6 * unit + WAIT
        begun = max(self.links, added)
        self.links = begun + 6 * unit
        summed = begun + 8 * unit + WAIT
        self.along = max(self.along, summed) + 4 * unit
        self.push(piece, [max(added, begun - LEAD), begun + 4 * unit + WAIT, summed, self.along + WAIT])

    def small(self, piece):
        self.push(piece, [self.now + 3.0 * number for number in (1, 2, 3, 4)])

    def take(self, count):
        ready, self.queue = self.queue[:count], self.queue[count:]
        return [(piece, number) for _, _, _, number, piece in ready]

    def slot(self, length):
        count = 0
        while count < len(self.queue) and self.queue[count][2] <= self.now:
            count += 1
        self.now += length + COST * count
        return self.take(count)

    def passed(self, length):
        self.now += length

    def force(self, *wanted):
        count = max([i + 1 for i, event in enumerate(self.queue) if (event[4], event[3]) in wanted], default=0)
        self.now = max([self.now] + [event[2] for event in self.queue[:count]])
        return self.take(count)


WAIT = 2.0
LEAD = 2.0
LAG = 2
FIRST = True
COST = 0.2
UNIT = 0.33


def each_item(body, slots, count, in_specs, out_specs, refs):
    def whole(*blocks):
        item = pl.program_id(0)

        def poll(half):
            for number, events in enumerate(slots):
                if events[half]:
                    pl.when(item == number)(functools.partial(play, events[half]))

        poll(0)
        body(item, lambda: poll(1), *blocks)

    pltpu.emit_pipeline(whole, grid=(count,), in_specs=in_specs, out_specs=out_specs)(*refs)


GATHER_PIECES = 16


def weight(ref, group):
    return jnp.concatenate([ref[group, 0].reshape(512, 256), ref[group, 1].reshape(512, 256)], 1)


def forward_kernel(
    rep,
    steps_ref, x_ref, qkv_ref, out_ref, up_ref, down_ref, time_ref, norm_ref, bias_ref,
    w_out, small_out, feats_out, entry_out, middle_out, qkv_out, probs_out, attn_out, hidden_out, slope_out, act_out,
    w, tw, nb, norms, bias, shifts, stream, attn, rounded, tile, send, recv, keep_sem, act_sem,
):
    place = Place(rep)
    z, yx, t = place.z, place.yx, place.t
    rows = stream.shape[0]
    items = rows // LENGTH

    pieces = []

    def piece(ref, *lead):
        number = len(pieces)
        pieces.append(
            Gather(
                place,
                lambda a, b: ref.at[(*lead, t, a, b)],
                lambda: ref.at[(*lead, t)],
                send.at[number],
                recv.at[number],
            )
        )
        return pieces[-1]

    norm_piece, bias_piece = piece(nb, 0), piece(nb, 1)
    time_pieces = [piece(tw, layer) for layer in range(LAYERS)]
    spans = ((0, 3), (3, 1), (4, 2), (6, 2), (8, 2), (10, 2))
    layer_pieces = [[piece(w, layer, pl.ds(*span)) for span in spans] for layer in range(LAYERS)]

    tile[...] = jnp.zeros(tile.shape, F32)
    for layer in range(LAYERS):
        for row in range(5):
            at = layer * 5 + row
            tile[0, at : at + 1, 0:16] = norm_ref[row, layer : layer + 1]
        tile[1, layer * 8 : (layer + 1) * 8, 0:8] = bias_ref[layer]
    nb[0, t, z, yx] = pltpu.roll(tile[0], (yx * 2 + t) * 16, 1)
    nb[1, t, z, yx] = pltpu.roll(tile[1], place.group * 8, 1)

    def own_attention(layer):
        tw[layer, t, z, yx] = time_ref[layer].astype(BF16)
        for slot in range(3):
            w[layer, slot, t, z, yx] = qkv_ref[layer, slot].astype(BF16)

    def own_feed(layer):
        w[layer, 3, t, z, yx] = out_ref[layer].astype(BF16)
        for part in range(4):
            own = slice(part * 256, (part + 1) * 256)
            w[layer, 4 + 2 * part, t, z, yx] = up_ref[layer, :, own].astype(BF16)
            w[layer, 5 + 2 * part, t, z, yx] = down_ref[layer, :, own].astype(BF16)

    own_attention(0)
    place.greet()
    opening = [norm_piece, time_pieces[0], layer_pieces[0][0]]
    rest = [layer_pieces[0][1], bias_piece] + layer_pieces[0][2:] + [time_pieces[1]] + layer_pieces[1]
    for entry in opening:
        entry.step(0)
    own_feed(0)
    own_attention(1)
    own_feed(1)
    for entry in rest:
        entry.step(0)
    for number in (1, 2, 3):
        for entry in opening:
            entry.step(number)

    times = Timeline()
    times.along, times.links = 6.0, 1.0
    for entry in rest:
        count = 0.25 if entry is bias_piece else 2 if entry is time_pieces[1] else None
        if count is None:
            count = [span[1] for layer in layer_pieces for one, span in zip(layer, spans) if one is entry][0]
        times.gather(entry, UNIT * count)
    times.now = 4.0

    line = lax.broadcasted_iota(jnp.int32, (8, 256), 0)
    column = lax.broadcasted_iota(jnp.int32, (8, 256), 1).astype(F32)
    angles = jnp.zeros((8, 256), F32)
    for item in range(items):
        angles = jnp.where(line == item, steps_ref[t * items + item].astype(F32), angles)
    angles = angles * jnp.exp(column * (-math.log(10000.0) / 256))
    live = line < items
    feats = jnp.concatenate(
        [jnp.where(live, jnp.sin(angles), 0.0), jnp.where(live, jnp.cos(angles), 0.0)], 1
    )
    feats_out[...] = feats
    feats_high = feats.astype(BF16)
    feats_low = (feats - feats_high.astype(F32)).astype(BF16)

    for entry in opening:
        entry.step(4)
    for zz in range(4):
        total = jnp.zeros((16, 128), F32)
        for part in range(8):
            total = total + nb[0, part % 2, zz, part // 2]
        norms[:, zz * 128 : (zz + 1) * 128] = total
    small_out[...] = norms[...]

    def spread_times(layer):
        table = [tw[layer, core].reshape(GROUPS, 16, 512) for core in range(2)]
        table = jnp.concatenate([table[0][:, None], table[1][:, None]], 1).reshape(512, 512)
        shifts[layer * 8 : (layer + 1) * 8] = nn(feats_high, table) + nn(feats_low, table)

    def spread_bias():
        for core in range(2):
            total = jnp.zeros((16, 128), F32)
            for part in range(16):
                total = total + nb[1, core, part // 4, part % 4]
            total = total.astype(BF16).astype(F32)
            for layer in range(LAYERS):
                for part in range(4):
                    for half in range(2):
                        row = layer * 8 + part * 2 + half
                        col = core * 256 + half * 128
                        bias[layer, part, 0:1, col : col + 128] = total[row : row + 1]

    lane = lax.broadcasted_iota(jnp.int32, (1, 128), 1)
    even_mask = jnp.where(lane < HEAD_DIM, 1.0, 0.0).astype(BF16)
    odd_mask = jnp.where(lane < HEAD_DIM, 0.0, 1.0).astype(BF16)
    wide = lambda cols: pl.BlockSpec((LENGTH, cols), lambda i: (i, 0))

    def attention_phase(layer):
        def body(item, poll, *refs):
            if layer == 0:
                x_blk, *refs = refs
            entry_blk, qkv_blk, probs_blk, attn_blk = refs
            here = pl.ds(pl.multiple_of(item * LENGTH, LENGTH), LENGTH)
            start = x_blk[...].astype(F32) if layer == 0 else stream[here]
            entry = start + shifts[pl.ds(layer * 8 + item, 1)]
            entry_blk[...] = entry
            stream[here] = entry
            hat, _ = normalize(entry)
            normed = (hat * norms[layer * 5 : layer * 5 + 1] + norms[layer * 5 + 1 : layer * 5 + 2]).astype(BF16)
            for slot in range(3):
                projected = nn(normed, weight(w.at[layer], slot)).astype(BF16)
                if slot == 0:
                    projected = projected * jnp.asarray(HEAD_DIM**-0.5, BF16)
                qkv_blk[:, slot * 512 : (slot + 1) * 512] = projected

            def scores(pair):
                query = qkv_blk[:, pair * 128 : (pair + 1) * 128]
                key = qkv_blk[:, 512 + pair * 128 : 512 + (pair + 1) * 128]
                return [nt(query * mask, key) for mask in (even_mask, odd_mask)]

            ahead = scores(0)
            for pair in range(4):
                both = ahead
                if pair < 3:
                    ahead = scores(pair + 1)
                span = slice(pair * 128, (pair + 1) * 128)
                value = qkv_blk[:, 1024 + pair * 128 : 1024 + (pair + 1) * 128]
                probs = []
                for side in range(2):
                    raised = jnp.exp(both[side] - jnp.max(both[side], -1, keepdims=True))
                    probs.append((raised * (1.0 / jnp.sum(raised, -1, keepdims=True))).astype(BF16))
                    probs_blk[0, pair * 2 + side] = probs[side]
                values = jnp.concatenate([value * even_mask, value * odd_mask], 0)
                joined = nn(jnp.concatenate(probs, 1), values).astype(BF16)
                attn_blk[:, span] = joined
                attn[here, span] = joined

        each_item(
            body, [(times.slot(ATTENTION), []) for _ in range(items)], items,
            [wide(512)] if layer == 0 else [],
            [wide(512), wide(1536), pl.BlockSpec((1, 8, 256, 256), lambda i: (i, 0, 0, 0)), wide(512)],
            ([x_ref] if layer == 0 else [])
            + [entry_out.at[layer], qkv_out.at[layer], probs_out.at[layer], attn_out.at[layer]],
        )

    def middle_phase(layer):
        def body(item, poll, middle_blk):
            here = pl.ds(pl.multiple_of(item * LENGTH, LENGTH), LENGTH)
            middle = stream[here] + nt(attn[here], weight(w.at[layer], 3))
            middle_blk[...] = middle
            hat, _ = normalize(middle)
            normed = hat * norms[layer * 5 + 2 : layer * 5 + 3] + norms[layer * 5 + 3 : layer * 5 + 4]
            rounded[here] = normed.astype(BF16)
            stream[here] = middle + norms[layer * 5 + 4 : layer * 5 + 5]

        slots = [(times.slot(MIDDLE), []) for _ in range(items)]
        each_item(body, slots, items, [], [wide(512)], [middle_out.at[layer]])

    def feed_phase(layer, keep):
        def body(part, poll, hidden_blk, slope_blk):
            blocks = [slice(i * LENGTH, (i + 1) * LENGTH) for i in range(items)]
            up, down, shift = weight(w.at[layer], 4 + 2 * part), weight(w.at[layer], 5 + 2 * part), bias[layer, part]
            lift = lambda i: nn(rounded[blocks[i]], up) + shift[0:1]

            def lower(i, hidden):
                stream[blocks[i]] += nt(hidden, down)

            ahead, held = lift(0), None
            for i in range(items):
                pre = ahead
                if i + 1 < items:
                    ahead = lift(i + 1)
                hidden, slope = gelu_and_slope(pre)
                if held is not None:
                    lower(i - 1, held)
                held = hidden.astype(BF16)
                hidden_blk[blocks[i]] = held
                slope_blk[blocks[i]] = slope.astype(BF16)
            lower(items - 1, held)

        slots = []
        for part in range(4):
            entry = layer_pieces[layer][2 + part]
            slots.append((times.force((entry, 4)) + [(Start(keep[2 + part]), 0)], []))
            times.passed(FEED)
        tall = pl.BlockSpec((rows, 512), lambda i: (0, i))
        each_item(body, slots, 4, [], [tall, tall], [hidden_out.at[layer], slope_out.at[layer]])

    spread_times(0)
    keeps = []
    for layer in range(LAYERS):
        keep = [
            pltpu.make_async_copy(w.at[layer, pl.ds(*span)], w_out.at[layer, pl.ds(*span)], keep_sem.at[layer, i])
            for i, span in enumerate(spans)
        ]
        keeps += keep
        if layer > 0:
            play(times.force((time_pieces[layer], 4), (layer_pieces[layer][0], 4)))
            spread_times(layer)
        keep[0].start()
        attention_phase(layer)
        play(times.force((layer_pieces[layer][1], 4), (bias_piece, 4)))
        keep[1].start()
        if layer == 0:
            spread_bias()
        middle_phase(layer)
        feed_phase(layer, keep)

    def finish_rows(item, carry):
        here = pl.ds(pl.multiple_of(item * LENGTH, LENGTH), LENGTH)
        rounded[here] = stream[here].astype(BF16)
        return carry

    lax.fori_loop(0, items, finish_rows, 0)
    last = pltpu.make_async_copy(rounded, act_out, act_sem)
    last.start()
    for entry in pieces:
        entry.finish()
    for copy in keeps + [last]:
        copy.wait()


ATTENTION, MIDDLE, FEED = 2.4, 0.8, 2.6
FEED_BACK, ATTENTION_BACK, GRAD = 2.2, 4.0, 0.9


class Start:
    def __init__(self, copy):
        self.copy = copy

    def step(self, number):
        self.copy.start()


def forward_call(rep, rows, steps, x, qkv, out, up, down, time, norm, bias):
    items = rows // LENGTH
    hbm = pl.BlockSpec(memory_space=pl.ANY)
    vmem = pl.BlockSpec(memory_space=pltpu.VMEM)
    smem = pl.BlockSpec(memory_space=pltpu.SMEM)
    shape = jax.ShapeDtypeStruct
    return pl.pallas_call(
        functools.partial(forward_kernel, rep),
        name="forward",
        in_specs=[smem, hbm] + [vmem] * 7,
        out_shape=[
            shape((LAYERS, 12, 2, 4, 4, 32, 256), BF16),
            shape((16, 512), F32),
            shape((8, 512), F32),
            shape((LAYERS, rows, 512), F32),
            shape((LAYERS, rows, 512), F32),
            shape((LAYERS, rows, 1536), BF16),
            shape((LAYERS, items, 8, 256, 256), BF16),
            shape((LAYERS, rows, 512), BF16),
            shape((LAYERS, rows, 2048), BF16),
            shape((LAYERS, rows, 2048), BF16),
            shape((rows, 512), BF16),
        ],
        out_specs=[hbm, vmem, vmem] + [hbm] * 8,
        scratch_shapes=[
            pltpu.VMEM((LAYERS, 12, 2, 4, 4, 32, 256), BF16),
            pltpu.VMEM((LAYERS, 2, 4, 4, 16, 512), BF16),
            pltpu.VMEM((2, 2, 4, 4, 16, 128), F32),
            pltpu.VMEM((16, 512), F32),
            pltpu.VMEM((LAYERS, 4, 8, 512), F32),
            pltpu.VMEM((16, 512), F32),
            pltpu.VMEM((rows, 512), F32),
            pltpu.VMEM((rows, 512), BF16),
            pltpu.VMEM((rows, 512), BF16),
            pltpu.VMEM((2, 16, 128), F32),
            pltpu.SemaphoreType.DMA((GATHER_PIECES, 8)),
            pltpu.SemaphoreType.DMA((GATHER_PIECES, 8)),
            pltpu.SemaphoreType.DMA((LAYERS, 6)),
            pltpu.SemaphoreType.DMA,
        ],
        compiler_params=pltpu.CompilerParams(collective_id=1, has_side_effects=True, vmem_limit_bytes=56 << 20),
    )(steps, x, qkv, out, up, down, time, norm, bias)


class Scatter(Exchange):
    slots = 10

    def __init__(self, place, grads, received, total, groups, send, recv):
        self.place, self.grads, self.received, self.total = place, grads, received, total
        self.first, self.count = groups
        self.span = pl.ds(*groups)
        self.send, self.recv = send, recv

    def copy(self, slot):
        p, span = self.place, self.span
        core, diag_y, diag_x, col_x, col_y, along = self.received
        low, high = pl.ds(0, 2), pl.ds(2, 2)
        to_x, to_y = p.device(p.z, p.yx_x, p.t), p.device(p.z, p.yx_y, p.t)
        if slot == 0:
            src, dst, device = self.grads.at[span, 1 - p.t], core.at[span], p.device(p.z, p.yx, 1 - p.t)
        elif slot == 1:
            src, dst, device = self.grads.at[span, p.t, low, p.yx_d], diag_y.at[span], to_y
        elif slot == 2:
            src, dst, device = self.grads.at[span, p.t, high, p.yx_d], diag_x.at[span], to_x
        elif slot == 3:
            src, dst, device = self.grads.at[span, p.t, low, p.yx_x], col_x.at[span, low], to_x
        elif slot == 4:
            src, dst, device = self.grads.at[span, p.t, high, p.yx_y], col_y.at[span, high], to_y
        elif slot == 5:
            src, dst, device = self.grads.at[span, p.t, high, p.yx_x], col_x.at[span, high], to_x
        elif slot == 6:
            src, dst, device = self.grads.at[span, p.t, low, p.yx_y], col_y.at[span, low], to_y
        else:
            there = p.z_ahead(slot - 6)
            src, dst, device = self.grads.at[span, p.t, there, p.yx], along.at[slot - 7, span], p.device(there, p.yx, p.t)
        return self.remote(slot, src, dst, device)

    def add(self, where, terms):
        def one(group, carry):
            ref = self.grads.at[(group, self.place.t) + where]
            value = ref[...].astype(F32)
            for term in terms:
                value = value + term[group].astype(F32)
            ref[...] = value.astype(BF16)
            return carry

        lax.fori_loop(self.first, self.first + self.count, one, 0)

    def step(self, number):
        p = self.place
        core, diag_y, diag_x, col_x, col_y, along = self.received
        every = slice(None)
        if number == 0:
            self.start(0)
        elif number == 1:
            self.arrived(0)
            self.add((every, every), [core])
            for slot in (1, 2, 5, 6):
                self.start(slot)
        elif number == 2:
            self.arrived(1)
            self.add((pl.ds(0, 2), p.yx_x), [diag_y])
            self.start(3)
            self.arrived(2)
            self.add((pl.ds(2, 2), p.yx_y), [diag_x])
            self.start(4)
        elif number == 3:
            self.arrived(3, 4, 5, 6)
            self.add((every, p.yx), [col_x, col_y])
            for slot in (7, 8, 9):
                self.start(slot)
        elif number == 4:
            self.arrived(7, 8, 9)

            def one(group, carry):
                value = self.grads[group, p.t, p.z, p.yx].astype(F32)
                for k in range(3):
                    value = value + along[k, group].astype(F32)
                self.total[group] = value
                return carry

            lax.fori_loop(self.first, self.first + self.count, one, 0)


class SmallSum(Exchange):
    slots = 6

    def __init__(self, place, sums, received, total, send, recv):
        self.place, self.sums, self.received, self.total = place, sums, received, total
        self.send, self.recv = send, recv

    def copy(self, slot):
        p = self.place
        if slot == 0:
            device = p.device(p.z, p.yx, 1 - p.t)
        elif slot < 3:
            device = p.device(p.z, p.yx_x if slot == 1 else p.yx_y, p.t)
        else:
            device = p.device(p.z_ahead(slot - 2), p.yx, p.t)
        return self.remote(slot, self.sums.at[min(slot, 3)], self.received.at[slot], device)

    def step(self, number):
        if number > 0:
            slots = (3, 4, 5) if number == 4 else (number - 1,)
            value = self.sums[number - 1]
            self.arrived(*slots)
            for slot in slots:
                value = value + self.received[slot]
            if number < 4:
                self.sums[number] = value
            else:
                self.total[...] = value
        if number < 3:
            self.start(number)
        elif number == 3:
            for slot in (3, 4, 5):
                self.start(slot)


GRAD_GROUPS = 13
SCATTER_PIECES = ((4, 2), (6, 2), (8, 2), (10, 2), (3, 1), (0, 1), (1, 1), (2, 1), (12, 1))


def backward_kernel(
    rep,
    scale_ref, small_ref, feats_ref, cot_ref, w_in, entry_in, middle_in, qkv_in, probs_in, attn_in, hidden_in, slope_in,
    grad_out, total_out, sums_out, time_out,
    w, gx, dattn, du, hidden, attn, n1t, n2t, gdt, got, dqkv, grads, item_grad, acc, acc_bias,
    r_core, r_dy, r_dx, r_x, r_y, r_z, sums, r_sums, r_time,
    w_sem, in_sem, send, recv, small_send, small_recv, time_send, time_recv,
):
    place = Place(rep)
    t = place.t
    rows = gx.shape[0]
    items = rows // LENGTH
    wide = lambda cols: pl.BlockSpec((LENGTH, cols), lambda i: (i, 0))
    lane = lax.broadcasted_iota(jnp.int32, (1, 128), 1)
    even_mask = jnp.where(lane < HEAD_DIM, 1.0, 0.0).astype(BF16)
    odd_mask = jnp.where(lane < HEAD_DIM, 0.0, 1.0).astype(BF16)
    times = Timeline()

    def load_weights(layer):
        copies = []
        for number, (first, count) in enumerate(((3, 9), (0, 3))):
            copy = pltpu.make_async_copy(
                w_in.at[layer, pl.ds(first, count)], w.at[pl.ds(first, count)], w_sem.at[layer, number]
            )
            copies.append(copy)
        return copies

    def load_stash(layer):
        return [
            pltpu.make_async_copy(hidden_in.at[layer], hidden, in_sem.at[layer, 0]),
            pltpu.make_async_copy(attn_in.at[layer], attn, in_sem.at[layer, 1]),
        ]

    def norm_back(hat, inverse, dy, layer, row, here):
        acc[row] += fold_rows(dy * hat)
        acc[row + 1] += fold_rows(dy)
        scaled = dy * small_ref[layer * 5 + row : layer * 5 + row + 1]
        mean = jnp.mean(scaled, -1, keepdims=True)
        along = jnp.mean(scaled * hat, -1, keepdims=True)
        return inverse * (scaled - mean - hat * along)

    def feed_phase(layer):
        last = layer == LAYERS - 1

        def body(item, poll, middle_blk, slope_blk, *rest):
            here = pl.ds(pl.multiple_of(item * LENGTH, LENGTH), LENGTH)
            if last:
                grad = rest[0][...].astype(F32) * scale_ref[t * items + item]
            else:
                grad = gx[here]
            acc[4] += fold_rows(grad)
            low = grad.astype(BF16)
            gdt[:, here] = low.T
            back = jnp.zeros((LENGTH, 512), F32)
            for part in range(4):
                span = slice(part * 512, (part + 1) * 512)
                dh = nn(low, weight(w, 5 + 2 * part))
                pre_grad = (dh * slope_blk[:, span].astype(F32)).astype(BF16)
                du[here, span] = pre_grad
                acc_bias[part] += fold_rows(pre_grad.astype(F32))
                back = back + nt(pre_grad, weight(w, 4 + 2 * part))
            hat, inverse = normalize(middle_blk[...])
            normed = hat * small_ref[layer * 5 + 2 : layer * 5 + 3] + small_ref[layer * 5 + 3 : layer * 5 + 4]
            n2t[:, here] = normed.astype(BF16).T
            grad = grad + norm_back(hat, inverse, back, layer, 2, here)
            gx[here] = grad
            low = grad.astype(BF16)
            got[:, here] = low.T
            dattn[here] = nn(low, weight(w, 3)).astype(BF16)

        each_item(
            body, [(times.slot(FEED_BACK), []) for _ in range(items)], items, [wide(512), wide(2048)] + ([wide(512)] if last else []), [],
            [middle_in.at[layer], slope_in.at[layer]] + ([cot_ref] if last else []),
        )

    def attention_phase(layer):
        def body(item, poll, entry_blk, qkv_blk, probs_blk, *rest):
            here = pl.ds(pl.multiple_of(item * LENGTH, LENGTH), LENGTH)
            def sides(pair):
                query = qkv_blk[:, pair * 128 : (pair + 1) * 128]
                key = qkv_blk[:, 512 + pair * 128 : 512 + (pair + 1) * 128]
                value = qkv_blk[:, 1024 + pair * 128 : 1024 + (pair + 1) * 128]
                back = dattn[here, pair * 128 : (pair + 1) * 128]
                split = lambda v: [v * even_mask, v * odd_mask]
                return split(query), split(key), value, split(back)

            def scores(pair):
                _, _, value, back = sides(pair)
                return [nt(side, value) for side in back]

            def products(pair, dscores):
                query, key, _, back = sides(pair)
                probs = [probs_blk[0, pair * 2 + side] for side in range(2)]
                tall = jnp.concatenate(dscores, 0)
                dq = nn(jnp.concatenate(dscores, 1), jnp.concatenate(key, 0)) * HEAD_DIM**-0.5
                dk = tn(tall, jnp.concatenate(query, 0))
                dv = tn(jnp.concatenate(probs, 0), jnp.concatenate(back, 0))
                for slot, value in enumerate((dq, dk, dv)):
                    dqkv[here, slot * 512 + pair * 128 : slot * 512 + (pair + 1) * 128] = value.astype(BF16)

            ahead, held = scores(0), None
            for pair in range(4):
                both = ahead
                if pair == 2:
                    poll()
                if pair < 3:
                    ahead = scores(pair + 1)
                dscores = []
                for side in range(2):
                    probs = probs_blk[0, pair * 2 + side].astype(F32)
                    mixed = probs * both[side]
                    dscores.append((mixed - probs * jnp.sum(mixed, -1, keepdims=True)).astype(BF16))
                if held is not None:
                    products(pair - 1, held)
                held = dscores
            products(3, held)
            back = jnp.zeros((LENGTH, 512), F32)
            for slot in range(3):
                back = back + nt(dqkv[here, slot * 512 : (slot + 1) * 512], weight(w, slot))
            hat, inverse = normalize(entry_blk[...])
            normed = hat * small_ref[layer * 5 : layer * 5 + 1] + small_ref[layer * 5 + 1 : layer * 5 + 2]
            n1t[:, here] = normed.astype(BF16).T
            grad = gx[here] + norm_back(hat, inverse, back, layer, 0, here)
            item_grad[pl.ds(item, 1)] = jnp.sum(grad, 0, keepdims=True)
            if layer == 0:
                rest[0][...] = grad.astype(BF16)
            else:
                gx[here] = grad

        slots = [(times.slot(ATTENTION_BACK / 2), times.slot(ATTENTION_BACK / 2)) for _ in range(items)]
        each_item(
            body, slots, items,
            [wide(512), wide(1536), pl.BlockSpec((1, 8, 256, 256), lambda i: (i, 0, 0, 0))],
            [wide(512)] if layer == 0 else [],
            [entry_in.at[layer], qkv_in.at[layer], probs_in.at[layer]] + ([grad_out] if layer == 0 else []),
        )

    def keep_grad(group, value):
        for half in range(2):
            grads[group, half] = value[:, half * 256 : (half + 1) * 256].astype(BF16).reshape(4, 4, 32, 256)

    def weight_grad(left, right, group, part):
        keep_grad(group, nn(left[...], right[:, part * 512 : (part + 1) * 512]))

    scatters, smalls = [], []
    for layer in range(LAYERS):
        received = [r.at[layer] for r in (r_core, r_dy, r_dx, r_x, r_y, r_z)]
        scatters.append(
            [
                Scatter(place, grads, received, total_out.at[layer], groups, send.at[layer, i], recv.at[layer, i])
                for i, groups in enumerate(SCATTER_PIECES)
            ]
        )
        smalls.append(
            SmallSum(place, sums.at[layer], r_sums.at[layer], sums_out.at[layer], small_send.at[layer], small_recv.at[layer])
        )

    order = [LAYERS - 1 - i for i in range(LAYERS)]
    weights = {order[0]: load_weights(order[0])}
    stash = {order[0]: load_stash(order[0])}
    for copy in weights[order[0]] + stash[order[0]]:
        copy.start()
    item_grad[...] = jnp.zeros(item_grad.shape, F32)
    place.greet()

    def clear(layer, piece):
        if layer != order[0]:
            before = scatters[order[order.index(layer) - 1]][scatters[layer].index(piece)]
            play(times.force((before, 4)))
            before.finish()

    def begin(piece):
        piece.step(0)
        times.scatter(piece, UNIT * piece.count)

    for turn, layer in enumerate(order):
        feed_pieces, late_pieces = scatters[layer][:5], scatters[layer][5:]
        acc[...] = jnp.zeros(acc.shape, F32)
        acc_bias[...] = jnp.zeros(acc_bias.shape, F32)
        weights[layer][0].wait()
        feed_phase(layer)
        stash[layer][0].wait()
        stash[layer][1].wait()
        weights[layer][1].wait()
        for part, piece in enumerate(feed_pieces):
            clear(layer, piece)
            if part < 4:
                weight_grad(n2t, du, 4 + 2 * part, part)
                weight_grad(gdt, hidden, 5 + 2 * part, part)
            else:
                weight_grad(got, attn, 3, 0)
            times.passed(GRAD * piece.count)
            begin(piece)
            play(times.slot(0.0))
        attention_phase(layer)
        if turn + 1 < LAYERS:
            after = order[turn + 1]
            weights[after] = load_weights(after)
            stash[after] = load_stash(after)
            for copy in weights[after] + stash[after]:
                copy.start()
        for piece in late_pieces:
            clear(layer, piece)
        spread = lax.dot_general(
            feats_ref[...], item_grad[...], (((0,), (0,)), ((), ())),
            precision=lax.Precision.HIGHEST, preferred_element_type=F32,
        )
        keep_grad(12, spread)
        begin(late_pieces[3])
        for row in range(5):
            sums[layer, 0, row : row + 1] = jnp.sum(acc[row], 0, keepdims=True)
        for part in range(4):
            sums[layer, 0, 5 + part : 6 + part] = jnp.sum(acc_bias[part], 0, keepdims=True)
        sums[layer, 0, 9:16] = jnp.zeros((7, 512), F32)
        smalls[layer].step(0)
        times.small(smalls[layer])
        for slot in range(3):
            weight_grad(n1t, dqkv, slot, slot)
            times.passed(GRAD)
            begin(late_pieces[slot])
            play(times.slot(0.0))
    play(times.force(*[(piece, 4) for layer in range(LAYERS) for piece in scatters[layer] + [smalls[layer]]]))

    swaps = []
    for layer in range(LAYERS):
        swap = pltpu.make_async_remote_copy(
            src_ref=total_out.at[layer, 12, pl.ds(pl.multiple_of((1 - t) * 16, 16), 16)],
            dst_ref=r_time.at[layer], send_sem=time_send.at[layer], recv_sem=time_recv.at[layer],
            device_id=place.device(place.z, place.yx, 1 - t), device_id_type=MESH,
        )
        swap.start()
        swaps.append(swap)
    for layer in range(LAYERS):
        swaps[layer].wait()
        time_out[layer, :, place.cols] = total_out[layer, 12, pl.ds(pl.multiple_of(t * 16, 16), 16)]
        time_out[layer, :, place.other_cols] = r_time[layer]
    for piece in scatters[order[-1]]:
        piece.finish()
    for piece in smalls:
        piece.finish()


def backward_call(rep, rows, scale, small, feats, cot, w, entry, middle, qkv, probs, attn, hidden, slope):
    items = rows // LENGTH
    hbm = pl.BlockSpec(memory_space=pl.ANY)
    vmem = pl.BlockSpec(memory_space=pltpu.VMEM)
    smem = pl.BlockSpec(memory_space=pltpu.SMEM)
    shape = jax.ShapeDtypeStruct
    pieces = len(SCATTER_PIECES)
    dma = pltpu.SemaphoreType.DMA
    return pl.pallas_call(
        functools.partial(backward_kernel, rep),
        name="backward",
        in_specs=[smem, vmem, vmem] + [hbm] * 9,
        out_shape=[
            shape((rows, 512), BF16),
            shape((LAYERS, GRAD_GROUPS, 32, 256), F32),
            shape((LAYERS, 16, 512), F32),
            shape((LAYERS, 16, 512), F32),
        ],
        out_specs=[hbm, vmem, vmem, vmem],
        scratch_shapes=[
            pltpu.VMEM((12, 2, 4, 4, 32, 256), BF16),
            pltpu.VMEM((rows, 512), F32),
            pltpu.VMEM((rows, 512), BF16),
            pltpu.VMEM((rows, 2048), BF16),
            pltpu.VMEM((rows, 2048), BF16),
            pltpu.VMEM((rows, 512), BF16),
            pltpu.VMEM((512, rows), BF16),
            pltpu.VMEM((512, rows), BF16),
            pltpu.VMEM((512, rows), BF16),
            pltpu.VMEM((512, rows), BF16),
            pltpu.VMEM((rows, 1536), BF16),
            pltpu.VMEM((GRAD_GROUPS, 2, 4, 4, 32, 256), BF16),
            pltpu.VMEM((8, 512), F32),
            pltpu.VMEM((5, 8, 512), F32),
            pltpu.VMEM((4, 8, 512), F32),
            pltpu.VMEM((LAYERS, GRAD_GROUPS, 4, 4, 32, 256), BF16),
            pltpu.VMEM((LAYERS, GRAD_GROUPS, 2, 32, 256), BF16),
            pltpu.VMEM((LAYERS, GRAD_GROUPS, 2, 32, 256), BF16),
            pltpu.VMEM((LAYERS, GRAD_GROUPS, 4, 32, 256), BF16),
            pltpu.VMEM((LAYERS, GRAD_GROUPS, 4, 32, 256), BF16),
            pltpu.VMEM((LAYERS, 3, GRAD_GROUPS, 32, 256), BF16),
            pltpu.VMEM((LAYERS, 4, 16, 512), F32),
            pltpu.VMEM((LAYERS, 6, 16, 512), F32),
            pltpu.VMEM((LAYERS, 16, 256), F32),
            dma((LAYERS, 2)),
            dma((LAYERS, 2)),
            dma((LAYERS, pieces, 10)),
            dma((LAYERS, pieces, 10)),
            dma((LAYERS, 6)),
            dma((LAYERS, 6)),
            dma((LAYERS,)),
            dma((LAYERS,)),
        ],
        compiler_params=pltpu.CompilerParams(collective_id=2, has_side_effects=True, vmem_limit_bytes=62 << 20),
    )(scale, small, feats, cot, w, entry, middle, qkv, probs, attn, hidden, slope)


def adamw(weight, gradient, first_moment, second_moment, rate):
    first_new = beta_first * first_moment + (1.0 - beta_first) * gradient
    second_new = beta_second * second_moment + (1.0 - beta_second) * gradient * gradient
    first_corr = first_new * (1.0 / (1.0 - beta_first**STEP))
    second_corr = second_new * (1.0 / (1.0 - beta_second**STEP))
    weight_new = weight - rate * (first_corr / (jnp.sqrt(second_corr) + adam_eps) + weight_decay * weight)
    return (weight_new, first_new, second_new)


def update_kernel(*refs):
    hbm, outs, ins = refs[:26], refs[26:50], refs[50:74]
    row, sems = refs[74:]
    copies = [pltpu.make_async_copy(src, dst, sems.at[i]) for i, (src, dst) in enumerate(zip(hbm[:24], ins))]
    copies += [pltpu.make_async_copy(hbm[24 + i], outs[i], sems.at[24 + i]) for i in range(2)]
    for copy in copies:
        copy.start()
    for copy in copies[:24]:
        copy.wait()
    total, sums, time_grad, *ins = ins
    outs = outs[2:]
    qkv, out, up, bias, down, norm, time = [ins[i * 3 : i * 3 + 3] for i in range(7)]
    qkv_new, key_second, value_second = outs[0:2], outs[2], outs[3]
    out_new, up_new, bias_new, down_new, norm_new, time_new = [outs[4 + i * 3 : 7 + i * 3] for i in range(6)]
    dp, t = lax.axis_index("dp"), lax.axis_index("tensor")

    def one(old, new, where, gradient, rate):
        values = adamw(old[0][where], gradient, old[1][where], old[2][where], rate)
        for ref, value in zip(new, values):
            ref[where] = value
        return values

    for layer in range(LAYERS):
        for slot in range(3):
            values = adamw(qkv[0][layer, slot], total[layer, slot], qkv[1][layer, slot], qkv[2][layer, slot], learn_rate)
            for ref, value in zip(qkv_new, values):
                ref[layer, slot] = value
            if slot < 2:
                key_second[layer, :, slot] = values[2]
            else:
                value_second[layer] = values[2]
        one(out, out_new, (layer,), total[layer, 3], learn_rate)
        for part in range(4):
            where = (layer, slice(None), slice(part * 256, (part + 1) * 256))
            one(up, up_new, where, total[layer, 4 + 2 * part], learn_rate)
            one(down, down_new, where, total[layer, 5 + 2 * part], learn_rate)
        one(time, time_new, (layer,), time_grad[layer], learn_rate)

        width = norm[0].shape[2]
        start = (dp * 2 + t) * width
        tile = sums[layer, :, pl.ds(pl.multiple_of(start // 128 * 128, 128), 128)]
        mine = pltpu.roll(tile, (128 - start % 128) % 128, 1)[0:5, 0:width]
        one(norm, norm_new, (slice(None), layer), mine, norm_rate)
        for part in range(4):
            for half in range(2):
                span = pl.ds(pl.multiple_of(t * 256 + half * 128, 128), 128)
                row[part * 2 + half : part * 2 + half + 1] = sums[layer, 5 + part : 6 + part, span]
        width = bias[0].shape[2]
        mine = pltpu.roll(row[...], (128 - dp * width) % 128, 1)[:, 0:width]
        one(bias, bias_new, (layer,), mine, learn_rate)
    for copy in copies[24:]:
        copy.wait()


def update_call(total, sums, time_grad, states, row_results):
    flat = [total, sums, time_grad] + [array for state in states for array in state]
    like = lambda array: jax.ShapeDtypeStruct(array.shape, array.dtype)
    rows = states[0][0].shape[2]
    shapes = [like(array) for array in list(row_results) + flat[3:]]
    shapes[4:5] = [
        jax.ShapeDtypeStruct((LAYERS, rows, 2, 256), F32),
        jax.ShapeDtypeStruct((LAYERS, rows, 256), F32),
    ]
    vmem = pl.BlockSpec(memory_space=pltpu.VMEM)
    hbm = pl.BlockSpec(memory_space=pl.ANY)
    return pl.pallas_call(
        update_kernel,
        name="update",
        in_specs=[hbm] * 26,
        out_shape=shapes,
        out_specs=[hbm] * 2 + [vmem] * 22,
        scratch_shapes=[pltpu.VMEM(array.shape, F32) for array in flat]
        + [pltpu.VMEM((8, 128), F32), pltpu.SemaphoreType.DMA((26,))],
        compiler_params=pltpu.CompilerParams(vmem_limit_bytes=56 << 20),
    )(*flat, *row_results)


def per_device(
    rep,
    inputs, cotangent, timesteps, item_scale,
    qkv_weight, qkv_first, qkv_second,
    out_weight, out_first, out_second,
    up_weight, up_first, up_second,
    up_bias, bias_first, bias_second,
    down_weight, down_first, down_second,
    norm_params, norm_first, norm_second,
    time_weight, time_first, time_second,
):
    rows = inputs.shape[0]
    dp, t = lax.axis_index("dp"), lax.axis_index("tensor")
    qkv, out, up, down, bias = qkv_weight, out_weight, up_weight, down_weight, up_bias
    norm, time = norm_params, time_weight
    teams = None
    if rep > 1:
        size = GROUPS * rep
        teams = [[g * rep + j for j in range(rep)] for g in range(GROUPS)]
        pairs = [[g * rep * 2 + j for j in range(rep * 2)] for g in range(GROUPS)]
        join = lambda v, axis: lax.all_gather(v, "dp", axis=axis, axis_index_groups=teams, tiled=True)
        join_both = lambda v, axis: lax.all_gather(
            v, ("dp", "tensor"), axis=axis, axis_index_groups=pairs, tiled=True
        )
        qkv, out, up, down, bias = join(qkv, 1), join(out, 2), join(up, 1), join(down, 2), join(bias, 2)
        norm, time = join_both(norm, 2), join_both(time, 1)
        norm = lax.dynamic_slice_in_dim(norm, t * 16, 16, 2)
        time = lax.dynamic_slice_in_dim(time, t * 16, 16, 1)

    slots = lambda *arrays: [jnp.transpose(v, (0, 2, 1, 3)) for v in arrays]
    flip = lambda *arrays: [jnp.swapaxes(v, 1, 2) for v in arrays]
    front = lambda *arrays: [jnp.swapaxes(v, 0, 1) for v in arrays]
    w, small, feats, entry, middle, qkv_rows, probs, attn, hidden, slope, activations = forward_call(
        rep, rows, timesteps, inputs, *slots(qkv), *flip(out), up, *flip(down), time, *front(norm), bias
    )
    input_grad, total, sums, time_grad = backward_call(
        rep, rows, item_scale, small, feats, cotangent, w, entry, middle, qkv_rows, probs, attn, hidden, slope
    )

    if rep > 1:
        total = lax.psum_scatter(total, "dp", scatter_dimension=2, axis_index_groups=teams, tiled=True)
        sums, time_grad = lax.psum((sums, time_grad), "dp", axis_index_groups=teams)
        time_grad = lax.all_gather(time_grad, "tensor", axis=1, tiled=True)
        width = time_weight.shape[1]
        time_grad = lax.dynamic_slice_in_dim(time_grad, ((dp % rep) * 2 + t) * width, width, 1)

    activations, input_grad, *new = update_call(
        total, sums, time_grad,
        [
            slots(qkv_weight, qkv_first, qkv_second),
            flip(out_weight, out_first, out_second),
            [up_weight, up_first, up_second],
            [up_bias, bias_first, bias_second],
            flip(down_weight, down_first, down_second),
            front(norm_params, norm_first, norm_second),
            [time_weight, time_first, time_second],
        ],
        (activations, input_grad),
    )
    return (
        activations, input_grad,
        *slots(*new[0:2]), new[2], new[3],
        *flip(*new[4:7]), *new[7:10], *new[10:13], *flip(*new[13:16]), *front(*new[16:19]), *new[19:22],
    )


def solution(mesh):
    rep = mesh.shape["dp"] // GROUPS
    shard = P(None, "dp", None, "tensor")
    rows = P(("dp", "tensor"), None)
    trans = P(None, "tensor", "dp")
    flat = P(None, "dp", "tensor")
    norm = P(None, None, ("dp", "tensor"))
    time = P(None, ("dp", "tensor"), None)
    return jax.shard_map(
        functools.partial(per_device, rep),
        mesh=mesh,
        in_specs=(rows, rows, P("dp"), P("dp")) + (shard,) * 3 + (trans,) * 3 + (flat,) * 3 + (trans,) * 6 + (norm,) * 3 + (time,) * 3,
        out_specs=(rows, rows, shard, shard, shard, flat) + (trans,) * 3 + (flat,) * 3 + (trans,) * 6 + (norm,) * 3 + (time,) * 3,
        check_vma=False,
    )
```

```python
import functools
import math

import jax
import jax.numpy as jnp
from jax import lax
from jax.experimental import pallas as pl
from jax.experimental.pallas import tpu as pltpu
from jax.sharding import PartitionSpec as P

HEAD_DIM = 64
LENGTH = 256
LAYERS = 2
STEP = 8
GROUPS = 16
MESH = pl.DeviceIdType.MESH
F32 = jnp.float32
BF16 = jnp.bfloat16

beta_first = 0.5
beta_second = 0.5
learn_rate = 0.1
norm_rate = 0.4
weight_decay = 0.01
adam_eps = 1e-08
norm_eps = 1e-05


def nn(a, b):
    return lax.dot_general(a, b, (((1,), (0,)), ((), ())), preferred_element_type=F32)


def nt(a, b):
    return lax.dot_general(a, b, (((1,), (1,)), ((), ())), preferred_element_type=F32)


def tn(a, b):
    return lax.dot_general(a, b, (((0,), (0,)), ((), ())), preferred_element_type=F32)


def normalize(values):
    center = values - jnp.mean(values, -1, keepdims=True)
    inverse = lax.rsqrt(jnp.mean(center * center, -1, keepdims=True) + norm_eps)
    return center * inverse, inverse


def fold_rows(values):
    rows, cols = values.shape
    return jnp.sum(values.reshape(rows // 8, 8, cols), 0)


def gelu_and_slope(x):
    below = 0.5 + 0.5 * lax.erf(x * math.sqrt(0.5))
    return x * below, below + x * (jnp.exp(x * x * -0.5) * (1.0 / math.sqrt(2.0 * math.pi)))


class Place:
    def __init__(self, rep):
        dp = lax.axis_index("dp")
        self.rep = rep
        self.copy = dp % rep
        self.group = dp // rep
        self.t = lax.axis_index("tensor")
        self.z = self.group // 4
        self.yx = self.group % 4
        x, y = self.yx % 2, self.yx // 2
        self.yx_x = self.yx + 1 - 2 * x
        self.yx_y = self.yx + 2 - 4 * y
        self.yx_d = 3 - self.yx
        self.cols = pl.ds(pl.multiple_of(self.t * 256, 256), 256)
        self.other_cols = pl.ds(pl.multiple_of((1 - self.t) * 256, 256), 256)

    def device(self, z, yx, t):
        return ((z * 4 + yx) * self.rep + self.copy, t)

    def z_ahead(self, k):
        return (self.z + k) % 4

    @property
    def partners(self):
        return [self.device(self.z_ahead(k), self.yx, self.t) for k in (1, 2, 3)] + [
            self.device(self.z, self.yx_x, self.t),
            self.device(self.z, self.yx_y, self.t),
            self.device(self.z, self.yx, 1 - self.t),
        ]

    def greet(self):
        barrier = pltpu.get_barrier_semaphore()
        for partner in self.partners:
            pl.semaphore_signal(barrier, inc=1, device_id=partner, device_id_type=MESH)
        pl.semaphore_wait(barrier, len(self.partners))


class Exchange:
    def start(self, slot):
        self.copy(slot).start()

    def arrived(self, *slots):
        for slot in slots:
            self.copy(slot).wait_recv()

    def finish(self):
        for slot in range(self.slots):
            self.copy(slot).wait_send()

    def remote(self, slot, src, dst, device):
        return pltpu.make_async_remote_copy(
            src_ref=src, dst_ref=dst, send_sem=self.send.at[slot], recv_sem=self.recv.at[slot],
            device_id=device, device_id_type=MESH,
        )


class Gather(Exchange):
    slots = 8

    def __init__(self, place, view, core_view, send, recv):
        self.place, self.view, self.core_view, self.send, self.recv = place, view, core_view, send, recv

    def copy(self, slot):
        p = self.place
        if slot < 3:
            ref, device = self.view(p.z, p.yx), p.device(p.z_ahead(slot + 1), p.yx, p.t)
        elif slot < 5:
            ref, device = self.view(slice(None), p.yx), p.device(p.z, p.yx_x if slot == 3 else p.yx_y, p.t)
        elif slot == 5:
            ref, device = self.view(pl.ds(0, 2), p.yx_x), p.device(p.z, p.yx_y, p.t)
        elif slot == 6:
            ref, device = self.view(pl.ds(2, 2), p.yx_y), p.device(p.z, p.yx_x, p.t)
        else:
            ref, device = self.core_view(), p.device(p.z, p.yx, 1 - p.t)
        return self.remote(slot, ref, ref, device)

    def step(self, number):
        if number == 0:
            for slot in (0, 1, 2):
                self.start(slot)
        elif number == 1:
            self.arrived(0, 1, 2)
            self.start(3)
            self.start(4)
        elif number == 2:
            self.arrived(3)
            self.start(5)
            self.arrived(4)
            self.start(6)
        elif number == 3:
            self.arrived(5, 6)
            self.start(7)
        elif number == 4:
            self.arrived(7)


def play(events):
    for piece, number in events:
        piece.step(number)


class Timeline:
    def __init__(self):
        self.now = 0.0
        self.queue = []
        self.links = 0.0
        self.along = 0.0
        self.count = 0

    def push(self, piece, dues):
        for number, due in enumerate(dues, 1):
            turn = self.count + (number - 1) * LAG
            self.queue.append((turn, number if FIRST else -number, due, number, piece))
        self.queue.sort(key=lambda event: event[:2])
        self.count += 1

    def gather(self, piece, unit):
        self.along += 4 * unit
        arrived = self.along + WAIT
        begun = max(self.links, arrived)
        self.links = begun + 6 * unit
        columns, diagonal = begun + 4 * unit + WAIT, begun + 8 * unit + WAIT
        self.push(piece, [max(arrived, begun - LEAD), columns, diagonal, diagonal + 1.6 * unit + WAIT])

    def scatter(self, piece, unit):
        added = self.now + 1.6 * unit + WAIT
        begun = max(self.links, added)
        self.links = begun + 6 * unit
        summed = begun + 8 * unit + WAIT
        self.along = max(self.along, summed) + 4 * unit
        self.push(piece, [max(added, begun - LEAD), begun + 4 * unit + WAIT, summed, self.along + WAIT])

    def small(self, piece):
        self.push(piece, [self.now + 3.0 * number for number in (1, 2, 3, 4)])

    def take(self, count):
        ready, self.queue = self.queue[:count], self.queue[count:]
        return [(piece, number) for _, _, _, number, piece in ready]

    def slot(self, length):
        count = 0
        while count < len(self.queue) and self.queue[count][2] <= self.now:
            count += 1
        self.now += length + COST * count
        return self.take(count)

    def passed(self, length):
        self.now += length

    def force(self, *wanted):
        count = max([i + 1 for i, event in enumerate(self.queue) if (event[4], event[3]) in wanted], default=0)
        self.now = max([self.now] + [event[2] for event in self.queue[:count]])
        return self.take(count)


WAIT = 5.0
LEAD = 2.0
LAG = 2
FIRST = True
COST = 0.2
UNIT = 0.33


def each_item(body, slots, count, in_specs, out_specs, refs):
    def whole(*blocks):
        item = pl.program_id(0)

        def poll(half):
            for number, events in enumerate(slots):
                if events[half]:
                    pl.when(item == number)(functools.partial(play, events[half]))

        poll(0)
        body(item, lambda: poll(1), *blocks)

    pltpu.emit_pipeline(whole, grid=(count,), in_specs=in_specs, out_specs=out_specs)(*refs)


GATHER_PIECES = 16


def weight(ref, group):
    return jnp.concatenate([ref[group, 0].reshape(512, 256), ref[group, 1].reshape(512, 256)], 1)


def forward_kernel(
    rep,
    steps_ref, x_ref, qkv_ref, out_ref, up_ref, down_ref, time_ref, norm_ref, bias_ref,
    w_out, small_out, feats_out, entry_out, middle_out, qkv_out, probs_out, attn_out, hidden_out, slope_out, act_out,
    w, tw, nb, norms, bias, shifts, stream, attn, rounded, tile, send, recv, keep_sem, act_sem,
):
    place = Place(rep)
    z, yx, t = place.z, place.yx, place.t
    rows = stream.shape[0]
    items = rows // LENGTH

    pieces = []

    def piece(ref, *lead):
        number = len(pieces)
        pieces.append(
            Gather(
                place,
                lambda a, b: ref.at[(*lead, t, a, b)],
                lambda: ref.at[(*lead, t)],
                send.at[number],
                recv.at[number],
            )
        )
        return pieces[-1]

    norm_piece, bias_piece = piece(nb, 0), piece(nb, 1)
    time_pieces = [piece(tw, layer) for layer in range(LAYERS)]
    spans = ((0, 3), (3, 1), (4, 2), (6, 2), (8, 2), (10, 2))
    layer_pieces = [[piece(w, layer, pl.ds(*span)) for span in spans] for layer in range(LAYERS)]

    tile[...] = jnp.zeros(tile.shape, F32)
    for layer in range(LAYERS):
        for row in range(5):
            at = layer * 5 + row
            tile[0, at : at + 1, 0:16] = norm_ref[row, layer : layer + 1]
        tile[1, layer * 8 : (layer + 1) * 8, 0:8] = bias_ref[layer]
    nb[0, t, z, yx] = pltpu.roll(tile[0], (yx * 2 + t) * 16, 1)
    nb[1, t, z, yx] = pltpu.roll(tile[1], place.group * 8, 1)

    def own_attention(layer):
        tw[layer, t, z, yx] = time_ref[layer].astype(BF16)
        for slot in range(3):
            w[layer, slot, t, z, yx] = qkv_ref[layer, slot].astype(BF16)

    def own_feed(layer):
        w[layer, 3, t, z, yx] = out_ref[layer].astype(BF16)
        for part in range(4):
            own = slice(part * 256, (part + 1) * 256)
            w[layer, 4 + 2 * part, t, z, yx] = up_ref[layer, :, own].astype(BF16)
            w[layer, 5 + 2 * part, t, z, yx] = down_ref[layer, :, own].astype(BF16)

    own_attention(0)
    place.greet()
    opening = [norm_piece, time_pieces[0], layer_pieces[0][0]]
    rest = [layer_pieces[0][1], bias_piece] + layer_pieces[0][2:] + [time_pieces[1]] + layer_pieces[1]
    for entry in opening:
        entry.step(0)
    own_feed(0)
    own_attention(1)
    own_feed(1)
    for entry in rest:
        entry.step(0)
    for number in (1, 2, 3):
        for entry in opening:
            entry.step(number)

    times = Timeline()
    times.along, times.links = 6.0, 1.0
    for entry in rest:
        count = 0.25 if entry is bias_piece else 2 if entry is time_pieces[1] else None
        if count is None:
            count = [span[1] for layer in layer_pieces for one, span in zip(layer, spans) if one is entry][0]
        times.gather(entry, UNIT * count)
    times.now = 4.0

    line = lax.broadcasted_iota(jnp.int32, (8, 256), 0)
    column = lax.broadcasted_iota(jnp.int32, (8, 256), 1).astype(F32)
    angles = jnp.zeros((8, 256), F32)
    for item in range(items):
        angles = jnp.where(line == item, steps_ref[t * items + item].astype(F32), angles)
    angles = angles * jnp.exp(column * (-math.log(10000.0) / 256))
    live = line < items
    feats = jnp.concatenate(
        [jnp.where(live, jnp.sin(angles), 0.0), jnp.where(live, jnp.cos(angles), 0.0)], 1
    )
    feats_out[...] = feats
    feats_high = feats.astype(BF16)
    feats_low = (feats - feats_high.astype(F32)).astype(BF16)

    for entry in opening:
        entry.step(4)
    for zz in range(4):
        total = jnp.zeros((16, 128), F32)
        for part in range(8):
            total = total + nb[0, part % 2, zz, part // 2]
        norms[:, zz * 128 : (zz + 1) * 128] = total
    small_out[...] = norms[...]

    def spread_times(layer):
        table = [tw[layer, core].reshape(GROUPS, 16, 512) for core in range(2)]
        table = jnp.concatenate([table[0][:, None], table[1][:, None]], 1).reshape(512, 512)
        shifts[layer * 8 : (layer + 1) * 8] = nn(feats_high, table) + nn(feats_low, table)

    def spread_bias():
        for core in range(2):
            total = jnp.zeros((16, 128), F32)
            for part in range(16):
                total = total + nb[1, core, part // 4, part % 4]
            total = total.astype(BF16).astype(F32)
            for layer in range(LAYERS):
                for part in range(4):
                    for half in range(2):
                        row = layer * 8 + part * 2 + half
                        col = core * 256 + half * 128
                        bias[layer, part, 0:1, col : col + 128] = total[row : row + 1]

    lane = lax.broadcasted_iota(jnp.int32, (1, 128), 1)
    even_mask = jnp.where(lane < HEAD_DIM, 1.0, 0.0).astype(BF16)
    odd_mask = jnp.where(lane < HEAD_DIM, 0.0, 1.0).astype(BF16)
    wide = lambda cols: pl.BlockSpec((LENGTH, cols), lambda i: (i, 0))

    def attention_phase(layer):
        def body(item, poll, *refs):
            if layer == 0:
                x_blk, *refs = refs
            entry_blk, qkv_blk, probs_blk, attn_blk = refs
            here = pl.ds(pl.multiple_of(item * LENGTH, LENGTH), LENGTH)
            start = x_blk[...].astype(F32) if layer == 0 else stream[here]
            entry = start + shifts[pl.ds(layer * 8 + item, 1)]
            entry_blk[...] = entry
            stream[here] = entry
            hat, _ = normalize(entry)
            normed = (hat * norms[layer * 5 : layer * 5 + 1] + norms[layer * 5 + 1 : layer * 5 + 2]).astype(BF16)
            for slot in range(3):
                projected = nn(normed, weight(w.at[layer], slot)).astype(BF16)
                if slot == 0:
                    projected = projected * jnp.asarray(HEAD_DIM**-0.5, BF16)
                qkv_blk[:, slot * 512 : (slot + 1) * 512] = projected

            def scores(pair):
                query = qkv_blk[:, pair * 128 : (pair + 1) * 128]
                key = qkv_blk[:, 512 + pair * 128 : 512 + (pair + 1) * 128]
                return [nt(query * mask, key) for mask in (even_mask, odd_mask)]

            ahead = scores(0)
            for pair in range(4):
                both = ahead
                if pair < 3:
                    ahead = scores(pair + 1)
                span = slice(pair * 128, (pair + 1) * 128)
                value = qkv_blk[:, 1024 + pair * 128 : 1024 + (pair + 1) * 128]
                probs = []
                for side in range(2):
                    raised = jnp.exp(both[side] - jnp.max(both[side], -1, keepdims=True))
                    probs.append((raised * (1.0 / jnp.sum(raised, -1, keepdims=True))).astype(BF16))
                    probs_blk[0, pair * 2 + side] = probs[side]
                values = jnp.concatenate([value * even_mask, value * odd_mask], 0)
                joined = nn(jnp.concatenate(probs, 1), values).astype(BF16)
                attn_blk[:, span] = joined
                attn[here, span] = joined

        each_item(
            body, [(times.slot(ATTENTION), []) for _ in range(items)], items,
            [wide(512)] if layer == 0 else [],
            [wide(512), wide(1536), pl.BlockSpec((1, 8, 256, 256), lambda i: (i, 0, 0, 0)), wide(512)],
            ([x_ref] if layer == 0 else [])
            + [entry_out.at[layer], qkv_out.at[layer], probs_out.at[layer], attn_out.at[layer]],
        )

    def middle_phase(layer):
        def body(item, poll, middle_blk):
            here = pl.ds(pl.multiple_of(item * LENGTH, LENGTH), LENGTH)
            middle = stream[here] + nt(attn[here], weight(w.at[layer], 3))
            middle_blk[...] = middle
            hat, _ = normalize(middle)
            normed = hat * norms[layer * 5 + 2 : layer * 5 + 3] + norms[layer * 5 + 3 : layer * 5 + 4]
            rounded[here] = normed.astype(BF16)
            stream[here] = middle + norms[layer * 5 + 4 : layer * 5 + 5]

        slots = [(times.slot(MIDDLE), []) for _ in range(items)]
        each_item(body, slots, items, [], [wide(512)], [middle_out.at[layer]])

    def feed_phase(layer, keep):
        def body(part, poll, hidden_blk, slope_blk):
            blocks = [slice(i * LENGTH, (i + 1) * LENGTH) for i in range(items)]
            up, down, shift = weight(w.at[layer], 4 + 2 * part), weight(w.at[layer], 5 + 2 * part), bias[layer, part]
            lift = lambda i: nn(rounded[blocks[i]], up) + shift[0:1]

            def lower(i, hidden):
                stream[blocks[i]] += nt(hidden, down)

            ahead, held = lift(0), None
            for i in range(items):
                pre = ahead
                if i + 1 < items:
                    ahead = lift(i + 1)
                hidden, slope = gelu_and_slope(pre)
                if held is not None:
                    lower(i - 1, held)
                held = hidden.astype(BF16)
                hidden_blk[blocks[i]] = held
                slope_blk[blocks[i]] = slope.astype(BF16)
            lower(items - 1, held)

        slots = []
        for part in range(4):
            entry = layer_pieces[layer][2 + part]
            slots.append((times.force((entry, 4)) + [(Start(keep[2 + part]), 0)], []))
            times.passed(FEED)
        tall = pl.BlockSpec((rows, 512), lambda i: (0, i))
        each_item(body, slots, 4, [], [tall, tall], [hidden_out.at[layer], slope_out.at[layer]])

    spread_times(0)
    keeps = []
    for layer in range(LAYERS):
        keep = [
            pltpu.make_async_copy(w.at[layer, pl.ds(*span)], w_out.at[layer, pl.ds(*span)], keep_sem.at[layer, i])
            for i, span in enumerate(spans)
        ]
        keeps += keep
        if layer > 0:
            play(times.force((time_pieces[layer], 4), (layer_pieces[layer][0], 4)))
            spread_times(layer)
        keep[0].start()
        attention_phase(layer)
        play(times.force((layer_pieces[layer][1], 4), (bias_piece, 4)))
        keep[1].start()
        if layer == 0:
            spread_bias()
        middle_phase(layer)
        feed_phase(layer, keep)

    def finish_rows(item, carry):
        here = pl.ds(pl.multiple_of(item * LENGTH, LENGTH), LENGTH)
        rounded[here] = stream[here].astype(BF16)
        return carry

    lax.fori_loop(0, items, finish_rows, 0)
    last = pltpu.make_async_copy(rounded, act_out, act_sem)
    last.start()
    for entry in pieces:
        entry.finish()
    for copy in keeps + [last]:
        copy.wait()


ATTENTION, MIDDLE, FEED = 2.2, 0.8, 2.4
FEED_BACK, ATTENTION_BACK, GRAD = 2.1, 2.7, 0.76


class Start:
    def __init__(self, copy):
        self.copy = copy

    def step(self, number):
        self.copy.start()


def forward_call(rep, rows, steps, x, qkv, out, up, down, time, norm, bias):
    items = rows // LENGTH
    hbm = pl.BlockSpec(memory_space=pl.ANY)
    vmem = pl.BlockSpec(memory_space=pltpu.VMEM)
    smem = pl.BlockSpec(memory_space=pltpu.SMEM)
    shape = jax.ShapeDtypeStruct
    return pl.pallas_call(
        functools.partial(forward_kernel, rep),
        name="forward",
        in_specs=[smem, hbm] + [vmem] * 7,
        out_shape=[
            shape((LAYERS, 12, 2, 4, 4, 32, 256), BF16),
            shape((16, 512), F32),
            shape((8, 512), F32),
            shape((LAYERS, rows, 512), F32),
            shape((LAYERS, rows, 512), F32),
            shape((LAYERS, rows, 1536), BF16),
            shape((LAYERS, items, 8, 256, 256), BF16),
            shape((LAYERS, rows, 512), BF16),
            shape((LAYERS, rows, 2048), BF16),
            shape((LAYERS, rows, 2048), BF16),
            shape((rows, 512), BF16),
        ],
        out_specs=[hbm, vmem, vmem] + [hbm] * 8,
        scratch_shapes=[
            pltpu.VMEM((LAYERS, 12, 2, 4, 4, 32, 256), BF16),
            pltpu.VMEM((LAYERS, 2, 4, 4, 16, 512), BF16),
            pltpu.VMEM((2, 2, 4, 4, 16, 128), F32),
            pltpu.VMEM((16, 512), F32),
            pltpu.VMEM((LAYERS, 4, 8, 512), F32),
            pltpu.VMEM((16, 512), F32),
            pltpu.VMEM((rows, 512), F32),
            pltpu.VMEM((rows, 512), BF16),
            pltpu.VMEM((rows, 512), BF16),
            pltpu.VMEM((2, 16, 128), F32),
            pltpu.SemaphoreType.DMA((GATHER_PIECES, 8)),
            pltpu.SemaphoreType.DMA((GATHER_PIECES, 8)),
            pltpu.SemaphoreType.DMA((LAYERS, 6)),
            pltpu.SemaphoreType.DMA,
        ],
        compiler_params=pltpu.CompilerParams(collective_id=1, has_side_effects=True, vmem_limit_bytes=56 << 20),
    )(steps, x, qkv, out, up, down, time, norm, bias)


class Scatter(Exchange):
    slots = 10

    def __init__(self, place, grads, received, total, groups, send, recv):
        self.place, self.grads, self.received, self.total = place, grads, received, total
        self.first, self.count = groups
        self.span = pl.ds(*groups)
        self.send, self.recv = send, recv

    def copy(self, slot):
        p, span = self.place, self.span
        core, diag_y, diag_x, col_x, col_y, along = self.received
        low, high = pl.ds(0, 2), pl.ds(2, 2)
        to_x, to_y = p.device(p.z, p.yx_x, p.t), p.device(p.z, p.yx_y, p.t)
        if slot == 0:
            src, dst, device = self.grads.at[span, 1 - p.t], core.at[span], p.device(p.z, p.yx, 1 - p.t)
        elif slot == 1:
            src, dst, device = self.grads.at[span, p.t, low, p.yx_d], diag_y.at[span], to_y
        elif slot == 2:
            src, dst, device = self.grads.at[span, p.t, high, p.yx_d], diag_x.at[span], to_x
        elif slot == 3:
            src, dst, device = self.grads.at[span, p.t, low, p.yx_x], col_x.at[span, low], to_x
        elif slot == 4:
            src, dst, device = self.grads.at[span, p.t, high, p.yx_y], col_y.at[span, high], to_y
        elif slot == 5:
            src, dst, device = self.grads.at[span, p.t, high, p.yx_x], col_x.at[span, high], to_x
        elif slot == 6:
            src, dst, device = self.grads.at[span, p.t, low, p.yx_y], col_y.at[span, low], to_y
        else:
            there = p.z_ahead(slot - 6)
            src, dst, device = self.grads.at[span, p.t, there, p.yx], along.at[slot - 7, span], p.device(there, p.yx, p.t)
        return self.remote(slot, src, dst, device)

    def add(self, where, terms):
        def one(group, carry):
            ref = self.grads.at[(group, self.place.t) + where]
            value = ref[...].astype(F32)
            for term in terms:
                value = value + term[group].astype(F32)
            ref[...] = value.astype(BF16)
            return carry

        lax.fori_loop(self.first, self.first + self.count, one, 0)

    def step(self, number):
        p = self.place
        core, diag_y, diag_x, col_x, col_y, along = self.received
        every = slice(None)
        if number == 0:
            self.start(0)
        elif number == 1:
            self.arrived(0)
            self.add((every, every), [core])
            for slot in (1, 2, 5, 6):
                self.start(slot)
        elif number == 2:
            self.arrived(1)
            self.add((pl.ds(0, 2), p.yx_x), [diag_y])
            self.start(3)
            self.arrived(2)
            self.add((pl.ds(2, 2), p.yx_y), [diag_x])
            self.start(4)
        elif number == 3:
            self.arrived(3, 4, 5, 6)
            self.add((every, p.yx), [col_x, col_y])
            for slot in (7, 8, 9):
                self.start(slot)
        elif number == 4:
            self.arrived(7, 8, 9)

            def one(group, carry):
                value = self.grads[group, p.t, p.z, p.yx].astype(F32)
                for k in range(3):
                    value = value + along[k, group].astype(F32)
                self.total[group] = value
                return carry

            lax.fori_loop(self.first, self.first + self.count, one, 0)


class SmallSum(Exchange):
    slots = 6

    def __init__(self, place, sums, received, total, send, recv):
        self.place, self.sums, self.received, self.total = place, sums, received, total
        self.send, self.recv = send, recv

    def copy(self, slot):
        p = self.place
        if slot == 0:
            device = p.device(p.z, p.yx, 1 - p.t)
        elif slot < 3:
            device = p.device(p.z, p.yx_x if slot == 1 else p.yx_y, p.t)
        else:
            device = p.device(p.z_ahead(slot - 2), p.yx, p.t)
        return self.remote(slot, self.sums.at[min(slot, 3)], self.received.at[slot], device)

    def step(self, number):
        if number > 0:
            slots = (3, 4, 5) if number == 4 else (number - 1,)
            value = self.sums[number - 1]
            self.arrived(*slots)
            for slot in slots:
                value = value + self.received[slot]
            if number < 4:
                self.sums[number] = value
            else:
                self.total[...] = value
        if number < 3:
            self.start(number)
        elif number == 3:
            for slot in (3, 4, 5):
                self.start(slot)


GRAD_GROUPS = 13
SCATTER_PIECES = ((4, 2), (6, 2), (8, 2), (10, 2), (3, 1), (0, 1), (1, 1), (2, 1), (12, 1))


def backward_kernel(
    rep,
    scale_ref, small_ref, feats_ref, cot_ref, w_in, entry_in, middle_in, qkv_in, probs_in, attn_in, hidden_in, slope_in,
    grad_out, total_out, sums_out, time_out,
    w, gx, dattn, du, hidden, attn, n1t, n2t, gdt, got, dqkv, grads, item_grad, acc, acc_bias,
    r_core, r_dy, r_dx, r_x, r_y, r_z, sums, r_sums, r_time,
    w_sem, in_sem, send, recv, small_send, small_recv, time_send, time_recv,
):
    place = Place(rep)
    t = place.t
    rows = gx.shape[0]
    items = rows // LENGTH
    wide = lambda cols: pl.BlockSpec((LENGTH, cols), lambda i: (i, 0))
    lane = lax.broadcasted_iota(jnp.int32, (1, 128), 1)
    even_mask = jnp.where(lane < HEAD_DIM, 1.0, 0.0).astype(BF16)
    odd_mask = jnp.where(lane < HEAD_DIM, 0.0, 1.0).astype(BF16)
    times = Timeline()

    def load_weights(layer):
        copies = []
        for number, (first, count) in enumerate(((3, 9), (0, 3))):
            copy = pltpu.make_async_copy(
                w_in.at[layer, pl.ds(first, count)], w.at[pl.ds(first, count)], w_sem.at[layer, number]
            )
            copies.append(copy)
        return copies

    def load_stash(layer):
        return [
            pltpu.make_async_copy(hidden_in.at[layer], hidden, in_sem.at[layer, 0]),
            pltpu.make_async_copy(attn_in.at[layer], attn, in_sem.at[layer, 1]),
        ]

    def norm_back(hat, inverse, dy, layer, row, here):
        acc[row] += fold_rows(dy * hat)
        acc[row + 1] += fold_rows(dy)
        scaled = dy * small_ref[layer * 5 + row : layer * 5 + row + 1]
        mean = jnp.mean(scaled, -1, keepdims=True)
        along = jnp.mean(scaled * hat, -1, keepdims=True)
        return inverse * (scaled - mean - hat * along)

    def feed_phase(layer):
        last = layer == LAYERS - 1

        def body(item, poll, middle_blk, slope_blk, *rest):
            here = pl.ds(pl.multiple_of(item * LENGTH, LENGTH), LENGTH)
            if last:
                grad = rest[0][...].astype(F32) * scale_ref[t * items + item]
            else:
                grad = gx[here]
            acc[4] += fold_rows(grad)
            low = grad.astype(BF16)
            gdt[:, here] = low.T
            back = jnp.zeros((LENGTH, 512), F32)
            for part in range(4):
                span = slice(part * 512, (part + 1) * 512)
                dh = nn(low, weight(w, 5 + 2 * part))
                pre_grad = (dh * slope_blk[:, span].astype(F32)).astype(BF16)
                du[here, span] = pre_grad
                acc_bias[part] += fold_rows(pre_grad.astype(F32))
                back = back + nt(pre_grad, weight(w, 4 + 2 * part))
            hat, inverse = normalize(middle_blk[...])
            normed = hat * small_ref[layer * 5 + 2 : layer * 5 + 3] + small_ref[layer * 5 + 3 : layer * 5 + 4]
            n2t[:, here] = normed.astype(BF16).T
            grad = grad + norm_back(hat, inverse, back, layer, 2, here)
            gx[here] = grad
            low = grad.astype(BF16)
            got[:, here] = low.T
            dattn[here] = nn(low, weight(w, 3)).astype(BF16)

        each_item(
            body, [(times.slot(FEED_BACK), []) for _ in range(items)], items, [wide(512), wide(2048)] + ([wide(512)] if last else []), [],
            [middle_in.at[layer], slope_in.at[layer]] + ([cot_ref] if last else []),
        )

    def attention_phase(layer):
        def body(item, poll, entry_blk, qkv_blk, probs_blk, *rest):
            here = pl.ds(pl.multiple_of(item * LENGTH, LENGTH), LENGTH)
            def sides(pair):
                query = qkv_blk[:, pair * 128 : (pair + 1) * 128]
                key = qkv_blk[:, 512 + pair * 128 : 512 + (pair + 1) * 128]
                value = qkv_blk[:, 1024 + pair * 128 : 1024 + (pair + 1) * 128]
                back = dattn[here, pair * 128 : (pair + 1) * 128]
                split = lambda v: [v * even_mask, v * odd_mask]
                return split(query), split(key), value, split(back)

            def scores(pair):
                _, _, value, back = sides(pair)
                return [nt(side, value) for side in back]

            def products(pair, dscores):
                query, key, _, back = sides(pair)
                probs = [probs_blk[0, pair * 2 + side] for side in range(2)]
                tall = jnp.concatenate(dscores, 0)
                dq = nn(jnp.concatenate(dscores, 1), jnp.concatenate(key, 0)) * HEAD_DIM**-0.5
                dk = tn(tall, jnp.concatenate(query, 0))
                dv = tn(jnp.concatenate(probs, 0), jnp.concatenate(back, 0))
                for slot, value in enumerate((dq, dk, dv)):
                    dqkv[here, slot * 512 + pair * 128 : slot * 512 + (pair + 1) * 128] = value.astype(BF16)

            ahead, held = scores(0), None
            for pair in range(4):
                both = ahead
                if pair == 2:
                    poll()
                if pair < 3:
                    ahead = scores(pair + 1)
                dscores = []
                for side in range(2):
                    probs = probs_blk[0, pair * 2 + side].astype(F32)
                    mixed = probs * both[side]
                    dscores.append((mixed - probs * jnp.sum(mixed, -1, keepdims=True)).astype(BF16))
                if held is not None:
                    products(pair - 1, held)
                held = dscores
            products(3, held)
            back = jnp.zeros((LENGTH, 512), F32)
            for slot in range(3):
                back = back + nt(dqkv[here, slot * 512 : (slot + 1) * 512], weight(w, slot))
            hat, inverse = normalize(entry_blk[...])
            normed = hat * small_ref[layer * 5 : layer * 5 + 1] + small_ref[layer * 5 + 1 : layer * 5 + 2]
            n1t[:, here] = normed.astype(BF16).T
            grad = gx[here] + norm_back(hat, inverse, back, layer, 0, here)
            item_grad[pl.ds(item, 1)] = jnp.sum(grad, 0, keepdims=True)
            if layer == 0:
                rest[0][...] = grad.astype(BF16)
            else:
                gx[here] = grad

        slots = [(times.slot(ATTENTION_BACK / 2), times.slot(ATTENTION_BACK / 2)) for _ in range(items)]
        each_item(
            body, slots, items,
            [wide(512), wide(1536), pl.BlockSpec((1, 8, 256, 256), lambda i: (i, 0, 0, 0))],
            [wide(512)] if layer == 0 else [],
            [entry_in.at[layer], qkv_in.at[layer], probs_in.at[layer]] + ([grad_out] if layer == 0 else []),
        )

    def keep_grad(group, value):
        for half in range(2):
            grads[group, half] = value[:, half * 256 : (half + 1) * 256].astype(BF16).reshape(4, 4, 32, 256)

    def weight_grad(left, right, group, part):
        keep_grad(group, nn(left[...], right[:, part * 512 : (part + 1) * 512]))

    scatters, smalls = [], []
    for layer in range(LAYERS):
        received = [r.at[layer] for r in (r_core, r_dy, r_dx, r_x, r_y, r_z)]
        scatters.append(
            [
                Scatter(place, grads, received, total_out.at[layer], groups, send.at[layer, i], recv.at[layer, i])
                for i, groups in enumerate(SCATTER_PIECES)
            ]
        )
        smalls.append(
            SmallSum(place, sums.at[layer], r_sums.at[layer], sums_out.at[layer], small_send.at[layer], small_recv.at[layer])
        )

    order = [LAYERS - 1 - i for i in range(LAYERS)]
    weights = {order[0]: load_weights(order[0])}
    stash = {order[0]: load_stash(order[0])}
    for copy in weights[order[0]] + stash[order[0]]:
        copy.start()
    item_grad[...] = jnp.zeros(item_grad.shape, F32)
    place.greet()

    def clear(layer, piece):
        if layer != order[0]:
            before = scatters[order[order.index(layer) - 1]][scatters[layer].index(piece)]
            play(times.force((before, 4)))
            before.finish()

    def begin(piece):
        piece.step(0)
        times.scatter(piece, UNIT * piece.count)

    for turn, layer in enumerate(order):
        feed_pieces, late_pieces = scatters[layer][:5], scatters[layer][5:]
        acc[...] = jnp.zeros(acc.shape, F32)
        acc_bias[...] = jnp.zeros(acc_bias.shape, F32)
        weights[layer][0].wait()
        feed_phase(layer)
        stash[layer][0].wait()
        stash[layer][1].wait()
        weights[layer][1].wait()
        for part, piece in enumerate(feed_pieces):
            clear(layer, piece)
            if part < 4:
                weight_grad(n2t, du, 4 + 2 * part, part)
                weight_grad(gdt, hidden, 5 + 2 * part, part)
            else:
                weight_grad(got, attn, 3, 0)
            times.passed(GRAD * piece.count)
            begin(piece)
            play(times.slot(0.0))
        attention_phase(layer)
        if turn + 1 < LAYERS:
            after = order[turn + 1]
            weights[after] = load_weights(after)
            stash[after] = load_stash(after)
            for copy in weights[after] + stash[after]:
                copy.start()
        for piece in late_pieces:
            clear(layer, piece)
        spread = lax.dot_general(
            feats_ref[...], item_grad[...], (((0,), (0,)), ((), ())),
            precision=lax.Precision.HIGHEST, preferred_element_type=F32,
        )
        keep_grad(12, spread)
        begin(late_pieces[3])
        for row in range(5):
            sums[layer, 0, row : row + 1] = jnp.sum(acc[row], 0, keepdims=True)
        for part in range(4):
            sums[layer, 0, 5 + part : 6 + part] = jnp.sum(acc_bias[part], 0, keepdims=True)
        sums[layer, 0, 9:16] = jnp.zeros((7, 512), F32)
        smalls[layer].step(0)
        times.small(smalls[layer])
        for slot in range(3):
            weight_grad(n1t, dqkv, slot, slot)
            times.passed(GRAD)
            begin(late_pieces[slot])
            play(times.slot(0.0))
    play(times.force(*[(piece, 4) for layer in range(LAYERS) for piece in scatters[layer] + [smalls[layer]]]))

    swaps = []
    for layer in range(LAYERS):
        swap = pltpu.make_async_remote_copy(
            src_ref=total_out.at[layer, 12, pl.ds(pl.multiple_of((1 - t) * 16, 16), 16)],
            dst_ref=r_time.at[layer], send_sem=time_send.at[layer], recv_sem=time_recv.at[layer],
            device_id=place.device(place.z, place.yx, 1 - t), device_id_type=MESH,
        )
        swap.start()
        swaps.append(swap)
    for layer in range(LAYERS):
        swaps[layer].wait()
        time_out[layer, :, place.cols] = total_out[layer, 12, pl.ds(pl.multiple_of(t * 16, 16), 16)]
        time_out[layer, :, place.other_cols] = r_time[layer]
    for piece in scatters[order[-1]]:
        piece.finish()
    for piece in smalls:
        piece.finish()


def backward_call(rep, rows, scale, small, feats, cot, w, entry, middle, qkv, probs, attn, hidden, slope):
    items = rows // LENGTH
    hbm = pl.BlockSpec(memory_space=pl.ANY)
    vmem = pl.BlockSpec(memory_space=pltpu.VMEM)
    smem = pl.BlockSpec(memory_space=pltpu.SMEM)
    shape = jax.ShapeDtypeStruct
    pieces = len(SCATTER_PIECES)
    dma = pltpu.SemaphoreType.DMA
    return pl.pallas_call(
        functools.partial(backward_kernel, rep),
        name="backward",
        in_specs=[smem, vmem, vmem] + [hbm] * 9,
        out_shape=[
            shape((rows, 512), BF16),
            shape((LAYERS, GRAD_GROUPS, 32, 256), F32),
            shape((LAYERS, 16, 512), F32),
            shape((LAYERS, 16, 512), F32),
        ],
        out_specs=[hbm, vmem, vmem, vmem],
        scratch_shapes=[
            pltpu.VMEM((12, 2, 4, 4, 32, 256), BF16),
            pltpu.VMEM((rows, 512), F32),
            pltpu.VMEM((rows, 512), BF16),
            pltpu.VMEM((rows, 2048), BF16),
            pltpu.VMEM((rows, 2048), BF16),
            pltpu.VMEM((rows, 512), BF16),
            pltpu.VMEM((512, rows), BF16),
            pltpu.VMEM((512, rows), BF16),
            pltpu.VMEM((512, rows), BF16),
            pltpu.VMEM((512, rows), BF16),
            pltpu.VMEM((rows, 1536), BF16),
            pltpu.VMEM((GRAD_GROUPS, 2, 4, 4, 32, 256), BF16),
            pltpu.VMEM((8, 512), F32),
            pltpu.VMEM((5, 8, 512), F32),
            pltpu.VMEM((4, 8, 512), F32),
            pltpu.VMEM((LAYERS, GRAD_GROUPS, 4, 4, 32, 256), BF16),
            pltpu.VMEM((LAYERS, GRAD_GROUPS, 2, 32, 256), BF16),
            pltpu.VMEM((LAYERS, GRAD_GROUPS, 2, 32, 256), BF16),
            pltpu.VMEM((LAYERS, GRAD_GROUPS, 4, 32, 256), BF16),
            pltpu.VMEM((LAYERS, GRAD_GROUPS, 4, 32, 256), BF16),
            pltpu.VMEM((LAYERS, 3, GRAD_GROUPS, 32, 256), BF16),
            pltpu.VMEM((LAYERS, 4, 16, 512), F32),
            pltpu.VMEM((LAYERS, 6, 16, 512), F32),
            pltpu.VMEM((LAYERS, 16, 256), F32),
            dma((LAYERS, 2)),
            dma((LAYERS, 2)),
            dma((LAYERS, pieces, 10)),
            dma((LAYERS, pieces, 10)),
            dma((LAYERS, 6)),
            dma((LAYERS, 6)),
            dma((LAYERS,)),
            dma((LAYERS,)),
        ],
        compiler_params=pltpu.CompilerParams(collective_id=2, has_side_effects=True, vmem_limit_bytes=62 << 20),
    )(scale, small, feats, cot, w, entry, middle, qkv, probs, attn, hidden, slope)


def adamw(weight, gradient, first_moment, second_moment, rate):
    first_new = beta_first * first_moment + (1.0 - beta_first) * gradient
    second_new = beta_second * second_moment + (1.0 - beta_second) * gradient * gradient
    first_corr = first_new * (1.0 / (1.0 - beta_first**STEP))
    second_corr = second_new * (1.0 / (1.0 - beta_second**STEP))
    weight_new = weight - rate * (first_corr / (jnp.sqrt(second_corr) + adam_eps) + weight_decay * weight)
    return (weight_new, first_new, second_new)


def update_kernel(*refs):
    hbm, outs, ins = refs[:26], refs[26:50], refs[50:74]
    row, sems = refs[74:]
    copies = [pltpu.make_async_copy(src, dst, sems.at[i]) for i, (src, dst) in enumerate(zip(hbm[:24], ins))]
    copies += [pltpu.make_async_copy(hbm[24 + i], outs[i], sems.at[24 + i]) for i in range(2)]
    for copy in copies:
        copy.start()
    for copy in copies[:24]:
        copy.wait()
    total, sums, time_grad, *ins = ins
    outs = outs[2:]
    qkv, out, up, bias, down, norm, time = [ins[i * 3 : i * 3 + 3] for i in range(7)]
    qkv_new, key_second, value_second = outs[0:2], outs[2], outs[3]
    out_new, up_new, bias_new, down_new, norm_new, time_new = [outs[4 + i * 3 : 7 + i * 3] for i in range(6)]
    dp, t = lax.axis_index("dp"), lax.axis_index("tensor")

    def one(old, new, where, gradient, rate):
        values = adamw(old[0][where], gradient, old[1][where], old[2][where], rate)
        for ref, value in zip(new, values):
            ref[where] = value
        return values

    for layer in range(LAYERS):
        for slot in range(3):
            values = adamw(qkv[0][layer, slot], total[layer, slot], qkv[1][layer, slot], qkv[2][layer, slot], learn_rate)
            for ref, value in zip(qkv_new, values):
                ref[layer, slot] = value
            if slot < 2:
                key_second[layer, :, slot] = values[2]
            else:
                value_second[layer] = values[2]
        one(out, out_new, (layer,), total[layer, 3], learn_rate)
        for part in range(4):
            where = (layer, slice(None), slice(part * 256, (part + 1) * 256))
            one(up, up_new, where, total[layer, 4 + 2 * part], learn_rate)
            one(down, down_new, where, total[layer, 5 + 2 * part], learn_rate)
        one(time, time_new, (layer,), time_grad[layer], learn_rate)

        width = norm[0].shape[2]
        start = (dp * 2 + t) * width
        tile = sums[layer, :, pl.ds(pl.multiple_of(start // 128 * 128, 128), 128)]
        mine = pltpu.roll(tile, (128 - start % 128) % 128, 1)[0:5, 0:width]
        one(norm, norm_new, (slice(None), layer), mine, norm_rate)
        for part in range(4):
            for half in range(2):
                span = pl.ds(pl.multiple_of(t * 256 + half * 128, 128), 128)
                row[part * 2 + half : part * 2 + half + 1] = sums[layer, 5 + part : 6 + part, span]
        width = bias[0].shape[2]
        mine = pltpu.roll(row[...], (128 - dp * width) % 128, 1)[:, 0:width]
        one(bias, bias_new, (layer,), mine, learn_rate)
    for copy in copies[24:]:
        copy.wait()


def update_call(total, sums, time_grad, states, row_results):
    flat = [total, sums, time_grad] + [array for state in states for array in state]
    like = lambda array: jax.ShapeDtypeStruct(array.shape, array.dtype)
    rows = states[0][0].shape[2]
    shapes = [like(array) for array in list(row_results) + flat[3:]]
    shapes[4:5] = [
        jax.ShapeDtypeStruct((LAYERS, rows, 2, 256), F32),
        jax.ShapeDtypeStruct((LAYERS, rows, 256), F32),
    ]
    vmem = pl.BlockSpec(memory_space=pltpu.VMEM)
    hbm = pl.BlockSpec(memory_space=pl.ANY)
    return pl.pallas_call(
        update_kernel,
        name="update",
        in_specs=[hbm] * 26,
        out_shape=shapes,
        out_specs=[vmem] * 24,
        scratch_shapes=[pltpu.VMEM(array.shape, F32) for array in flat]
        + [pltpu.VMEM((8, 128), F32), pltpu.SemaphoreType.DMA((26,))],
        compiler_params=pltpu.CompilerParams(vmem_limit_bytes=56 << 20),
    )(*flat, *row_results)


def per_device(
    rep,
    inputs, cotangent, timesteps, item_scale,
    qkv_weight, qkv_first, qkv_second,
    out_weight, out_first, out_second,
    up_weight, up_first, up_second,
    up_bias, bias_first, bias_second,
    down_weight, down_first, down_second,
    norm_params, norm_first, norm_second,
    time_weight, time_first, time_second,
):
    rows = inputs.shape[0]
    dp, t = lax.axis_index("dp"), lax.axis_index("tensor")
    qkv, out, up, down, bias = qkv_weight, out_weight, up_weight, down_weight, up_bias
    norm, time = norm_params, time_weight
    teams = None
    if rep > 1:
        size = GROUPS * rep
        teams = [[g * rep + j for j in range(rep)] for g in range(GROUPS)]
        pairs = [[g * rep * 2 + j for j in range(rep * 2)] for g in range(GROUPS)]
        join = lambda v, axis: lax.all_gather(v, "dp", axis=axis, axis_index_groups=teams, tiled=True)
        join_both = lambda v, axis: lax.all_gather(
            v, ("dp", "tensor"), axis=axis, axis_index_groups=pairs, tiled=True
        )
        qkv, out, up, down, bias = join(qkv, 1), join(out, 2), join(up, 1), join(down, 2), join(bias, 2)
        norm, time = join_both(norm, 2), join_both(time, 1)
        norm = lax.dynamic_slice_in_dim(norm, t * 16, 16, 2)
        time = lax.dynamic_slice_in_dim(time, t * 16, 16, 1)

    slots = lambda *arrays: [jnp.transpose(v, (0, 2, 1, 3)) for v in arrays]
    flip = lambda *arrays: [jnp.swapaxes(v, 1, 2) for v in arrays]
    front = lambda *arrays: [jnp.swapaxes(v, 0, 1) for v in arrays]
    w, small, feats, entry, middle, qkv_rows, probs, attn, hidden, slope, activations = forward_call(
        rep, rows, timesteps, inputs, *slots(qkv), *flip(out), up, *flip(down), time, *front(norm), bias
    )
    input_grad, total, sums, time_grad = backward_call(
        rep, rows, item_scale, small, feats, cotangent, w, entry, middle, qkv_rows, probs, attn, hidden, slope
    )

    if rep > 1:
        total = lax.psum_scatter(total, "dp", scatter_dimension=2, axis_index_groups=teams, tiled=True)
        sums, time_grad = lax.psum((sums, time_grad), "dp", axis_index_groups=teams)
        time_grad = lax.all_gather(time_grad, "tensor", axis=1, tiled=True)
        width = time_weight.shape[1]
        time_grad = lax.dynamic_slice_in_dim(time_grad, ((dp % rep) * 2 + t) * width, width, 1)

    activations, input_grad, *new = update_call(
        total, sums, time_grad,
        [
            slots(qkv_weight, qkv_first, qkv_second),
            flip(out_weight, out_first, out_second),
            [up_weight, up_first, up_second],
            [up_bias, bias_first, bias_second],
            flip(down_weight, down_first, down_second),
            front(norm_params, norm_first, norm_second),
            [time_weight, time_first, time_second],
        ],
        (activations, input_grad),
    )
    return (
        activations, input_grad,
        *slots(*new[0:2]), new[2], new[3],
        *flip(*new[4:7]), *new[7:10], *new[10:13], *flip(*new[13:16]), *front(*new[16:19]), *new[19:22],
    )


def solution(mesh):
    rep = mesh.shape["dp"] // GROUPS
    shard = P(None, "dp", None, "tensor")
    rows = P(("dp", "tensor"), None)
    trans = P(None, "tensor", "dp")
    flat = P(None, "dp", "tensor")
    norm = P(None, None, ("dp", "tensor"))
    time = P(None, ("dp", "tensor"), None)
    return jax.shard_map(
        functools.partial(per_device, rep),
        mesh=mesh,
        in_specs=(rows, rows, P("dp"), P("dp")) + (shard,) * 3 + (trans,) * 3 + (flat,) * 3 + (trans,) * 6 + (norm,) * 3 + (time,) * 3,
        out_specs=(rows, rows, shard, shard, shard, flat) + (trans,) * 3 + (flat,) * 3 + (trans,) * 6 + (norm,) * 3 + (time,) * 3,
        check_vma=False,
    )
```

```python
import functools
import math

import jax
import jax.numpy as jnp
from jax import lax
from jax.experimental import pallas as pl
from jax.experimental.pallas import tpu as pltpu
from jax.sharding import PartitionSpec as P

HEAD_DIM = 64
LENGTH = 256
LAYERS = 2
STEP = 8
GROUPS = 16
MESH = pl.DeviceIdType.MESH
F32 = jnp.float32
BF16 = jnp.bfloat16

beta_first = 0.5
beta_second = 0.5
learn_rate = 0.1
norm_rate = 0.4
weight_decay = 0.01
adam_eps = 1e-08
norm_eps = 1e-05


def nn(a, b):
    return lax.dot_general(a, b, (((1,), (0,)), ((), ())), preferred_element_type=F32)


def nt(a, b):
    return lax.dot_general(a, b, (((1,), (1,)), ((), ())), preferred_element_type=F32)


def tn(a, b):
    return lax.dot_general(a, b, (((0,), (0,)), ((), ())), preferred_element_type=F32)


def normalize(values):
    center = values - jnp.mean(values, -1, keepdims=True)
    inverse = lax.rsqrt(jnp.mean(center * center, -1, keepdims=True) + norm_eps)
    return center * inverse, inverse


def fold_rows(values):
    rows, cols = values.shape
    return jnp.sum(values.reshape(rows // 8, 8, cols), 0)


def gelu_and_slope(x):
    below = 0.5 + 0.5 * lax.erf(x * math.sqrt(0.5))
    return x * below, below + x * (jnp.exp(x * x * -0.5) * (1.0 / math.sqrt(2.0 * math.pi)))


class Place:
    def __init__(self, rep):
        dp = lax.axis_index("dp")
        self.rep = rep
        self.copy = dp % rep
        self.group = dp // rep
        self.t = lax.axis_index("tensor")
        self.z = self.group // 4
        self.yx = self.group % 4
        x, y = self.yx % 2, self.yx // 2
        self.yx_x = self.yx + 1 - 2 * x
        self.yx_y = self.yx + 2 - 4 * y
        self.yx_d = 3 - self.yx
        self.cols = pl.ds(pl.multiple_of(self.t * 256, 256), 256)
        self.other_cols = pl.ds(pl.multiple_of((1 - self.t) * 256, 256), 256)

    def device(self, z, yx, t):
        return ((z * 4 + yx) * self.rep + self.copy, t)

    def z_ahead(self, k):
        return (self.z + k) % 4

    @property
    def partners(self):
        return [self.device(self.z_ahead(k), self.yx, self.t) for k in (1, 2, 3)] + [
            self.device(self.z, self.yx_x, self.t),
            self.device(self.z, self.yx_y, self.t),
            self.device(self.z, self.yx, 1 - self.t),
        ]

    def greet(self):
        barrier = pltpu.get_barrier_semaphore()
        for partner in self.partners:
            pl.semaphore_signal(barrier, inc=1, device_id=partner, device_id_type=MESH)
        pl.semaphore_wait(barrier, len(self.partners))


class Exchange:
    def start(self, slot):
        self.copy(slot).start()

    def arrived(self, *slots):
        for slot in slots:
            self.copy(slot).wait_recv()

    def finish(self):
        for slot in range(self.slots):
            self.copy(slot).wait_send()

    def remote(self, slot, src, dst, device):
        return pltpu.make_async_remote_copy(
            src_ref=src, dst_ref=dst, send_sem=self.send.at[slot], recv_sem=self.recv.at[slot],
            device_id=device, device_id_type=MESH,
        )


class Gather(Exchange):
    slots = 8

    def __init__(self, place, view, core_view, send, recv):
        self.place, self.view, self.core_view, self.send, self.recv = place, view, core_view, send, recv

    def copy(self, slot):
        p = self.place
        if slot < 3:
            ref, device = self.view(p.z, p.yx), p.device(p.z_ahead(slot + 1), p.yx, p.t)
        elif slot < 5:
            ref, device = self.view(slice(None), p.yx), p.device(p.z, p.yx_x if slot == 3 else p.yx_y, p.t)
        elif slot == 5:
            ref, device = self.view(pl.ds(0, 2), p.yx_x), p.device(p.z, p.yx_y, p.t)
        elif slot == 6:
            ref, device = self.view(pl.ds(2, 2), p.yx_y), p.device(p.z, p.yx_x, p.t)
        else:
            ref, device = self.core_view(), p.device(p.z, p.yx, 1 - p.t)
        return self.remote(slot, ref, ref, device)

    def step(self, number):
        if number == 0:
            for slot in (0, 1, 2):
                self.start(slot)
        elif number == 1:
            self.arrived(0, 1, 2)
            self.start(3)
            self.start(4)
        elif number == 2:
            self.arrived(3)
            self.start(5)
            self.arrived(4)
            self.start(6)
        elif number == 3:
            self.arrived(5, 6)
            self.start(7)
        elif number == 4:
            self.arrived(7)


def play(events):
    for piece, number in events:
        piece.step(number)


class Timeline:
    def __init__(self):
        self.now = 0.0
        self.queue = []
        self.links = 0.0
        self.along = 0.0
        self.count = 0

    def push(self, piece, dues, turns):
        for number, (due, turn) in enumerate(zip(dues, turns), 1):
            self.queue.append((self.count + turn, due, number, piece))
        self.queue.sort(key=lambda event: event[0])
        self.count += 1

    def gather(self, piece, unit):
        self.along += 4 * unit
        arrived = self.along + GATHER_WAIT
        begun = max(self.links, arrived)
        self.links = begun + 6 * unit
        columns, diagonal = begun + 4 * unit + GATHER_WAIT, begun + 6 * unit + GATHER_WAIT
        self.push(piece, [max(arrived, begun - LEAD), columns, diagonal, diagonal + 1.6 * unit + GATHER_WAIT], GATHER_TURNS)

    def scatter(self, piece, unit):
        added = self.now + 1.6 * unit + WAIT
        begun = max(self.links, added)
        self.links = begun + 6 * unit
        summed = begun + 8 * unit + WAIT
        self.along = max(self.along, summed) + 4 * unit
        self.push(piece, [max(added, begun - LEAD), begun + 4 * unit + WAIT, summed, self.along + WAIT], SCATTER_TURNS)

    def small(self, piece):
        self.push(piece, [self.now + 3.0 * number for number in (1, 2, 3, 4)], SCATTER_TURNS)

    def take(self, count):
        ready, self.queue = self.queue[:count], self.queue[count:]
        return [(piece, number) for _, _, number, piece in ready]

    def slot(self, length):
        count = 0
        while count < len(self.queue) and self.queue[count][1] <= self.now:
            count += 1
        self.now += length + COST * count
        return self.take(count)

    def passed(self, length):
        self.now += length

    def force(self, *wanted):
        count = max([i + 1 for i, event in enumerate(self.queue) if (event[3], event[2]) in wanted], default=0)
        self.now = max([self.now] + [event[1] for event in self.queue[:count]])
        return self.take(count)


WAIT = 5.0
GATHER_WAIT = 3.0
LEAD = 2.0
GATHER_TURNS = (-1.9, 0.0, 1.05, 2.3)
SCATTER_TURNS = (0.0, 2.1, 4.2, 6.3)
COST = 0.2
UNIT = 0.33


def each_item(body, slots, count, in_specs, out_specs, refs):
    def whole(*blocks):
        item = pl.program_id(0)

        def poll(half):
            for number, events in enumerate(slots):
                if events[half]:
                    pl.when(item == number)(functools.partial(play, events[half]))

        poll(0)
        body(item, lambda: poll(1), *blocks)

    pltpu.emit_pipeline(whole, grid=(count,), in_specs=in_specs, out_specs=out_specs)(*refs)


GATHER_PIECES = 16


def weight(ref, group):
    return jnp.concatenate([ref[group, 0].reshape(512, 256), ref[group, 1].reshape(512, 256)], 1)


def forward_kernel(
    rep,
    steps_ref, x_ref, qkv_ref, out_ref, up_ref, down_ref, time_ref, norm_ref, bias_ref,
    w_out, small_out, feats_out, entry_out, middle_out, qkv_out, probs_out, attn_out, hidden_out, slope_out, act_out,
    w, tw, nb, norms, bias, shifts, stream, attn, rounded, tile, send, recv, keep_sem, act_sem,
):
    place = Place(rep)
    z, yx, t = place.z, place.yx, place.t
    rows = stream.shape[0]
    items = rows // LENGTH

    pieces = []

    def piece(ref, *lead):
        number = len(pieces)
        pieces.append(
            Gather(
                place,
                lambda a, b: ref.at[(*lead, t, a, b)],
                lambda: ref.at[(*lead, t)],
                send.at[number],
                recv.at[number],
            )
        )
        return pieces[-1]

    norm_piece, bias_piece = piece(nb, 0), piece(nb, 1)
    time_pieces = [piece(tw, layer) for layer in range(LAYERS)]
    spans = ((0, 3), (3, 1), (4, 2), (6, 2), (8, 2), (10, 2))
    layer_pieces = [[piece(w, layer, pl.ds(*span)) for span in spans] for layer in range(LAYERS)]

    tile[...] = jnp.zeros(tile.shape, F32)
    for layer in range(LAYERS):
        for row in range(5):
            at = layer * 5 + row
            tile[0, at : at + 1, 0:16] = norm_ref[row, layer : layer + 1]
        tile[1, layer * 8 : (layer + 1) * 8, 0:8] = bias_ref[layer]
    nb[0, t, z, yx] = pltpu.roll(tile[0], (yx * 2 + t) * 16, 1)
    nb[1, t, z, yx] = pltpu.roll(tile[1], place.group * 8, 1)

    def own_attention(layer):
        tw[layer, t, z, yx] = time_ref[layer].astype(BF16)
        for slot in range(3):
            w[layer, slot, t, z, yx] = qkv_ref[layer, slot].astype(BF16)

    def own_feed(layer):
        w[layer, 3, t, z, yx] = out_ref[layer].astype(BF16)
        for part in range(4):
            own = slice(part * 256, (part + 1) * 256)
            w[layer, 4 + 2 * part, t, z, yx] = up_ref[layer, :, own].astype(BF16)
            w[layer, 5 + 2 * part, t, z, yx] = down_ref[layer, :, own].astype(BF16)

    own_attention(0)
    place.greet()
    opening = [norm_piece, time_pieces[0], layer_pieces[0][0]]
    rest = [layer_pieces[0][1], bias_piece] + layer_pieces[0][2:] + [time_pieces[1]] + layer_pieces[1]
    for entry in opening:
        entry.step(0)
    own_feed(0)
    own_attention(1)
    own_feed(1)
    for entry in rest:
        entry.step(0)
    sizes = {norm_piece: 0.25, bias_piece: 0.25}
    for layer in range(LAYERS):
        sizes[time_pieces[layer]] = 2
        sizes.update((entry, span[1]) for entry, span in zip(layer_pieces[layer], spans))
    times = Timeline()
    for entry in opening + rest:
        times.gather(entry, UNIT * sizes[entry])
    wanted = [(entry, 4) for entry in opening]
    play(times.force(*[(entry, 3) for entry in opening]))

    line = lax.broadcasted_iota(jnp.int32, (8, 256), 0)
    column = lax.broadcasted_iota(jnp.int32, (8, 256), 1).astype(F32)
    angles = jnp.zeros((8, 256), F32)
    for item in range(items):
        angles = jnp.where(line == item, steps_ref[t * items + item].astype(F32), angles)
    angles = angles * jnp.exp(column * (-math.log(10000.0) / 256))
    live = line < items
    feats = jnp.concatenate(
        [jnp.where(live, jnp.sin(angles), 0.0), jnp.where(live, jnp.cos(angles), 0.0)], 1
    )
    feats_out[...] = feats
    feats_high = feats.astype(BF16)
    feats_low = (feats - feats_high.astype(F32)).astype(BF16)

    play(times.force(*wanted))
    for zz in range(4):
        total = jnp.zeros((16, 128), F32)
        for part in range(8):
            total = total + nb[0, part % 2, zz, part // 2]
        norms[:, zz * 128 : (zz + 1) * 128] = total
    small_out[...] = norms[...]

    def spread_times(layer):
        table = [tw[layer, core].reshape(GROUPS, 16, 512) for core in range(2)]
        table = jnp.concatenate([table[0][:, None], table[1][:, None]], 1).reshape(512, 512)
        shifts[layer * 8 : (layer + 1) * 8] = nn(feats_high, table) + nn(feats_low, table)

    def spread_bias():
        for core in range(2):
            total = jnp.zeros((16, 128), F32)
            for part in range(16):
                total = total + nb[1, core, part // 4, part % 4]
            total = total.astype(BF16).astype(F32)
            for layer in range(LAYERS):
                for part in range(4):
                    for half in range(2):
                        row = layer * 8 + part * 2 + half
                        col = core * 256 + half * 128
                        bias[layer, part, 0:1, col : col + 128] = total[row : row + 1]

    lane = lax.broadcasted_iota(jnp.int32, (1, 128), 1)
    even_mask = jnp.where(lane < HEAD_DIM, 1.0, 0.0).astype(BF16)
    odd_mask = jnp.where(lane < HEAD_DIM, 0.0, 1.0).astype(BF16)
    wide = lambda cols: pl.BlockSpec((LENGTH, cols), lambda i: (i, 0))

    def attention_phase(layer):
        def body(item, poll, *refs):
            if layer == 0:
                x_blk, *refs = refs
            entry_blk, qkv_blk, probs_blk, attn_blk = refs
            here = pl.ds(pl.multiple_of(item * LENGTH, LENGTH), LENGTH)
            start = x_blk[...].astype(F32) if layer == 0 else stream[here]
            entry = start + shifts[pl.ds(layer * 8 + item, 1)]
            entry_blk[...] = entry
            stream[here] = entry
            hat, _ = normalize(entry)
            normed = (hat * norms[layer * 5 : layer * 5 + 1] + norms[layer * 5 + 1 : layer * 5 + 2]).astype(BF16)
            for slot in range(3):
                projected = nn(normed, weight(w.at[layer], slot)).astype(BF16)
                if slot == 0:
                    projected = projected * jnp.asarray(HEAD_DIM**-0.5, BF16)
                qkv_blk[:, slot * 512 : (slot + 1) * 512] = projected

            def scores(pair):
                query = qkv_blk[:, pair * 128 : (pair + 1) * 128]
                key = qkv_blk[:, 512 + pair * 128 : 512 + (pair + 1) * 128]
                return [nt(query * mask, key) for mask in (even_mask, odd_mask)]

            ahead = scores(0)
            for pair in range(4):
                both = ahead
                if pair < 3:
                    ahead = scores(pair + 1)
                span = slice(pair * 128, (pair + 1) * 128)
                value = qkv_blk[:, 1024 + pair * 128 : 1024 + (pair + 1) * 128]
                probs = []
                for side in range(2):
                    raised = jnp.exp(both[side] - jnp.max(both[side], -1, keepdims=True))
                    probs.append((raised * (1.0 / jnp.sum(raised, -1, keepdims=True))).astype(BF16))
                    probs_blk[0, pair * 2 + side] = probs[side]
                values = jnp.concatenate([value * even_mask, value * odd_mask], 0)
                joined = nn(jnp.concatenate(probs, 1), values).astype(BF16)
                attn_blk[:, span] = joined
                attn[here, span] = joined

        each_item(
            body, [(times.slot(ATTENTION), []) for _ in range(items)], items,
            [wide(512)] if layer == 0 else [],
            [wide(512), wide(1536), pl.BlockSpec((1, 8, 256, 256), lambda i: (i, 0, 0, 0)), wide(512)],
            ([x_ref] if layer == 0 else [])
            + [entry_out.at[layer], qkv_out.at[layer], probs_out.at[layer], attn_out.at[layer]],
        )

    def middle_phase(layer):
        def body(item, poll, middle_blk):
            here = pl.ds(pl.multiple_of(item * LENGTH, LENGTH), LENGTH)
            middle = stream[here] + nt(attn[here], weight(w.at[layer], 3))
            middle_blk[...] = middle
            hat, _ = normalize(middle)
            normed = hat * norms[layer * 5 + 2 : layer * 5 + 3] + norms[layer * 5 + 3 : layer * 5 + 4]
            rounded[here] = normed.astype(BF16)
            stream[here] = middle + norms[layer * 5 + 4 : layer * 5 + 5]

        slots = [(times.slot(MIDDLE), []) for _ in range(items)]
        each_item(body, slots, items, [], [wide(512)], [middle_out.at[layer]])

    def feed_phase(layer, keep):
        def body(part, poll, hidden_blk, slope_blk):
            blocks = [slice(i * LENGTH, (i + 1) * LENGTH) for i in range(items)]
            up, down, shift = weight(w.at[layer], 4 + 2 * part), weight(w.at[layer], 5 + 2 * part), bias[layer, part]
            lift = lambda i: nn(rounded[blocks[i]], up) + shift[0:1]

            def lower(i, hidden):
                stream[blocks[i]] += nt(hidden, down)

            ahead, held = lift(0), None
            for i in range(items):
                pre = ahead
                if i + 1 < items:
                    ahead = lift(i + 1)
                hidden, slope = gelu_and_slope(pre)
                if held is not None:
                    lower(i - 1, held)
                held = hidden.astype(BF16)
                hidden_blk[blocks[i]] = held
                slope_blk[blocks[i]] = slope.astype(BF16)
            lower(items - 1, held)

        slots = []
        for part in range(4):
            entry = layer_pieces[layer][2 + part]
            slots.append((times.force((entry, 4)) + [(Start(keep[2 + part]), 0)], []))
            times.passed(FEED)
        tall = pl.BlockSpec((rows, 512), lambda i: (0, i))
        each_item(body, slots, 4, [], [tall, tall], [hidden_out.at[layer], slope_out.at[layer]])

    spread_times(0)
    keeps = []
    for layer in range(LAYERS):
        keep = [
            pltpu.make_async_copy(w.at[layer, pl.ds(*span)], w_out.at[layer, pl.ds(*span)], keep_sem.at[layer, i])
            for i, span in enumerate(spans)
        ]
        keeps += keep
        if layer > 0:
            play(times.force((time_pieces[layer], 4), (layer_pieces[layer][0], 4)))
            spread_times(layer)
        keep[0].start()
        attention_phase(layer)
        play(times.force((layer_pieces[layer][1], 4), (bias_piece, 4)))
        keep[1].start()
        if layer == 0:
            spread_bias()
        middle_phase(layer)
        feed_phase(layer, keep)

    def finish_rows(item, carry):
        here = pl.ds(pl.multiple_of(item * LENGTH, LENGTH), LENGTH)
        rounded[here] = stream[here].astype(BF16)
        return carry

    lax.fori_loop(0, items, finish_rows, 0)
    last = pltpu.make_async_copy(rounded, act_out, act_sem)
    last.start()
    for entry in pieces:
        entry.finish()
    for copy in keeps + [last]:
        copy.wait()


ATTENTION, MIDDLE, FEED = 2.2, 0.8, 2.4
FEED_BACK, ATTENTION_BACK, GRAD = 2.1, 2.7, 0.76


class Start:
    def __init__(self, copy):
        self.copy = copy

    def step(self, number):
        self.copy.start()


def forward_call(rep, rows, steps, x, qkv, out, up, down, time, norm, bias):
    items = rows // LENGTH
    hbm = pl.BlockSpec(memory_space=pl.ANY)
    vmem = pl.BlockSpec(memory_space=pltpu.VMEM)
    smem = pl.BlockSpec(memory_space=pltpu.SMEM)
    shape = jax.ShapeDtypeStruct
    return pl.pallas_call(
        functools.partial(forward_kernel, rep),
        name="forward",
        in_specs=[smem, hbm] + [vmem] * 7,
        out_shape=[
            shape((LAYERS, 12, 2, 4, 4, 32, 256), BF16),
            shape((16, 512), F32),
            shape((8, 512), F32),
            shape((LAYERS, rows, 512), F32),
            shape((LAYERS, rows, 512), F32),
            shape((LAYERS, rows, 1536), BF16),
            shape((LAYERS, items, 8, 256, 256), BF16),
            shape((LAYERS, rows, 512), BF16),
            shape((LAYERS, rows, 2048), BF16),
            shape((LAYERS, rows, 2048), BF16),
            shape((rows, 512), BF16),
        ],
        out_specs=[hbm, vmem, vmem] + [hbm] * 8,
        scratch_shapes=[
            pltpu.VMEM((LAYERS, 12, 2, 4, 4, 32, 256), BF16),
            pltpu.VMEM((LAYERS, 2, 4, 4, 16, 512), BF16),
            pltpu.VMEM((2, 2, 4, 4, 16, 128), F32),
            pltpu.VMEM((16, 512), F32),
            pltpu.VMEM((LAYERS, 4, 8, 512), F32),
            pltpu.VMEM((16, 512), F32),
            pltpu.VMEM((rows, 512), F32),
            pltpu.VMEM((rows, 512), BF16),
            pltpu.VMEM((rows, 512), BF16),
            pltpu.VMEM((2, 16, 128), F32),
            pltpu.SemaphoreType.DMA((GATHER_PIECES, 8)),
            pltpu.SemaphoreType.DMA((GATHER_PIECES, 8)),
            pltpu.SemaphoreType.DMA((LAYERS, 6)),
            pltpu.SemaphoreType.DMA,
        ],
        compiler_params=pltpu.CompilerParams(collective_id=1, has_side_effects=True, vmem_limit_bytes=56 << 20),
    )(steps, x, qkv, out, up, down, time, norm, bias)


class Scatter(Exchange):
    slots = 10

    def __init__(self, place, grads, received, total, groups, send, recv):
        self.place, self.grads, self.received, self.total = place, grads, received, total
        self.first, self.count = groups
        self.span = pl.ds(*groups)
        self.send, self.recv = send, recv

    def copy(self, slot):
        p, span = self.place, self.span
        core, diag_y, diag_x, col_x, col_y, along = self.received
        low, high = pl.ds(0, 2), pl.ds(2, 2)
        to_x, to_y = p.device(p.z, p.yx_x, p.t), p.device(p.z, p.yx_y, p.t)
        if slot == 0:
            src, dst, device = self.grads.at[span, 1 - p.t], core.at[span], p.device(p.z, p.yx, 1 - p.t)
        elif slot == 1:
            src, dst, device = self.grads.at[span, p.t, low, p.yx_d], diag_y.at[span], to_y
        elif slot == 2:
            src, dst, device = self.grads.at[span, p.t, high, p.yx_d], diag_x.at[span], to_x
        elif slot == 3:
            src, dst, device = self.grads.at[span, p.t, low, p.yx_x], col_x.at[span, low], to_x
        elif slot == 4:
            src, dst, device = self.grads.at[span, p.t, high, p.yx_y], col_y.at[span, high], to_y
        elif slot == 5:
            src, dst, device = self.grads.at[span, p.t, high, p.yx_x], col_x.at[span, high], to_x
        elif slot == 6:
            src, dst, device = self.grads.at[span, p.t, low, p.yx_y], col_y.at[span, low], to_y
        else:
            there = p.z_ahead(slot - 6)
            src, dst, device = self.grads.at[span, p.t, there, p.yx], along.at[slot - 7, span], p.device(there, p.yx, p.t)
        return self.remote(slot, src, dst, device)

    def add(self, where, terms):
        def one(group, carry):
            ref = self.grads.at[(group, self.place.t) + where]
            value = ref[...].astype(F32)
            for term in terms:
                value = value + term[group].astype(F32)
            ref[...] = value.astype(BF16)
            return carry

        lax.fori_loop(self.first, self.first + self.count, one, 0)

    def step(self, number):
        p = self.place
        core, diag_y, diag_x, col_x, col_y, along = self.received
        every = slice(None)
        if number == 0:
            self.start(0)
        elif number == 1:
            self.arrived(0)
            self.add((every, every), [core])
            for slot in (1, 2, 5, 6):
                self.start(slot)
        elif number == 2:
            self.arrived(1)
            self.add((pl.ds(0, 2), p.yx_x), [diag_y])
            self.start(3)
            self.arrived(2)
            self.add((pl.ds(2, 2), p.yx_y), [diag_x])
            self.start(4)
        elif number == 3:
            self.arrived(3, 4, 5, 6)
            self.add((every, p.yx), [col_x, col_y])
            for slot in (7, 8, 9):
                self.start(slot)
        elif number == 4:
            self.arrived(7, 8, 9)

            def one(group, carry):
                value = self.grads[group, p.t, p.z, p.yx].astype(F32)
                for k in range(3):
                    value = value + along[k, group].astype(F32)
                self.total[group] = value
                return carry

            lax.fori_loop(self.first, self.first + self.count, one, 0)


class SmallSum(Exchange):
    slots = 6

    def __init__(self, place, sums, received, total, send, recv):
        self.place, self.sums, self.received, self.total = place, sums, received, total
        self.send, self.recv = send, recv

    def copy(self, slot):
        p = self.place
        if slot == 0:
            device = p.device(p.z, p.yx, 1 - p.t)
        elif slot < 3:
            device = p.device(p.z, p.yx_x if slot == 1 else p.yx_y, p.t)
        else:
            device = p.device(p.z_ahead(slot - 2), p.yx, p.t)
        return self.remote(slot, self.sums.at[min(slot, 3)], self.received.at[slot], device)

    def step(self, number):
        if number > 0:
            slots = (3, 4, 5) if number == 4 else (number - 1,)
            value = self.sums[number - 1]
            self.arrived(*slots)
            for slot in slots:
                value = value + self.received[slot]
            if number < 4:
                self.sums[number] = value
            else:
                self.total[...] = value
        if number < 3:
            self.start(number)
        elif number == 3:
            for slot in (3, 4, 5):
                self.start(slot)


GRAD_GROUPS = 13
SCATTER_PIECES = ((4, 2), (6, 2), (8, 2), (10, 2), (3, 1), (0, 1), (1, 1), (2, 1), (12, 1))


def backward_kernel(
    rep,
    scale_ref, small_ref, feats_ref, cot_ref, w_in, entry_in, middle_in, qkv_in, probs_in, attn_in, hidden_in, slope_in,
    grad_out, total_out, sums_out, time_out,
    w, gx, dattn, du, hidden, attn, n1t, n2t, gdt, got, dqkv, grads, item_grad, acc, acc_bias,
    r_core, r_dy, r_dx, r_x, r_y, r_z, sums, r_sums, r_time,
    w_sem, in_sem, send, recv, small_send, small_recv, time_send, time_recv,
):
    place = Place(rep)
    t = place.t
    rows = gx.shape[0]
    items = rows // LENGTH
    wide = lambda cols: pl.BlockSpec((LENGTH, cols), lambda i: (i, 0))
    lane = lax.broadcasted_iota(jnp.int32, (1, 128), 1)
    even_mask = jnp.where(lane < HEAD_DIM, 1.0, 0.0).astype(BF16)
    odd_mask = jnp.where(lane < HEAD_DIM, 0.0, 1.0).astype(BF16)
    times = Timeline()

    def load_weights(layer):
        copies = []
        for number, (first, count) in enumerate(((3, 9), (0, 3))):
            copy = pltpu.make_async_copy(
                w_in.at[layer, pl.ds(first, count)], w.at[pl.ds(first, count)], w_sem.at[layer, number]
            )
            copies.append(copy)
        return copies

    def load_stash(layer):
        return [
            pltpu.make_async_copy(hidden_in.at[layer], hidden, in_sem.at[layer, 0]),
            pltpu.make_async_copy(attn_in.at[layer], attn, in_sem.at[layer, 1]),
        ]

    def norm_back(hat, inverse, dy, layer, row, here):
        acc[row] += fold_rows(dy * hat)
        acc[row + 1] += fold_rows(dy)
        scaled = dy * small_ref[layer * 5 + row : layer * 5 + row + 1]
        mean = jnp.mean(scaled, -1, keepdims=True)
        along = jnp.mean(scaled * hat, -1, keepdims=True)
        return inverse * (scaled - mean - hat * along)

    def feed_phase(layer):
        last = layer == LAYERS - 1

        def body(item, poll, middle_blk, slope_blk, *rest):
            here = pl.ds(pl.multiple_of(item * LENGTH, LENGTH), LENGTH)
            if last:
                grad = rest[0][...].astype(F32) * scale_ref[t * items + item]
            else:
                grad = gx[here]
            acc[4] += fold_rows(grad)
            low = grad.astype(BF16)
            gdt[:, here] = low.T
            back = jnp.zeros((LENGTH, 512), F32)
            for part in range(4):
                span = slice(part * 512, (part + 1) * 512)
                dh = nn(low, weight(w, 5 + 2 * part))
                pre_grad = (dh * slope_blk[:, span].astype(F32)).astype(BF16)
                du[here, span] = pre_grad
                acc_bias[part] += fold_rows(pre_grad.astype(F32))
                back = back + nt(pre_grad, weight(w, 4 + 2 * part))
            hat, inverse = normalize(middle_blk[...])
            normed = hat * small_ref[layer * 5 + 2 : layer * 5 + 3] + small_ref[layer * 5 + 3 : layer * 5 + 4]
            n2t[:, here] = normed.astype(BF16).T
            grad = grad + norm_back(hat, inverse, back, layer, 2, here)
            gx[here] = grad
            low = grad.astype(BF16)
            got[:, here] = low.T
            dattn[here] = nn(low, weight(w, 3)).astype(BF16)

        each_item(
            body, [(times.slot(FEED_BACK), []) for _ in range(items)], items, [wide(512), wide(2048)] + ([wide(512)] if last else []), [],
            [middle_in.at[layer], slope_in.at[layer]] + ([cot_ref] if last else []),
        )

    def attention_phase(layer):
        def body(item, poll, entry_blk, qkv_blk, probs_blk, *rest):
            here = pl.ds(pl.multiple_of(item * LENGTH, LENGTH), LENGTH)
            def sides(pair):
                query = qkv_blk[:, pair * 128 : (pair + 1) * 128]
                key = qkv_blk[:, 512 + pair * 128 : 512 + (pair + 1) * 128]
                value = qkv_blk[:, 1024 + pair * 128 : 1024 + (pair + 1) * 128]
                back = dattn[here, pair * 128 : (pair + 1) * 128]
                split = lambda v: [v * even_mask, v * odd_mask]
                return split(query), split(key), value, split(back)

            def scores(pair):
                _, _, value, back = sides(pair)
                return [nt(side, value) for side in back]

            def products(pair, dscores):
                query, key, _, back = sides(pair)
                probs = [probs_blk[0, pair * 2 + side] for side in range(2)]
                tall = jnp.concatenate(dscores, 0)
                dq = nn(jnp.concatenate(dscores, 1), jnp.concatenate(key, 0)) * HEAD_DIM**-0.5
                dk = tn(tall, jnp.concatenate(query, 0))
                dv = tn(jnp.concatenate(probs, 0), jnp.concatenate(back, 0))
                for slot, value in enumerate((dq, dk, dv)):
                    dqkv[here, slot * 512 + pair * 128 : slot * 512 + (pair + 1) * 128] = value.astype(BF16)

            ahead, held = scores(0), None
            for pair in range(4):
                both = ahead
                if pair == 2:
                    poll()
                if pair < 3:
                    ahead = scores(pair + 1)
                dscores = []
                for side in range(2):
                    probs = probs_blk[0, pair * 2 + side].astype(F32)
                    mixed = probs * both[side]
                    dscores.append((mixed - probs * jnp.sum(mixed, -1, keepdims=True)).astype(BF16))
                if held is not None:
                    products(pair - 1, held)
                held = dscores
            products(3, held)
            back = jnp.zeros((LENGTH, 512), F32)
            for slot in range(3):
                back = back + nt(dqkv[here, slot * 512 : (slot + 1) * 512], weight(w, slot))
            hat, inverse = normalize(entry_blk[...])
            normed = hat * small_ref[layer * 5 : layer * 5 + 1] + small_ref[layer * 5 + 1 : layer * 5 + 2]
            n1t[:, here] = normed.astype(BF16).T
            grad = gx[here] + norm_back(hat, inverse, back, layer, 0, here)
            item_grad[pl.ds(item, 1)] = jnp.sum(grad, 0, keepdims=True)
            if layer == 0:
                rest[0][...] = grad.astype(BF16)
            else:
                gx[here] = grad

        slots = [(times.slot(ATTENTION_BACK / 2), times.slot(ATTENTION_BACK / 2)) for _ in range(items)]
        each_item(
            body, slots, items,
            [wide(512), wide(1536), pl.BlockSpec((1, 8, 256, 256), lambda i: (i, 0, 0, 0))],
            [wide(512)] if layer == 0 else [],
            [entry_in.at[layer], qkv_in.at[layer], probs_in.at[layer]] + ([grad_out] if layer == 0 else []),
        )

    def keep_grad(group, value):
        for half in range(2):
            grads[group, half] = value[:, half * 256 : (half + 1) * 256].astype(BF16).reshape(4, 4, 32, 256)

    def weight_grad(left, right, group, part):
        keep_grad(group, nn(left[...], right[:, part * 512 : (part + 1) * 512]))

    scatters, smalls = [], []
    for layer in range(LAYERS):
        received = [r.at[layer] for r in (r_core, r_dy, r_dx, r_x, r_y, r_z)]
        scatters.append(
            [
                Scatter(place, grads, received, total_out.at[layer], groups, send.at[layer, i], recv.at[layer, i])
                for i, groups in enumerate(SCATTER_PIECES)
            ]
        )
        smalls.append(
            SmallSum(place, sums.at[layer], r_sums.at[layer], sums_out.at[layer], small_send.at[layer], small_recv.at[layer])
        )

    order = [LAYERS - 1 - i for i in range(LAYERS)]
    weights = {order[0]: load_weights(order[0])}
    stash = {order[0]: load_stash(order[0])}
    for copy in weights[order[0]] + stash[order[0]]:
        copy.start()
    item_grad[...] = jnp.zeros(item_grad.shape, F32)
    place.greet()

    def clear(layer, piece):
        if layer != order[0]:
            before = scatters[order[order.index(layer) - 1]][scatters[layer].index(piece)]
            play(times.force((before, 4)))
            before.finish()

    def begin(piece):
        piece.step(0)
        times.scatter(piece, UNIT * piece.count)

    for turn, layer in enumerate(order):
        feed_pieces, late_pieces = scatters[layer][:5], scatters[layer][5:]
        acc[...] = jnp.zeros(acc.shape, F32)
        acc_bias[...] = jnp.zeros(acc_bias.shape, F32)
        weights[layer][0].wait()
        feed_phase(layer)
        stash[layer][0].wait()
        stash[layer][1].wait()
        weights[layer][1].wait()
        for part, piece in enumerate(feed_pieces):
            clear(layer, piece)
            if part < 4:
                weight_grad(n2t, du, 4 + 2 * part, part)
                weight_grad(gdt, hidden, 5 + 2 * part, part)
            else:
                weight_grad(got, attn, 3, 0)
            times.passed(GRAD * piece.count)
            begin(piece)
            play(times.slot(0.0))
        attention_phase(layer)
        if turn + 1 < LAYERS:
            after = order[turn + 1]
            weights[after] = load_weights(after)
            stash[after] = load_stash(after)
            for copy in weights[after] + stash[after]:
                copy.start()
        for piece in late_pieces:
            clear(layer, piece)
        spread = lax.dot_general(
            feats_ref[...], item_grad[...], (((0,), (0,)), ((), ())),
            precision=lax.Precision.HIGHEST, preferred_element_type=F32,
        )
        keep_grad(12, spread)
        begin(late_pieces[3])
        for row in range(5):
            sums[layer, 0, row : row + 1] = jnp.sum(acc[row], 0, keepdims=True)
        for part in range(4):
            sums[layer, 0, 5 + part : 6 + part] = jnp.sum(acc_bias[part], 0, keepdims=True)
        sums[layer, 0, 9:16] = jnp.zeros((7, 512), F32)
        smalls[layer].step(0)
        times.small(smalls[layer])
        for slot in range(3):
            weight_grad(n1t, dqkv, slot, slot)
            times.passed(GRAD)
            begin(late_pieces[slot])
            play(times.slot(0.0))
    play(times.force(*[(piece, 4) for layer in range(LAYERS) for piece in scatters[layer] + [smalls[layer]]]))

    swaps = []
    for layer in range(LAYERS):
        swap = pltpu.make_async_remote_copy(
            src_ref=total_out.at[layer, 12, pl.ds(pl.multiple_of((1 - t) * 16, 16), 16)],
            dst_ref=r_time.at[layer], send_sem=time_send.at[layer], recv_sem=time_recv.at[layer],
            device_id=place.device(place.z, place.yx, 1 - t), device_id_type=MESH,
        )
        swap.start()
        swaps.append(swap)
    for layer in range(LAYERS):
        swaps[layer].wait()
        time_out[layer, :, place.cols] = total_out[layer, 12, pl.ds(pl.multiple_of(t * 16, 16), 16)]
        time_out[layer, :, place.other_cols] = r_time[layer]
    for piece in scatters[order[-1]]:
        piece.finish()
    for piece in smalls:
        piece.finish()


def backward_call(rep, rows, scale, small, feats, cot, w, entry, middle, qkv, probs, attn, hidden, slope):
    items = rows // LENGTH
    hbm = pl.BlockSpec(memory_space=pl.ANY)
    vmem = pl.BlockSpec(memory_space=pltpu.VMEM)
    smem = pl.BlockSpec(memory_space=pltpu.SMEM)
    shape = jax.ShapeDtypeStruct
    pieces = len(SCATTER_PIECES)
    dma = pltpu.SemaphoreType.DMA
    return pl.pallas_call(
        functools.partial(backward_kernel, rep),
        name="backward",
        in_specs=[smem, vmem, vmem] + [hbm] * 9,
        out_shape=[
            shape((rows, 512), BF16),
            shape((LAYERS, GRAD_GROUPS, 32, 256), F32),
            shape((LAYERS, 16, 512), F32),
            shape((LAYERS, 16, 512), F32),
        ],
        out_specs=[hbm, vmem, vmem, vmem],
        scratch_shapes=[
            pltpu.VMEM((12, 2, 4, 4, 32, 256), BF16),
            pltpu.VMEM((rows, 512), F32),
            pltpu.VMEM((rows, 512), BF16),
            pltpu.VMEM((rows, 2048), BF16),
            pltpu.VMEM((rows, 2048), BF16),
            pltpu.VMEM((rows, 512), BF16),
            pltpu.VMEM((512, rows), BF16),
            pltpu.VMEM((512, rows), BF16),
            pltpu.VMEM((512, rows), BF16),
            pltpu.VMEM((512, rows), BF16),
            pltpu.VMEM((rows, 1536), BF16),
            pltpu.VMEM((GRAD_GROUPS, 2, 4, 4, 32, 256), BF16),
            pltpu.VMEM((8, 512), F32),
            pltpu.VMEM((5, 8, 512), F32),
            pltpu.VMEM((4, 8, 512), F32),
            pltpu.VMEM((LAYERS, GRAD_GROUPS, 4, 4, 32, 256), BF16),
            pltpu.VMEM((LAYERS, GRAD_GROUPS, 2, 32, 256), BF16),
            pltpu.VMEM((LAYERS, GRAD_GROUPS, 2, 32, 256), BF16),
            pltpu.VMEM((LAYERS, GRAD_GROUPS, 4, 32, 256), BF16),
            pltpu.VMEM((LAYERS, GRAD_GROUPS, 4, 32, 256), BF16),
            pltpu.VMEM((LAYERS, 3, GRAD_GROUPS, 32, 256), BF16),
            pltpu.VMEM((LAYERS, 4, 16, 512), F32),
            pltpu.VMEM((LAYERS, 6, 16, 512), F32),
            pltpu.VMEM((LAYERS, 16, 256), F32),
            dma((LAYERS, 2)),
            dma((LAYERS, 2)),
            dma((LAYERS, pieces, 10)),
            dma((LAYERS, pieces, 10)),
            dma((LAYERS, 6)),
            dma((LAYERS, 6)),
            dma((LAYERS,)),
            dma((LAYERS,)),
        ],
        compiler_params=pltpu.CompilerParams(collective_id=2, has_side_effects=True, vmem_limit_bytes=62 << 20),
    )(scale, small, feats, cot, w, entry, middle, qkv, probs, attn, hidden, slope)


def adamw(weight, gradient, first_moment, second_moment, rate):
    first_new = beta_first * first_moment + (1.0 - beta_first) * gradient
    second_new = beta_second * second_moment + (1.0 - beta_second) * gradient * gradient
    first_corr = first_new * (1.0 / (1.0 - beta_first**STEP))
    second_corr = second_new * (1.0 / (1.0 - beta_second**STEP))
    weight_new = weight - rate * (first_corr / (jnp.sqrt(second_corr) + adam_eps) + weight_decay * weight)
    return (weight_new, first_new, second_new)


def update_kernel(*refs):
    hbm, outs, ins = refs[:26], refs[26:50], refs[50:74]
    row, sems = refs[74:]
    copies = [pltpu.make_async_copy(src, dst, sems.at[i]) for i, (src, dst) in enumerate(zip(hbm[:24], ins))]
    copies += [pltpu.make_async_copy(hbm[24 + i], outs[i], sems.at[24 + i]) for i in range(2)]
    for copy in copies:
        copy.start()
    for copy in copies[:24]:
        copy.wait()
    total, sums, time_grad, *ins = ins
    outs = outs[2:]
    qkv, out, up, bias, down, norm, time = [ins[i * 3 : i * 3 + 3] for i in range(7)]
    qkv_new, key_second, value_second = outs[0:2], outs[2], outs[3]
    out_new, up_new, bias_new, down_new, norm_new, time_new = [outs[4 + i * 3 : 7 + i * 3] for i in range(6)]
    dp, t = lax.axis_index("dp"), lax.axis_index("tensor")

    def one(old, new, where, gradient, rate):
        values = adamw(old[0][where], gradient, old[1][where], old[2][where], rate)
        for ref, value in zip(new, values):
            ref[where] = value
        return values

    for layer in range(LAYERS):
        for slot in range(3):
            values = adamw(qkv[0][layer, slot], total[layer, slot], qkv[1][layer, slot], qkv[2][layer, slot], learn_rate)
            for ref, value in zip(qkv_new, values):
                ref[layer, slot] = value
            if slot < 2:
                key_second[layer, :, slot] = values[2]
            else:
                value_second[layer] = values[2]
        one(out, out_new, (layer,), total[layer, 3], learn_rate)
        for part in range(4):
            where = (layer, slice(None), slice(part * 256, (part + 1) * 256))
            one(up, up_new, where, total[layer, 4 + 2 * part], learn_rate)
            one(down, down_new, where, total[layer, 5 + 2 * part], learn_rate)
        one(time, time_new, (layer,), time_grad[layer], learn_rate)

        width = norm[0].shape[2]
        start = (dp * 2 + t) * width
        tile = sums[layer, :, pl.ds(pl.multiple_of(start // 128 * 128, 128), 128)]
        mine = pltpu.roll(tile, (128 - start % 128) % 128, 1)[0:5, 0:width]
        one(norm, norm_new, (slice(None), layer), mine, norm_rate)
        for part in range(4):
            for half in range(2):
                span = pl.ds(pl.multiple_of(t * 256 + half * 128, 128), 128)
                row[part * 2 + half : part * 2 + half + 1] = sums[layer, 5 + part : 6 + part, span]
        width = bias[0].shape[2]
        mine = pltpu.roll(row[...], (128 - dp * width) % 128, 1)[:, 0:width]
        one(bias, bias_new, (layer,), mine, learn_rate)
    for copy in copies[24:]:
        copy.wait()


def update_call(total, sums, time_grad, states, row_results):
    flat = [total, sums, time_grad] + [array for state in states for array in state]
    like = lambda array: jax.ShapeDtypeStruct(array.shape, array.dtype)
    rows = states[0][0].shape[2]
    shapes = [like(array) for array in list(row_results) + flat[3:]]
    shapes[4:5] = [
        jax.ShapeDtypeStruct((LAYERS, rows, 2, 256), F32),
        jax.ShapeDtypeStruct((LAYERS, rows, 256), F32),
    ]
    vmem = pl.BlockSpec(memory_space=pltpu.VMEM)
    hbm = pl.BlockSpec(memory_space=pl.ANY)
    return pl.pallas_call(
        update_kernel,
        name="update",
        in_specs=[hbm] * 26,
        out_shape=shapes,
        out_specs=[vmem] * 24,
        scratch_shapes=[pltpu.VMEM(array.shape, F32) for array in flat]
        + [pltpu.VMEM((8, 128), F32), pltpu.SemaphoreType.DMA((26,))],
        compiler_params=pltpu.CompilerParams(vmem_limit_bytes=56 << 20),
    )(*flat, *row_results)


def per_device(
    rep,
    inputs, cotangent, timesteps, item_scale,
    qkv_weight, qkv_first, qkv_second,
    out_weight, out_first, out_second,
    up_weight, up_first, up_second,
    up_bias, bias_first, bias_second,
    down_weight, down_first, down_second,
    norm_params, norm_first, norm_second,
    time_weight, time_first, time_second,
):
    rows = inputs.shape[0]
    dp, t = lax.axis_index("dp"), lax.axis_index("tensor")
    qkv, out, up, down, bias = qkv_weight, out_weight, up_weight, down_weight, up_bias
    norm, time = norm_params, time_weight
    teams = None
    if rep > 1:
        size = GROUPS * rep
        teams = [[g * rep + j for j in range(rep)] for g in range(GROUPS)]
        pairs = [[g * rep * 2 + j for j in range(rep * 2)] for g in range(GROUPS)]
        join = lambda v, axis: lax.all_gather(v, "dp", axis=axis, axis_index_groups=teams, tiled=True)
        join_both = lambda v, axis: lax.all_gather(
            v, ("dp", "tensor"), axis=axis, axis_index_groups=pairs, tiled=True
        )
        qkv, out, up, down, bias = join(qkv, 1), join(out, 2), join(up, 1), join(down, 2), join(bias, 2)
        norm, time = join_both(norm, 2), join_both(time, 1)
        norm = lax.dynamic_slice_in_dim(norm, t * 16, 16, 2)
        time = lax.dynamic_slice_in_dim(time, t * 16, 16, 1)

    slots = lambda *arrays: [jnp.transpose(v, (0, 2, 1, 3)) for v in arrays]
    flip = lambda *arrays: [jnp.swapaxes(v, 1, 2) for v in arrays]
    front = lambda *arrays: [jnp.swapaxes(v, 0, 1) for v in arrays]
    w, small, feats, entry, middle, qkv_rows, probs, attn, hidden, slope, activations = forward_call(
        rep, rows, timesteps, inputs, *slots(qkv), *flip(out), up, *flip(down), time, *front(norm), bias
    )
    input_grad, total, sums, time_grad = backward_call(
        rep, rows, item_scale, small, feats, cotangent, w, entry, middle, qkv_rows, probs, attn, hidden, slope
    )

    if rep > 1:
        total = lax.psum_scatter(total, "dp", scatter_dimension=2, axis_index_groups=teams, tiled=True)
        sums, time_grad = lax.psum((sums, time_grad), "dp", axis_index_groups=teams)
        time_grad = lax.all_gather(time_grad, "tensor", axis=1, tiled=True)
        width = time_weight.shape[1]
        time_grad = lax.dynamic_slice_in_dim(time_grad, ((dp % rep) * 2 + t) * width, width, 1)

    activations, input_grad, *new = update_call(
        total, sums, time_grad,
        [
            slots(qkv_weight, qkv_first, qkv_second),
            flip(out_weight, out_first, out_second),
            [up_weight, up_first, up_second],
            [up_bias, bias_first, bias_second],
            flip(down_weight, down_first, down_second),
            front(norm_params, norm_first, norm_second),
            [time_weight, time_first, time_second],
        ],
        (activations, input_grad),
    )
    return (
        activations, input_grad,
        *slots(*new[0:2]), new[2], new[3],
        *flip(*new[4:7]), *new[7:10], *new[10:13], *flip(*new[13:16]), *front(*new[16:19]), *new[19:22],
    )


def solution(mesh):
    rep = mesh.shape["dp"] // GROUPS
    shard = P(None, "dp", None, "tensor")
    rows = P(("dp", "tensor"), None)
    trans = P(None, "tensor", "dp")
    flat = P(None, "dp", "tensor")
    norm = P(None, None, ("dp", "tensor"))
    time = P(None, ("dp", "tensor"), None)
    return jax.shard_map(
        functools.partial(per_device, rep),
        mesh=mesh,
        in_specs=(rows, rows, P("dp"), P("dp")) + (shard,) * 3 + (trans,) * 3 + (flat,) * 3 + (trans,) * 6 + (norm,) * 3 + (time,) * 3,
        out_specs=(rows, rows, shard, shard, shard, flat) + (trans,) * 3 + (flat,) * 3 + (trans,) * 6 + (norm,) * 3 + (time,) * 3,
        check_vma=False,
    )
```

```python
import functools
import math

import jax
import jax.numpy as jnp
from jax import lax
from jax.experimental import pallas as pl
from jax.experimental.pallas import tpu as pltpu
from jax.sharding import PartitionSpec as P

HEAD_DIM = 64
LENGTH = 256
LAYERS = 2
STEP = 8
GROUPS = 16
MESH = pl.DeviceIdType.MESH
F32 = jnp.float32
BF16 = jnp.bfloat16

beta_first = 0.5
beta_second = 0.5
learn_rate = 0.1
norm_rate = 0.4
weight_decay = 0.01
adam_eps = 1e-08
norm_eps = 1e-05


def nn(a, b):
    return lax.dot_general(a, b, (((1,), (0,)), ((), ())), preferred_element_type=F32)


def nt(a, b):
    return lax.dot_general(a, b, (((1,), (1,)), ((), ())), preferred_element_type=F32)


def tn(a, b):
    return lax.dot_general(a, b, (((0,), (0,)), ((), ())), preferred_element_type=F32)


def normalize(values):
    center = values - jnp.mean(values, -1, keepdims=True)
    inverse = lax.rsqrt(jnp.mean(center * center, -1, keepdims=True) + norm_eps)
    return center * inverse, inverse


def fold_rows(values):
    rows, cols = values.shape
    return jnp.sum(values.reshape(rows // 8, 8, cols), 0)


def gelu_and_slope(x):
    below = 0.5 + 0.5 * lax.erf(x * math.sqrt(0.5))
    return x * below, below + x * (jnp.exp(x * x * -0.5) * (1.0 / math.sqrt(2.0 * math.pi)))


class Place:
    def __init__(self, rep):
        dp = lax.axis_index("dp")
        self.rep = rep
        self.copy = dp % rep
        self.group = dp // rep
        self.t = lax.axis_index("tensor")
        self.z = self.group // 4
        self.yx = self.group % 4
        x, y = self.yx % 2, self.yx // 2
        self.yx_x = self.yx + 1 - 2 * x
        self.yx_y = self.yx + 2 - 4 * y
        self.yx_d = 3 - self.yx
        self.cols = pl.ds(pl.multiple_of(self.t * 256, 256), 256)
        self.other_cols = pl.ds(pl.multiple_of((1 - self.t) * 256, 256), 256)

    def device(self, z, yx, t):
        return ((z * 4 + yx) * self.rep + self.copy, t)

    def z_ahead(self, k):
        return (self.z + k) % 4

    @property
    def partners(self):
        return [self.device(self.z_ahead(k), self.yx, self.t) for k in (1, 2, 3)] + [
            self.device(self.z, self.yx_x, self.t),
            self.device(self.z, self.yx_y, self.t),
            self.device(self.z, self.yx, 1 - self.t),
        ]

    def greet(self):
        barrier = pltpu.get_barrier_semaphore()
        for partner in self.partners:
            pl.semaphore_signal(barrier, inc=1, device_id=partner, device_id_type=MESH)
        pl.semaphore_wait(barrier, len(self.partners))


class Exchange:
    def start(self, slot):
        self.copy(slot).start()

    def arrived(self, *slots):
        for slot in slots:
            self.copy(slot).wait_recv()

    def finish(self):
        for slot in range(self.slots):
            self.copy(slot).wait_send()

    def remote(self, slot, src, dst, device):
        return pltpu.make_async_remote_copy(
            src_ref=src, dst_ref=dst, send_sem=self.send.at[slot], recv_sem=self.recv.at[slot],
            device_id=device, device_id_type=MESH,
        )


class Gather(Exchange):
    slots = 8

    def __init__(self, place, view, core_view, send, recv):
        self.place, self.view, self.core_view, self.send, self.recv = place, view, core_view, send, recv

    def copy(self, slot):
        p = self.place
        if slot < 3:
            ref, device = self.view(p.z, p.yx), p.device(p.z_ahead(slot + 1), p.yx, p.t)
        elif slot < 5:
            ref, device = self.view(slice(None), p.yx), p.device(p.z, p.yx_x if slot == 3 else p.yx_y, p.t)
        elif slot == 5:
            ref, device = self.view(pl.ds(0, 2), p.yx_x), p.device(p.z, p.yx_y, p.t)
        elif slot == 6:
            ref, device = self.view(pl.ds(2, 2), p.yx_y), p.device(p.z, p.yx_x, p.t)
        else:
            ref, device = self.core_view(), p.device(p.z, p.yx, 1 - p.t)
        return self.remote(slot, ref, ref, device)

    def step(self, number):
        if number == 0:
            for slot in (0, 1, 2):
                self.start(slot)
        elif number == 1:
            self.arrived(0, 1, 2)
            self.start(3)
            self.start(4)
        elif number == 2:
            self.arrived(3)
            self.start(5)
            self.arrived(4)
            self.start(6)
        elif number == 3:
            self.arrived(5, 6)
            self.start(7)
        elif number == 4:
            self.arrived(7)


def play(events):
    for piece, number in events:
        piece.step(number)


class Timeline:
    def __init__(self):
        self.now = 0.0
        self.queue = []
        self.links = 0.0
        self.along = 0.0
        self.count = 0

    def push(self, piece, dues, turns):
        for number, (due, turn) in enumerate(zip(dues, turns), 1):
            self.queue.append((self.count + turn, due, number, piece))
        self.queue.sort(key=lambda event: event[0])
        self.count += 1

    def gather(self, piece, unit):
        self.along += 4 * unit
        arrived = self.along + GATHER_WAIT
        begun = max(self.links, arrived)
        self.links = begun + 6 * unit
        columns, diagonal = begun + 4 * unit + GATHER_WAIT, begun + 6 * unit + GATHER_WAIT
        self.push(piece, [max(arrived, begun - LEAD), columns, diagonal, diagonal + 1.6 * unit + GATHER_WAIT], GATHER_TURNS)

    def scatter(self, piece, unit):
        added = self.now + 1.6 * unit + WAIT
        begun = max(self.links, added)
        self.links = begun + 6 * unit
        summed = begun + 8 * unit + WAIT
        self.along = max(self.along, summed) + 4 * unit
        self.push(piece, [max(added, begun - LEAD), begun + 4 * unit + WAIT, summed, self.along + WAIT], SCATTER_TURNS)

    def small(self, piece):
        self.push(piece, [self.now + 3.0 * number for number in (1, 2, 3, 4)], SCATTER_TURNS)

    def take(self, count):
        ready, self.queue = self.queue[:count], self.queue[count:]
        return [(piece, number) for _, _, number, piece in ready]

    def slot(self, length):
        count = 0
        while count < len(self.queue) and self.queue[count][1] <= self.now:
            count += 1
        self.now += length + COST * count
        return self.take(count)

    def passed(self, length):
        self.now += length

    def force(self, *wanted):
        count = max([i + 1 for i, event in enumerate(self.queue) if (event[3], event[2]) in wanted], default=0)
        self.now = max([self.now] + [event[1] for event in self.queue[:count]])
        return self.take(count)


WAIT = 5.0
GATHER_WAIT = 3.0
LEAD = 2.0
GATHER_TURNS = (-1.9, 0.0, 1.05, 2.3)
SCATTER_TURNS = (0.0, 1.1, 3.2, 5.3)
COST = 0.2
UNIT = 0.33


def each_item(body, slots, count, in_specs, out_specs, refs):
    def whole(*blocks):
        item = pl.program_id(0)

        def poll(half):
            for number, events in enumerate(slots):
                if events[half]:
                    pl.when(item == number)(functools.partial(play, events[half]))

        poll(0)
        body(item, poll, *blocks)

    pltpu.emit_pipeline(whole, grid=(count,), in_specs=in_specs, out_specs=out_specs)(*refs)


GATHER_PIECES = 16


def weight(ref, group):
    return jnp.concatenate([ref[group, 0].reshape(512, 256), ref[group, 1].reshape(512, 256)], 1)


def forward_kernel(
    rep,
    steps_ref, x_ref, qkv_ref, out_ref, up_ref, down_ref, time_ref, norm_ref, bias_ref,
    w_out, small_out, feats_out, entry_out, middle_out, qkv_out, probs_out, attn_out, hidden_out, slope_out, act_out,
    w, tw, nb, norms, bias, shifts, stream, attn, rounded, tile, send, recv, keep_sem, act_sem,
):
    place = Place(rep)
    z, yx, t = place.z, place.yx, place.t
    rows = stream.shape[0]
    items = rows // LENGTH

    pieces = []

    def piece(ref, *lead):
        number = len(pieces)
        pieces.append(
            Gather(
                place,
                lambda a, b: ref.at[(*lead, t, a, b)],
                lambda: ref.at[(*lead, t)],
                send.at[number],
                recv.at[number],
            )
        )
        return pieces[-1]

    norm_piece, bias_piece = piece(nb, 0), piece(nb, 1)
    time_pieces = [piece(tw, layer) for layer in range(LAYERS)]
    spans = ((0, 3), (3, 1), (4, 2), (6, 2), (8, 2), (10, 2))
    layer_pieces = [[piece(w, layer, pl.ds(*span)) for span in spans] for layer in range(LAYERS)]

    tile[...] = jnp.zeros(tile.shape, F32)
    for layer in range(LAYERS):
        for row in range(5):
            at = layer * 5 + row
            tile[0, at : at + 1, 0:16] = norm_ref[row, layer : layer + 1]
        tile[1, layer * 8 : (layer + 1) * 8, 0:8] = bias_ref[layer]
    nb[0, t, z, yx] = pltpu.roll(tile[0], (yx * 2 + t) * 16, 1)
    nb[1, t, z, yx] = pltpu.roll(tile[1], place.group * 8, 1)

    def own_attention(layer):
        tw[layer, t, z, yx] = time_ref[layer].astype(BF16)
        for slot in range(3):
            w[layer, slot, t, z, yx] = qkv_ref[layer, slot].astype(BF16)

    def own_feed(layer):
        w[layer, 3, t, z, yx] = out_ref[layer].astype(BF16)
        for part in range(4):
            own = slice(part * 256, (part + 1) * 256)
            w[layer, 4 + 2 * part, t, z, yx] = up_ref[layer, :, own].astype(BF16)
            w[layer, 5 + 2 * part, t, z, yx] = down_ref[layer, :, own].astype(BF16)

    own_attention(0)
    place.greet()
    opening = [norm_piece, time_pieces[0], layer_pieces[0][0]]
    rest = [layer_pieces[0][1], bias_piece] + layer_pieces[0][2:] + [time_pieces[1]] + layer_pieces[1]
    for entry in opening:
        entry.step(0)
    own_feed(0)
    own_attention(1)
    own_feed(1)
    for entry in rest:
        entry.step(0)
    sizes = {norm_piece: 0.25, bias_piece: 0.25}
    for layer in range(LAYERS):
        sizes[time_pieces[layer]] = 2
        sizes.update((entry, span[1]) for entry, span in zip(layer_pieces[layer], spans))
    times = Timeline()
    for entry in opening + rest:
        times.gather(entry, UNIT * sizes[entry])
    wanted = [(entry, 4) for entry in opening]
    play(times.force(*[(entry, 3) for entry in opening]))

    line = lax.broadcasted_iota(jnp.int32, (8, 256), 0)
    column = lax.broadcasted_iota(jnp.int32, (8, 256), 1).astype(F32)
    angles = jnp.zeros((8, 256), F32)
    for item in range(items):
        angles = jnp.where(line == item, steps_ref[t * items + item].astype(F32), angles)
    angles = angles * jnp.exp(column * (-math.log(10000.0) / 256))
    live = line < items
    feats = jnp.concatenate(
        [jnp.where(live, jnp.sin(angles), 0.0), jnp.where(live, jnp.cos(angles), 0.0)], 1
    )
    feats_out[...] = feats
    feats_high = feats.astype(BF16)
    feats_low = (feats - feats_high.astype(F32)).astype(BF16)

    play(times.force(*wanted))
    for zz in range(4):
        total = jnp.zeros((16, 128), F32)
        for part in range(8):
            total = total + nb[0, part % 2, zz, part // 2]
        norms[:, zz * 128 : (zz + 1) * 128] = total
    small_out[...] = norms[...]

    def spread_times(layer):
        table = [tw[layer, core].reshape(GROUPS, 16, 512) for core in range(2)]
        table = jnp.concatenate([table[0][:, None], table[1][:, None]], 1).reshape(512, 512)
        shifts[layer * 8 : (layer + 1) * 8] = nn(feats_high, table) + nn(feats_low, table)

    def spread_bias():
        for core in range(2):
            total = jnp.zeros((16, 128), F32)
            for part in range(16):
                total = total + nb[1, core, part // 4, part % 4]
            total = total.astype(BF16).astype(F32)
            for layer in range(LAYERS):
                for part in range(4):
                    for half in range(2):
                        row = layer * 8 + part * 2 + half
                        col = core * 256 + half * 128
                        bias[layer, part, 0:1, col : col + 128] = total[row : row + 1]

    lane = lax.broadcasted_iota(jnp.int32, (1, 128), 1)
    even_mask = jnp.where(lane < HEAD_DIM, 1.0, 0.0).astype(BF16)
    odd_mask = jnp.where(lane < HEAD_DIM, 0.0, 1.0).astype(BF16)
    wide = lambda cols: pl.BlockSpec((LENGTH, cols), lambda i: (i, 0))

    def attention_phase(layer):
        def body(item, poll, *refs):
            if layer == 0:
                x_blk, *refs = refs
            entry_blk, qkv_blk, probs_blk, attn_blk = refs
            here = pl.ds(pl.multiple_of(item * LENGTH, LENGTH), LENGTH)
            start = x_blk[...].astype(F32) if layer == 0 else stream[here]
            entry = start + shifts[pl.ds(layer * 8 + item, 1)]
            entry_blk[...] = entry
            stream[here] = entry
            hat, _ = normalize(entry)
            normed = (hat * norms[layer * 5 : layer * 5 + 1] + norms[layer * 5 + 1 : layer * 5 + 2]).astype(BF16)
            for slot in range(3):
                projected = nn(normed, weight(w.at[layer], slot)).astype(BF16)
                if slot == 0:
                    projected = projected * jnp.asarray(HEAD_DIM**-0.5, BF16)
                qkv_blk[:, slot * 512 : (slot + 1) * 512] = projected

            def scores(pair):
                query = qkv_blk[:, pair * 128 : (pair + 1) * 128]
                key = qkv_blk[:, 512 + pair * 128 : 512 + (pair + 1) * 128]
                return [nt(query * mask, key) for mask in (even_mask, odd_mask)]

            ahead = scores(0)
            for pair in range(4):
                both = ahead
                if pair < 3:
                    ahead = scores(pair + 1)
                span = slice(pair * 128, (pair + 1) * 128)
                value = qkv_blk[:, 1024 + pair * 128 : 1024 + (pair + 1) * 128]
                probs = []
                for side in range(2):
                    raised = jnp.exp(both[side] - jnp.max(both[side], -1, keepdims=True))
                    probs.append((raised * (1.0 / jnp.sum(raised, -1, keepdims=True))).astype(BF16))
                    probs_blk[0, pair * 2 + side] = probs[side]
                values = jnp.concatenate([value * even_mask, value * odd_mask], 0)
                joined = nn(jnp.concatenate(probs, 1), values).astype(BF16)
                attn_blk[:, span] = joined
                attn[here, span] = joined

        each_item(
            body, [(times.slot(ATTENTION),) for _ in range(items)], items,
            [wide(512)] if layer == 0 else [],
            [wide(512), wide(1536), pl.BlockSpec((1, 8, 256, 256), lambda i: (i, 0, 0, 0)), wide(512)],
            ([x_ref] if layer == 0 else [])
            + [entry_out.at[layer], qkv_out.at[layer], probs_out.at[layer], attn_out.at[layer]],
        )

    def middle_phase(layer):
        def body(item, poll, middle_blk):
            here = pl.ds(pl.multiple_of(item * LENGTH, LENGTH), LENGTH)
            middle = stream[here] + nt(attn[here], weight(w.at[layer], 3))
            middle_blk[...] = middle
            hat, _ = normalize(middle)
            normed = hat * norms[layer * 5 + 2 : layer * 5 + 3] + norms[layer * 5 + 3 : layer * 5 + 4]
            rounded[here] = normed.astype(BF16)
            stream[here] = middle + norms[layer * 5 + 4 : layer * 5 + 5]

        slots = [(times.slot(MIDDLE), []) for _ in range(items)]
        each_item(body, slots, items, [], [wide(512)], [middle_out.at[layer]])

    def feed_phase(layer, keep):
        def body(part, poll, hidden_blk, slope_blk):
            blocks = [slice(i * LENGTH, (i + 1) * LENGTH) for i in range(items)]
            up, down, shift = weight(w.at[layer], 4 + 2 * part), weight(w.at[layer], 5 + 2 * part), bias[layer, part]
            lift = lambda i: nn(rounded[blocks[i]], up) + shift[0:1]

            def lower(i, hidden):
                stream[blocks[i]] += nt(hidden, down)

            ahead, held = lift(0), None
            for i in range(items):
                pre = ahead
                if i + 1 < items:
                    ahead = lift(i + 1)
                hidden, slope = gelu_and_slope(pre)
                if held is not None:
                    lower(i - 1, held)
                held = hidden.astype(BF16)
                hidden_blk[blocks[i]] = held
                slope_blk[blocks[i]] = slope.astype(BF16)
            lower(items - 1, held)

        slots = []
        for part in range(4):
            entry = layer_pieces[layer][2 + part]
            slots.append((times.force((entry, 4)) + [(Start(keep[2 + part]), 0)], []))
            times.passed(FEED)
        tall = pl.BlockSpec((rows, 512), lambda i: (0, i))
        each_item(body, slots, 4, [], [tall, tall], [hidden_out.at[layer], slope_out.at[layer]])

    spread_times(0)
    keeps = []
    for layer in range(LAYERS):
        keep = [
            pltpu.make_async_copy(w.at[layer, pl.ds(*span)], w_out.at[layer, pl.ds(*span)], keep_sem.at[layer, i])
            for i, span in enumerate(spans)
        ]
        keeps += keep
        if layer > 0:
            play(times.force((time_pieces[layer], 4), (layer_pieces[layer][0], 4)))
            spread_times(layer)
        keep[0].start()
        attention_phase(layer)
        play(times.force((layer_pieces[layer][1], 4), (bias_piece, 4)))
        keep[1].start()
        if layer == 0:
            spread_bias()
        middle_phase(layer)
        feed_phase(layer, keep)

    def finish_rows(item, carry):
        here = pl.ds(pl.multiple_of(item * LENGTH, LENGTH), LENGTH)
        rounded[here] = stream[here].astype(BF16)
        return carry

    lax.fori_loop(0, items, finish_rows, 0)
    last = pltpu.make_async_copy(rounded, act_out, act_sem)
    last.start()
    for entry in pieces:
        entry.finish()
    for copy in keeps + [last]:
        copy.wait()


ATTENTION, MIDDLE, FEED = 2.2, 0.8, 2.4
FEED_BACK, ATTENTION_BACK, GRAD = 1.9, 2.7, 0.76


class Start:
    def __init__(self, copy):
        self.copy = copy

    def step(self, number):
        self.copy.start()


def forward_call(rep, rows, steps, x, qkv, out, up, down, time, norm, bias):
    items = rows // LENGTH
    hbm = pl.BlockSpec(memory_space=pl.ANY)
    vmem = pl.BlockSpec(memory_space=pltpu.VMEM)
    smem = pl.BlockSpec(memory_space=pltpu.SMEM)
    shape = jax.ShapeDtypeStruct
    return pl.pallas_call(
        functools.partial(forward_kernel, rep),
        name="forward",
        in_specs=[smem, hbm] + [vmem] * 7,
        out_shape=[
            shape((LAYERS, 12, 2, 4, 4, 32, 256), BF16),
            shape((16, 512), F32),
            shape((8, 512), F32),
            shape((LAYERS, rows, 512), F32),
            shape((LAYERS, rows, 512), F32),
            shape((LAYERS, rows, 1536), BF16),
            shape((LAYERS, items, 8, 256, 256), BF16),
            shape((LAYERS, rows, 512), BF16),
            shape((LAYERS, rows, 2048), BF16),
            shape((LAYERS, rows, 2048), BF16),
            shape((rows, 512), BF16),
        ],
        out_specs=[hbm, vmem, vmem] + [hbm] * 8,
        scratch_shapes=[
            pltpu.VMEM((LAYERS, 12, 2, 4, 4, 32, 256), BF16),
            pltpu.VMEM((LAYERS, 2, 4, 4, 16, 512), BF16),
            pltpu.VMEM((2, 2, 4, 4, 16, 128), F32),
            pltpu.VMEM((16, 512), F32),
            pltpu.VMEM((LAYERS, 4, 8, 512), F32),
            pltpu.VMEM((16, 512), F32),
            pltpu.VMEM((rows, 512), F32),
            pltpu.VMEM((rows, 512), BF16),
            pltpu.VMEM((rows, 512), BF16),
            pltpu.VMEM((2, 16, 128), F32),
            pltpu.SemaphoreType.DMA((GATHER_PIECES, 8)),
            pltpu.SemaphoreType.DMA((GATHER_PIECES, 8)),
            pltpu.SemaphoreType.DMA((LAYERS, 6)),
            pltpu.SemaphoreType.DMA,
        ],
        compiler_params=pltpu.CompilerParams(collective_id=1, has_side_effects=True, vmem_limit_bytes=56 << 20),
    )(steps, x, qkv, out, up, down, time, norm, bias)


class Scatter(Exchange):
    slots = 10

    def __init__(self, place, grads, received, total, groups, send, recv):
        self.place, self.grads, self.received, self.total = place, grads, received, total
        self.first, self.count = groups
        self.span = pl.ds(*groups)
        self.send, self.recv = send, recv

    def copy(self, slot):
        p, span = self.place, self.span
        core, diag_y, diag_x, col_x, col_y, along = self.received
        low, high = pl.ds(0, 2), pl.ds(2, 2)
        to_x, to_y = p.device(p.z, p.yx_x, p.t), p.device(p.z, p.yx_y, p.t)
        if slot == 0:
            src, dst, device = self.grads.at[span, 1 - p.t], core.at[span], p.device(p.z, p.yx, 1 - p.t)
        elif slot == 1:
            src, dst, device = self.grads.at[span, p.t, low, p.yx_d], diag_y.at[span], to_y
        elif slot == 2:
            src, dst, device = self.grads.at[span, p.t, high, p.yx_d], diag_x.at[span], to_x
        elif slot == 3:
            src, dst, device = self.grads.at[span, p.t, low, p.yx_x], col_x.at[span, low], to_x
        elif slot == 4:
            src, dst, device = self.grads.at[span, p.t, high, p.yx_y], col_y.at[span, high], to_y
        elif slot == 5:
            src, dst, device = self.grads.at[span, p.t, high, p.yx_x], col_x.at[span, high], to_x
        elif slot == 6:
            src, dst, device = self.grads.at[span, p.t, low, p.yx_y], col_y.at[span, low], to_y
        else:
            there = p.z_ahead(slot - 6)
            src, dst, device = self.grads.at[span, p.t, there, p.yx], along.at[slot - 7, span], p.device(there, p.yx, p.t)
        return self.remote(slot, src, dst, device)

    def add(self, where, terms):
        def one(group, carry):
            ref = self.grads.at[(group, self.place.t) + where]
            value = ref[...].astype(F32)
            for term in terms:
                value = value + term[group].astype(F32)
            ref[...] = value.astype(BF16)
            return carry

        lax.fori_loop(self.first, self.first + self.count, one, 0)

    def step(self, number):
        p = self.place
        core, diag_y, diag_x, col_x, col_y, along = self.received
        every = slice(None)
        if number == 0:
            self.start(0)
        elif number == 1:
            self.arrived(0)
            self.add((every, every), [core])
            for slot in (1, 2, 5, 6):
                self.start(slot)
        elif number == 2:
            self.arrived(1)
            self.add((pl.ds(0, 2), p.yx_x), [diag_y])
            self.start(3)
            self.arrived(2)
            self.add((pl.ds(2, 2), p.yx_y), [diag_x])
            self.start(4)
        elif number == 3:
            self.arrived(3, 4, 5, 6)
            self.add((every, p.yx), [col_x, col_y])
            for slot in (7, 8, 9):
                self.start(slot)
        elif number == 4:
            self.arrived(7, 8, 9)

            def one(group, carry):
                value = self.grads[group, p.t, p.z, p.yx].astype(F32)
                for k in range(3):
                    value = value + along[k, group].astype(F32)
                self.total[group] = value
                return carry

            lax.fori_loop(self.first, self.first + self.count, one, 0)


class SmallSum(Exchange):
    slots = 6

    def __init__(self, place, sums, received, total, send, recv):
        self.place, self.sums, self.received, self.total = place, sums, received, total
        self.send, self.recv = send, recv

    def copy(self, slot):
        p = self.place
        if slot == 0:
            device = p.device(p.z, p.yx, 1 - p.t)
        elif slot < 3:
            device = p.device(p.z, p.yx_x if slot == 1 else p.yx_y, p.t)
        else:
            device = p.device(p.z_ahead(slot - 2), p.yx, p.t)
        return self.remote(slot, self.sums.at[min(slot, 3)], self.received.at[slot], device)

    def step(self, number):
        if number > 0:
            slots = (3, 4, 5) if number == 4 else (number - 1,)
            value = self.sums[number - 1]
            self.arrived(*slots)
            for slot in slots:
                value = value + self.received[slot]
            if number < 4:
                self.sums[number] = value
            else:
                self.total[...] = value
        if number < 3:
            self.start(number)
        elif number == 3:
            for slot in (3, 4, 5):
                self.start(slot)


GRAD_GROUPS = 13
SCATTER_PIECES = ((4, 2), (6, 2), (8, 2), (10, 2), (3, 1), (0, 1), (1, 1), (2, 1), (12, 1))


def backward_kernel(
    rep,
    scale_ref, small_ref, feats_ref, cot_ref, w_in, entry_in, middle_in, qkv_in, probs_in, attn_in, hidden_in, slope_in,
    grad_out, total_out, sums_out, time_out,
    w, gx, dattn, du, hidden, attn, n1t, n2t, gdt, got, dqkv, grads, item_grad, acc, acc_bias,
    r_core, r_dy, r_dx, r_x, r_y, r_z, sums, r_sums, r_time,
    w_sem, in_sem, send, recv, small_send, small_recv, time_send, time_recv,
):
    place = Place(rep)
    t = place.t
    rows = gx.shape[0]
    items = rows // LENGTH
    wide = lambda cols: pl.BlockSpec((LENGTH, cols), lambda i: (i, 0))
    lane = lax.broadcasted_iota(jnp.int32, (1, 128), 1)
    even_mask = jnp.where(lane < HEAD_DIM, 1.0, 0.0).astype(BF16)
    odd_mask = jnp.where(lane < HEAD_DIM, 0.0, 1.0).astype(BF16)
    times = Timeline()

    def load_weights(layer):
        copies = []
        for number, (first, count) in enumerate(((3, 9), (0, 3))):
            copy = pltpu.make_async_copy(
                w_in.at[layer, pl.ds(first, count)], w.at[pl.ds(first, count)], w_sem.at[layer, number]
            )
            copies.append(copy)
        return copies

    def load_stash(layer):
        return [
            pltpu.make_async_copy(hidden_in.at[layer], hidden, in_sem.at[layer, 0]),
            pltpu.make_async_copy(attn_in.at[layer], attn, in_sem.at[layer, 1]),
        ]

    def norm_back(hat, inverse, dy, layer, row, here):
        acc[row] += fold_rows(dy * hat)
        acc[row + 1] += fold_rows(dy)
        scaled = dy * small_ref[layer * 5 + row : layer * 5 + row + 1]
        mean = jnp.mean(scaled, -1, keepdims=True)
        along = jnp.mean(scaled * hat, -1, keepdims=True)
        return inverse * (scaled - mean - hat * along)

    def feed_phase(layer):
        last = layer == LAYERS - 1

        def body(item, poll, middle_blk, slope_blk, *rest):
            here = pl.ds(pl.multiple_of(item * LENGTH, LENGTH), LENGTH)
            if last:
                grad = rest[0][...].astype(F32) * scale_ref[t * items + item]
            else:
                grad = gx[here]
            acc[4] += fold_rows(grad)
            low = grad.astype(BF16)
            gdt[:, here] = low.T
            lift = lambda part: nn(low, weight(w, 5 + 2 * part))
            lower = lambda part, value: nt(value, weight(w, 4 + 2 * part))
            back, ahead, held = jnp.zeros((LENGTH, 512), F32), lift(0), None
            for part in range(4):
                span = slice(part * 512, (part + 1) * 512)
                dh = ahead
                if part == 2:
                    poll(1)
                if part < 3:
                    ahead = lift(part + 1)
                pre_grad = (dh * slope_blk[:, span].astype(F32)).astype(BF16)
                du[here, span] = pre_grad
                acc_bias[part] += fold_rows(pre_grad.astype(F32))
                if held is not None:
                    back = back + lower(part - 1, held)
                held = pre_grad
            back = back + lower(3, held)
            hat, inverse = normalize(middle_blk[...])
            normed = hat * small_ref[layer * 5 + 2 : layer * 5 + 3] + small_ref[layer * 5 + 3 : layer * 5 + 4]
            n2t[:, here] = normed.astype(BF16).T
            grad = grad + norm_back(hat, inverse, back, layer, 2, here)
            gx[here] = grad
            low = grad.astype(BF16)
            got[:, here] = low.T
            dattn[here] = nn(low, weight(w, 3)).astype(BF16)

        each_item(
            body, [[times.slot(FEED_BACK / 2) for _ in range(2)] for _ in range(items)], items, [wide(512), wide(2048)] + ([wide(512)] if last else []), [],
            [middle_in.at[layer], slope_in.at[layer]] + ([cot_ref] if last else []),
        )

    def attention_phase(layer):
        def body(item, poll, entry_blk, qkv_blk, probs_blk, *rest):
            here = pl.ds(pl.multiple_of(item * LENGTH, LENGTH), LENGTH)
            def sides(pair):
                query = qkv_blk[:, pair * 128 : (pair + 1) * 128]
                key = qkv_blk[:, 512 + pair * 128 : 512 + (pair + 1) * 128]
                value = qkv_blk[:, 1024 + pair * 128 : 1024 + (pair + 1) * 128]
                back = dattn[here, pair * 128 : (pair + 1) * 128]
                split = lambda v: [v * even_mask, v * odd_mask]
                return split(query), split(key), value, split(back)

            def scores(pair):
                _, _, value, back = sides(pair)
                return [nt(side, value) for side in back]

            def products(pair, dscores):
                query, key, _, back = sides(pair)
                probs = [probs_blk[0, pair * 2 + side] for side in range(2)]
                tall = jnp.concatenate(dscores, 0)
                dq = nn(jnp.concatenate(dscores, 1), jnp.concatenate(key, 0)) * HEAD_DIM**-0.5
                dk = tn(tall, jnp.concatenate(query, 0))
                dv = tn(jnp.concatenate(probs, 0), jnp.concatenate(back, 0))
                for slot, value in enumerate((dq, dk, dv)):
                    dqkv[here, slot * 512 + pair * 128 : slot * 512 + (pair + 1) * 128] = value.astype(BF16)

            ahead, held = scores(0), None
            for pair in range(4):
                both = ahead
                if pair > 0:
                    poll(pair)
                if pair < 3:
                    ahead = scores(pair + 1)
                dscores = []
                for side in range(2):
                    probs = probs_blk[0, pair * 2 + side].astype(F32)
                    mixed = probs * both[side]
                    dscores.append((mixed - probs * jnp.sum(mixed, -1, keepdims=True)).astype(BF16))
                if held is not None:
                    products(pair - 1, held)
                held = dscores
            products(3, held)
            back = jnp.zeros((LENGTH, 512), F32)
            for slot in range(3):
                back = back + nt(dqkv[here, slot * 512 : (slot + 1) * 512], weight(w, slot))
            hat, inverse = normalize(entry_blk[...])
            normed = hat * small_ref[layer * 5 : layer * 5 + 1] + small_ref[layer * 5 + 1 : layer * 5 + 2]
            n1t[:, here] = normed.astype(BF16).T
            grad = gx[here] + norm_back(hat, inverse, back, layer, 0, here)
            item_grad[pl.ds(item, 1)] = jnp.sum(grad, 0, keepdims=True)
            if layer == 0:
                rest[0][...] = grad.astype(BF16)
            else:
                gx[here] = grad

        slots = [[times.slot(ATTENTION_BACK / 4) for _ in range(4)] for _ in range(items)]
        each_item(
            body, slots, items,
            [wide(512), wide(1536), pl.BlockSpec((1, 8, 256, 256), lambda i: (i, 0, 0, 0))],
            [wide(512)] if layer == 0 else [],
            [entry_in.at[layer], qkv_in.at[layer], probs_in.at[layer]] + ([grad_out] if layer == 0 else []),
        )

    def keep_grad(group, value):
        for half in range(2):
            grads[group, half] = value[:, half * 256 : (half + 1) * 256].astype(BF16).reshape(4, 4, 32, 256)

    def weight_grad(left, right, group, part):
        keep_grad(group, nn(left[...], right[:, part * 512 : (part + 1) * 512]))

    scatters, smalls = [], []
    for layer in range(LAYERS):
        received = [r.at[layer] for r in (r_core, r_dy, r_dx, r_x, r_y, r_z)]
        scatters.append(
            [
                Scatter(place, grads, received, total_out.at[layer], groups, send.at[layer, i], recv.at[layer, i])
                for i, groups in enumerate(SCATTER_PIECES)
            ]
        )
        smalls.append(
            SmallSum(place, sums.at[layer], r_sums.at[layer], sums_out.at[layer], small_send.at[layer], small_recv.at[layer])
        )

    order = [LAYERS - 1 - i for i in range(LAYERS)]
    weights = {order[0]: load_weights(order[0])}
    stash = {order[0]: load_stash(order[0])}
    for copy in weights[order[0]] + stash[order[0]]:
        copy.start()
    item_grad[...] = jnp.zeros(item_grad.shape, F32)
    place.greet()

    def clear(layer, piece):
        if layer != order[0]:
            before = scatters[order[order.index(layer) - 1]][scatters[layer].index(piece)]
            play(times.force((before, 4)))
            before.finish()

    def begin(piece):
        piece.step(0)
        times.scatter(piece, UNIT * piece.count)

    for turn, layer in enumerate(order):
        feed_pieces, late_pieces = scatters[layer][:5], scatters[layer][5:]
        acc[...] = jnp.zeros(acc.shape, F32)
        acc_bias[...] = jnp.zeros(acc_bias.shape, F32)
        weights[layer][0].wait()
        feed_phase(layer)
        stash[layer][0].wait()
        stash[layer][1].wait()
        weights[layer][1].wait()
        for part, piece in enumerate(feed_pieces):
            clear(layer, piece)
            if part < 4:
                weight_grad(n2t, du, 4 + 2 * part, part)
                weight_grad(gdt, hidden, 5 + 2 * part, part)
            else:
                weight_grad(got, attn, 3, 0)
            times.passed(GRAD * piece.count)
            begin(piece)
            play(times.slot(0.0))
        attention_phase(layer)
        if turn + 1 < LAYERS:
            after = order[turn + 1]
            weights[after] = load_weights(after)
            stash[after] = load_stash(after)
            for copy in weights[after] + stash[after]:
                copy.start()
        for piece in late_pieces:
            clear(layer, piece)
        spread = lax.dot_general(
            feats_ref[...], item_grad[...], (((0,), (0,)), ((), ())),
            precision=lax.Precision.HIGHEST, preferred_element_type=F32,
        )
        keep_grad(12, spread)
        begin(late_pieces[3])
        for row in range(5):
            sums[layer, 0, row : row + 1] = jnp.sum(acc[row], 0, keepdims=True)
        for part in range(4):
            sums[layer, 0, 5 + part : 6 + part] = jnp.sum(acc_bias[part], 0, keepdims=True)
        sums[layer, 0, 9:16] = jnp.zeros((7, 512), F32)
        smalls[layer].step(0)
        times.small(smalls[layer])
        for slot in range(3):
            weight_grad(n1t, dqkv, slot, slot)
            times.passed(GRAD)
            begin(late_pieces[slot])
            play(times.slot(0.0))
    play(times.force(*[(piece, 4) for layer in range(LAYERS) for piece in scatters[layer] + [smalls[layer]]]))

    swaps = []
    for layer in range(LAYERS):
        swap = pltpu.make_async_remote_copy(
            src_ref=total_out.at[layer, 12, pl.ds(pl.multiple_of((1 - t) * 16, 16), 16)],
            dst_ref=r_time.at[layer], send_sem=time_send.at[layer], recv_sem=time_recv.at[layer],
            device_id=place.device(place.z, place.yx, 1 - t), device_id_type=MESH,
        )
        swap.start()
        swaps.append(swap)
    for layer in range(LAYERS):
        swaps[layer].wait()
        time_out[layer, :, place.cols] = total_out[layer, 12, pl.ds(pl.multiple_of(t * 16, 16), 16)]
        time_out[layer, :, place.other_cols] = r_time[layer]
    for piece in scatters[order[-1]]:
        piece.finish()
    for piece in smalls:
        piece.finish()


def backward_call(rep, rows, scale, small, feats, cot, w, entry, middle, qkv, probs, attn, hidden, slope):
    items = rows // LENGTH
    hbm = pl.BlockSpec(memory_space=pl.ANY)
    vmem = pl.BlockSpec(memory_space=pltpu.VMEM)
    smem = pl.BlockSpec(memory_space=pltpu.SMEM)
    shape = jax.ShapeDtypeStruct
    pieces = len(SCATTER_PIECES)
    dma = pltpu.SemaphoreType.DMA
    return pl.pallas_call(
        functools.partial(backward_kernel, rep),
        name="backward",
        in_specs=[smem, vmem, vmem] + [hbm] * 9,
        out_shape=[
            shape((rows, 512), BF16),
            shape((LAYERS, GRAD_GROUPS, 32, 256), F32),
            shape((LAYERS, 16, 512), F32),
            shape((LAYERS, 16, 512), F32),
        ],
        out_specs=[hbm, vmem, vmem, vmem],
        scratch_shapes=[
            pltpu.VMEM((12, 2, 4, 4, 32, 256), BF16),
            pltpu.VMEM((rows, 512), F32),
            pltpu.VMEM((rows, 512), BF16),
            pltpu.VMEM((rows, 2048), BF16),
            pltpu.VMEM((rows, 2048), BF16),
            pltpu.VMEM((rows, 512), BF16),
            pltpu.VMEM((512, rows), BF16),
            pltpu.VMEM((512, rows), BF16),
            pltpu.VMEM((512, rows), BF16),
            pltpu.VMEM((512, rows), BF16),
            pltpu.VMEM((rows, 1536), BF16),
            pltpu.VMEM((GRAD_GROUPS, 2, 4, 4, 32, 256), BF16),
            pltpu.VMEM((8, 512), F32),
            pltpu.VMEM((5, 8, 512), F32),
            pltpu.VMEM((4, 8, 512), F32),
            pltpu.VMEM((LAYERS, GRAD_GROUPS, 4, 4, 32, 256), BF16),
            pltpu.VMEM((LAYERS, GRAD_GROUPS, 2, 32, 256), BF16),
            pltpu.VMEM((LAYERS, GRAD_GROUPS, 2, 32, 256), BF16),
            pltpu.VMEM((LAYERS, GRAD_GROUPS, 4, 32, 256), BF16),
            pltpu.VMEM((LAYERS, GRAD_GROUPS, 4, 32, 256), BF16),
            pltpu.VMEM((LAYERS, 3, GRAD_GROUPS, 32, 256), BF16),
            pltpu.VMEM((LAYERS, 4, 16, 512), F32),
            pltpu.VMEM((LAYERS, 6, 16, 512), F32),
            pltpu.VMEM((LAYERS, 16, 256), F32),
            dma((LAYERS, 2)),
            dma((LAYERS, 2)),
            dma((LAYERS, pieces, 10)),
            dma((LAYERS, pieces, 10)),
            dma((LAYERS, 6)),
            dma((LAYERS, 6)),
            dma((LAYERS,)),
            dma((LAYERS,)),
        ],
        compiler_params=pltpu.CompilerParams(collective_id=2, has_side_effects=True, vmem_limit_bytes=62 << 20),
    )(scale, small, feats, cot, w, entry, middle, qkv, probs, attn, hidden, slope)


def adamw(weight, gradient, first_moment, second_moment, rate):
    first_new = beta_first * first_moment + (1.0 - beta_first) * gradient
    second_new = beta_second * second_moment + (1.0 - beta_second) * gradient * gradient
    first_corr = first_new * (1.0 / (1.0 - beta_first**STEP))
    second_corr = second_new * (1.0 / (1.0 - beta_second**STEP))
    weight_new = weight - rate * (first_corr / (jnp.sqrt(second_corr) + adam_eps) + weight_decay * weight)
    return (weight_new, first_new, second_new)


def update_kernel(*refs):
    hbm, outs, ins = refs[:26], refs[26:50], refs[50:74]
    row, sems = refs[74:]
    copies = [pltpu.make_async_copy(src, dst, sems.at[i]) for i, (src, dst) in enumerate(zip(hbm[:24], ins))]
    copies += [pltpu.make_async_copy(hbm[24 + i], outs[i], sems.at[24 + i]) for i in range(2)]
    for copy in copies:
        copy.start()
    for copy in copies[:24]:
        copy.wait()
    total, sums, time_grad, *ins = ins
    outs = outs[2:]
    qkv, out, up, bias, down, norm, time = [ins[i * 3 : i * 3 + 3] for i in range(7)]
    qkv_new, key_second, value_second = outs[0:2], outs[2], outs[3]
    out_new, up_new, bias_new, down_new, norm_new, time_new = [outs[4 + i * 3 : 7 + i * 3] for i in range(6)]
    dp, t = lax.axis_index("dp"), lax.axis_index("tensor")

    def one(old, new, where, gradient, rate):
        values = adamw(old[0][where], gradient, old[1][where], old[2][where], rate)
        for ref, value in zip(new, values):
            ref[where] = value
        return values

    for layer in range(LAYERS):
        for slot in range(3):
            values = adamw(qkv[0][layer, slot], total[layer, slot], qkv[1][layer, slot], qkv[2][layer, slot], learn_rate)
            for ref, value in zip(qkv_new, values):
                ref[layer, slot] = value
            if slot < 2:
                key_second[layer, :, slot] = values[2]
            else:
                value_second[layer] = values[2]
        one(out, out_new, (layer,), total[layer, 3], learn_rate)
        for part in range(4):
            where = (layer, slice(None), slice(part * 256, (part + 1) * 256))
            one(up, up_new, where, total[layer, 4 + 2 * part], learn_rate)
            one(down, down_new, where, total[layer, 5 + 2 * part], learn_rate)
        one(time, time_new, (layer,), time_grad[layer], learn_rate)

        width = norm[0].shape[2]
        start = (dp * 2 + t) * width
        tile = sums[layer, :, pl.ds(pl.multiple_of(start // 128 * 128, 128), 128)]
        mine = pltpu.roll(tile, (128 - start % 128) % 128, 1)[0:5, 0:width]
        one(norm, norm_new, (slice(None), layer), mine, norm_rate)
        for part in range(4):
            for half in range(2):
                span = pl.ds(pl.multiple_of(t * 256 + half * 128, 128), 128)
                row[part * 2 + half : part * 2 + half + 1] = sums[layer, 5 + part : 6 + part, span]
        width = bias[0].shape[2]
        mine = pltpu.roll(row[...], (128 - dp * width) % 128, 1)[:, 0:width]
        one(bias, bias_new, (layer,), mine, learn_rate)
    for copy in copies[24:]:
        copy.wait()


def update_call(total, sums, time_grad, states, row_results):
    flat = [total, sums, time_grad] + [array for state in states for array in state]
    like = lambda array: jax.ShapeDtypeStruct(array.shape, array.dtype)
    rows = states[0][0].shape[2]
    shapes = [like(array) for array in list(row_results) + flat[3:]]
    shapes[4:5] = [
        jax.ShapeDtypeStruct((LAYERS, rows, 2, 256), F32),
        jax.ShapeDtypeStruct((LAYERS, rows, 256), F32),
    ]
    vmem = pl.BlockSpec(memory_space=pltpu.VMEM)
    hbm = pl.BlockSpec(memory_space=pl.ANY)
    return pl.pallas_call(
        update_kernel,
        name="update",
        in_specs=[hbm] * 26,
        out_shape=shapes,
        out_specs=[vmem] * 24,
        scratch_shapes=[pltpu.VMEM(array.shape, F32) for array in flat]
        + [pltpu.VMEM((8, 128), F32), pltpu.SemaphoreType.DMA((26,))],
        compiler_params=pltpu.CompilerParams(vmem_limit_bytes=56 << 20),
    )(*flat, *row_results)


def per_device(
    rep,
    inputs, cotangent, timesteps, item_scale,
    qkv_weight, qkv_first, qkv_second,
    out_weight, out_first, out_second,
    up_weight, up_first, up_second,
    up_bias, bias_first, bias_second,
    down_weight, down_first, down_second,
    norm_params, norm_first, norm_second,
    time_weight, time_first, time_second,
):
    rows = inputs.shape[0]
    dp, t = lax.axis_index("dp"), lax.axis_index("tensor")
    qkv, out, up, down, bias = qkv_weight, out_weight, up_weight, down_weight, up_bias
    norm, time = norm_params, time_weight
    teams = None
    if rep > 1:
        size = GROUPS * rep
        teams = [[g * rep + j for j in range(rep)] for g in range(GROUPS)]
        pairs = [[g * rep * 2 + j for j in range(rep * 2)] for g in range(GROUPS)]
        join = lambda v, axis: lax.all_gather(v, "dp", axis=axis, axis_index_groups=teams, tiled=True)
        join_both = lambda v, axis: lax.all_gather(
            v, ("dp", "tensor"), axis=axis, axis_index_groups=pairs, tiled=True
        )
        qkv, out, up, down, bias = join(qkv, 1), join(out, 2), join(up, 1), join(down, 2), join(bias, 2)
        norm, time = join_both(norm, 2), join_both(time, 1)
        norm = lax.dynamic_slice_in_dim(norm, t * 16, 16, 2)
        time = lax.dynamic_slice_in_dim(time, t * 16, 16, 1)

    slots = lambda *arrays: [jnp.transpose(v, (0, 2, 1, 3)) for v in arrays]
    flip = lambda *arrays: [jnp.swapaxes(v, 1, 2) for v in arrays]
    front = lambda *arrays: [jnp.swapaxes(v, 0, 1) for v in arrays]
    w, small, feats, entry, middle, qkv_rows, probs, attn, hidden, slope, activations = forward_call(
        rep, rows, timesteps, inputs, *slots(qkv), *flip(out), up, *flip(down), time, *front(norm), bias
    )
    input_grad, total, sums, time_grad = backward_call(
        rep, rows, item_scale, small, feats, cotangent, w, entry, middle, qkv_rows, probs, attn, hidden, slope
    )

    if rep > 1:
        total = lax.psum_scatter(total, "dp", scatter_dimension=2, axis_index_groups=teams, tiled=True)
        sums, time_grad = lax.psum((sums, time_grad), "dp", axis_index_groups=teams)
        time_grad = lax.all_gather(time_grad, "tensor", axis=1, tiled=True)
        width = time_weight.shape[1]
        time_grad = lax.dynamic_slice_in_dim(time_grad, ((dp % rep) * 2 + t) * width, width, 1)

    activations, input_grad, *new = update_call(
        total, sums, time_grad,
        [
            slots(qkv_weight, qkv_first, qkv_second),
            flip(out_weight, out_first, out_second),
            [up_weight, up_first, up_second],
            [up_bias, bias_first, bias_second],
            flip(down_weight, down_first, down_second),
            front(norm_params, norm_first, norm_second),
            [time_weight, time_first, time_second],
        ],
        (activations, input_grad),
    )
    return (
        activations, input_grad,
        *slots(*new[0:2]), new[2], new[3],
        *flip(*new[4:7]), *new[7:10], *new[10:13], *flip(*new[13:16]), *front(*new[16:19]), *new[19:22],
    )


def solution(mesh):
    rep = mesh.shape["dp"] // GROUPS
    shard = P(None, "dp", None, "tensor")
    rows = P(("dp", "tensor"), None)
    trans = P(None, "tensor", "dp")
    flat = P(None, "dp", "tensor")
    norm = P(None, None, ("dp", "tensor"))
    time = P(None, ("dp", "tensor"), None)
    return jax.shard_map(
        functools.partial(per_device, rep),
        mesh=mesh,
        in_specs=(rows, rows, P("dp"), P("dp")) + (shard,) * 3 + (trans,) * 3 + (flat,) * 3 + (trans,) * 6 + (norm,) * 3 + (time,) * 3,
        out_specs=(rows, rows, shard, shard, shard, flat) + (trans,) * 3 + (flat,) * 3 + (trans,) * 6 + (norm,) * 3 + (time,) * 3,
        check_vma=False,
    )
```

```python
import functools
import math

import jax
import jax.numpy as jnp
from jax import lax
from jax.experimental import pallas as pl
from jax.experimental.pallas import tpu as pltpu
from jax.sharding import PartitionSpec as P

HEAD_DIM = 64
LENGTH = 256
LAYERS = 2
STEP = 8
GROUPS = 16
MESH = pl.DeviceIdType.MESH
F32 = jnp.float32
BF16 = jnp.bfloat16

beta_first = 0.5
beta_second = 0.5
learn_rate = 0.1
norm_rate = 0.4
weight_decay = 0.01
adam_eps = 1e-08
norm_eps = 1e-05


def nn(a, b):
    return lax.dot_general(a, b, (((1,), (0,)), ((), ())), preferred_element_type=F32)


def nt(a, b):
    return lax.dot_general(a, b, (((1,), (1,)), ((), ())), preferred_element_type=F32)


def tn(a, b):
    return lax.dot_general(a, b, (((0,), (0,)), ((), ())), preferred_element_type=F32)


def normalize(values):
    center = values - jnp.mean(values, -1, keepdims=True)
    inverse = lax.rsqrt(jnp.mean(center * center, -1, keepdims=True) + norm_eps)
    return center * inverse, inverse


def fold_rows(values):
    rows, cols = values.shape
    return jnp.sum(values.reshape(rows // 8, 8, cols), 0)


def gelu_and_slope(x):
    below = 0.5 + 0.5 * lax.erf(x * math.sqrt(0.5))
    return x * below, below + x * (jnp.exp(x * x * -0.5) * (1.0 / math.sqrt(2.0 * math.pi)))


class Place:
    def __init__(self, rep):
        dp = lax.axis_index("dp")
        self.rep = rep
        self.copy = dp % rep
        self.group = dp // rep
        self.t = lax.axis_index("tensor")
        self.z = self.group // 4
        self.yx = self.group % 4
        x, y = self.yx % 2, self.yx // 2
        self.yx_x = self.yx + 1 - 2 * x
        self.yx_y = self.yx + 2 - 4 * y
        self.yx_d = 3 - self.yx
        self.cols = pl.ds(pl.multiple_of(self.t * 256, 256), 256)
        self.other_cols = pl.ds(pl.multiple_of((1 - self.t) * 256, 256), 256)

    def device(self, z, yx, t):
        return ((z * 4 + yx) * self.rep + self.copy, t)

    def z_ahead(self, k):
        return (self.z + k) % 4

    @property
    def partners(self):
        return [self.device(self.z_ahead(k), self.yx, self.t) for k in (1, 2, 3)] + [
            self.device(self.z, self.yx_x, self.t),
            self.device(self.z, self.yx_y, self.t),
            self.device(self.z, self.yx, 1 - self.t),
        ]

    def greet(self):
        barrier = pltpu.get_barrier_semaphore()
        for partner in self.partners:
            pl.semaphore_signal(barrier, inc=1, device_id=partner, device_id_type=MESH)
        pl.semaphore_wait(barrier, len(self.partners))


class Exchange:
    def start(self, slot):
        self.copy(slot).start()

    def arrived(self, *slots):
        for slot in slots:
            self.copy(slot).wait_recv()

    def finish(self):
        for slot in range(self.slots):
            self.copy(slot).wait_send()

    def remote(self, slot, src, dst, device):
        return pltpu.make_async_remote_copy(
            src_ref=src, dst_ref=dst, send_sem=self.send.at[slot], recv_sem=self.recv.at[slot],
            device_id=device, device_id_type=MESH,
        )


class Gather(Exchange):
    slots = 8

    def __init__(self, place, view, core_view, send, recv):
        self.place, self.view, self.core_view, self.send, self.recv = place, view, core_view, send, recv

    def copy(self, slot):
        p = self.place
        if slot < 3:
            ref, device = self.view(p.z, p.yx), p.device(p.z_ahead(slot + 1), p.yx, p.t)
        elif slot < 5:
            ref, device = self.view(slice(None), p.yx), p.device(p.z, p.yx_x if slot == 3 else p.yx_y, p.t)
        elif slot == 5:
            ref, device = self.view(pl.ds(0, 2), p.yx_x), p.device(p.z, p.yx_y, p.t)
        elif slot == 6:
            ref, device = self.view(pl.ds(2, 2), p.yx_y), p.device(p.z, p.yx_x, p.t)
        else:
            ref, device = self.core_view(), p.device(p.z, p.yx, 1 - p.t)
        return self.remote(slot, ref, ref, device)

    def step(self, number):
        if number == 0:
            for slot in (0, 1, 2):
                self.start(slot)
        elif number == 1:
            self.arrived(0, 1, 2)
            self.start(3)
            self.start(4)
        elif number == 2:
            self.arrived(3)
            self.start(5)
            self.arrived(4)
            self.start(6)
        elif number == 3:
            self.arrived(5, 6)
            self.start(7)
        elif number == 4:
            self.arrived(7)


def play(events):
    for piece, number in events:
        piece.step(number)


class Timeline:
    def __init__(self):
        self.now = 0.0
        self.queue = []
        self.links = 0.0
        self.along = 0.0
        self.count = 0

    def push(self, piece, dues, turns):
        for number, (due, turn) in enumerate(zip(dues, turns), 1):
            self.queue.append((self.count + turn, due, number, piece))
        self.queue.sort(key=lambda event: event[0])
        self.count += 1

    def gather(self, piece, unit):
        self.along += 4 * unit
        arrived = self.along + GATHER_WAIT
        begun = max(self.links, arrived)
        self.links = begun + 6 * unit
        columns, diagonal = begun + 4 * unit + GATHER_WAIT, begun + 6 * unit + GATHER_WAIT
        self.push(piece, [max(arrived, begun - LEAD), columns, diagonal, diagonal + 1.6 * unit + GATHER_WAIT], GATHER_TURNS)

    def scatter(self, piece, unit):
        added = self.now + 1.6 * unit + WAIT
        begun = max(self.links, added)
        self.links = begun + 6 * unit
        summed = begun + 8 * unit + WAIT
        self.along = max(self.along, summed) + 4 * unit
        self.push(piece, [max(added, begun - LEAD), begun + 4 * unit + WAIT, summed, self.along + WAIT], SCATTER_TURNS)

    def small(self, piece):
        self.push(piece, [self.now + 3.0 * number for number in (1, 2, 3, 4)], SCATTER_TURNS)

    def take(self, count):
        ready, self.queue = self.queue[:count], self.queue[count:]
        return [(piece, number) for _, _, number, piece in ready]

    def slot(self, length):
        count = 0
        while count < len(self.queue) and self.queue[count][1] <= self.now:
            count += 1
        self.now += length + COST * count
        return self.take(count)

    def passed(self, length):
        self.now += length

    def force(self, *wanted):
        count = max([i + 1 for i, event in enumerate(self.queue) if (event[3], event[2]) in wanted], default=0)
        self.now = max([self.now] + [event[1] for event in self.queue[:count]])
        return self.take(count)


WAIT = 5.0
GATHER_WAIT = 3.0
LEAD = 2.0
GATHER_TURNS = (-1.9, 0.0, 1.05, 2.3)
SCATTER_TURNS = (0.0, 1.1, 3.2, 5.3)
COST = 0.2
UNIT = 0.33


def each_item(body, slots, count, in_specs, out_specs, refs):
    def whole(*blocks):
        item = pl.program_id(0)

        def poll(half):
            for number, events in enumerate(slots):
                if events[half]:
                    pl.when(item == number)(functools.partial(play, events[half]))

        poll(0)
        body(item, poll, *blocks)

    pltpu.emit_pipeline(whole, grid=(count,), in_specs=in_specs, out_specs=out_specs)(*refs)


GATHER_PIECES = 16


def weight(ref, group):
    return jnp.concatenate([ref[group, 0].reshape(512, 256), ref[group, 1].reshape(512, 256)], 1)


def forward_kernel(
    rep,
    steps_ref, x_ref, qkv_ref, out_ref, up_ref, down_ref, time_ref, norm_ref, bias_ref,
    w_out, small_out, feats_out, entry_out, middle_out, qkv_out, probs_out, attn_out, hidden_out, slope_out, act_out,
    w, tw, nb, norms, bias, shifts, stream, attn, rounded, tile, send, recv, keep_sem, act_sem,
):
    place = Place(rep)
    z, yx, t = place.z, place.yx, place.t
    rows = stream.shape[0]
    items = rows // LENGTH

    pieces = []

    def piece(ref, *lead):
        number = len(pieces)
        pieces.append(
            Gather(
                place,
                lambda a, b: ref.at[(*lead, t, a, b)],
                lambda: ref.at[(*lead, t)],
                send.at[number],
                recv.at[number],
            )
        )
        return pieces[-1]

    norm_piece, bias_piece = piece(nb, 0), piece(nb, 1)
    time_pieces = [piece(tw, layer) for layer in range(LAYERS)]
    spans = ((0, 3), (3, 1), (4, 2), (6, 2), (8, 2), (10, 2))
    layer_pieces = [[piece(w, layer, pl.ds(*span)) for span in spans] for layer in range(LAYERS)]

    tile[...] = jnp.zeros(tile.shape, F32)
    for layer in range(LAYERS):
        for row in range(5):
            at = layer * 5 + row
            tile[0, at : at + 1, 0:16] = norm_ref[row, layer : layer + 1]
        tile[1, layer * 8 : (layer + 1) * 8, 0:8] = bias_ref[layer]
    nb[0, t, z, yx] = pltpu.roll(tile[0], (yx * 2 + t) * 16, 1)
    nb[1, t, z, yx] = pltpu.roll(tile[1], place.group * 8, 1)

    def own_attention(layer):
        tw[layer, t, z, yx] = time_ref[layer].astype(BF16)
        for slot in range(3):
            w[layer, slot, t, z, yx] = qkv_ref[layer, slot].astype(BF16)

    def own_feed(layer):
        w[layer, 3, t, z, yx] = out_ref[layer].astype(BF16)
        for part in range(4):
            own = slice(part * 256, (part + 1) * 256)
            w[layer, 4 + 2 * part, t, z, yx] = up_ref[layer, :, own].astype(BF16)
            w[layer, 5 + 2 * part, t, z, yx] = down_ref[layer, :, own].astype(BF16)

    own_attention(0)
    place.greet()
    opening = [norm_piece, time_pieces[0], layer_pieces[0][0]]
    rest = [layer_pieces[0][1], bias_piece] + layer_pieces[0][2:] + [time_pieces[1]] + layer_pieces[1]
    for entry in opening:
        entry.step(0)
    own_feed(0)
    own_attention(1)
    own_feed(1)
    for entry in rest:
        entry.step(0)
    sizes = {norm_piece: 0.25, bias_piece: 0.25}
    for layer in range(LAYERS):
        sizes[time_pieces[layer]] = 2
        sizes.update((entry, span[1]) for entry, span in zip(layer_pieces[layer], spans))
    times = Timeline()
    for entry in opening + rest:
        times.gather(entry, UNIT * sizes[entry])
    wanted = [(entry, 4) for entry in opening]
    play(times.force(*[(entry, 3) for entry in opening]))

    line = lax.broadcasted_iota(jnp.int32, (8, 256), 0)
    column = lax.broadcasted_iota(jnp.int32, (8, 256), 1).astype(F32)
    angles = jnp.zeros((8, 256), F32)
    for item in range(items):
        angles = jnp.where(line == item, steps_ref[t * items + item].astype(F32), angles)
    angles = angles * jnp.exp(column * (-math.log(10000.0) / 256))
    live = line < items
    feats = jnp.concatenate(
        [jnp.where(live, jnp.sin(angles), 0.0), jnp.where(live, jnp.cos(angles), 0.0)], 1
    )
    feats_out[...] = feats
    feats_high = feats.astype(BF16)
    feats_low = (feats - feats_high.astype(F32)).astype(BF16)

    play(times.force(*wanted))
    for zz in range(4):
        total = jnp.zeros((16, 128), F32)
        for part in range(8):
            total = total + nb[0, part % 2, zz, part // 2]
        norms[:, zz * 128 : (zz + 1) * 128] = total
    small_out[...] = norms[...]

    def spread_times(layer):
        table = [tw[layer, core].reshape(GROUPS, 16, 512) for core in range(2)]
        table = jnp.concatenate([table[0][:, None], table[1][:, None]], 1).reshape(512, 512)
        shifts[layer * 8 : (layer + 1) * 8] = nn(feats_high, table) + nn(feats_low, table)

    def spread_bias():
        for core in range(2):
            total = jnp.zeros((16, 128), F32)
            for part in range(16):
                total = total + nb[1, core, part // 4, part % 4]
            total = total.astype(BF16).astype(F32)
            for layer in range(LAYERS):
                for part in range(4):
                    for half in range(2):
                        row = layer * 8 + part * 2 + half
                        col = core * 256 + half * 128
                        bias[layer, part, 0:1, col : col + 128] = total[row : row + 1]

    lane = lax.broadcasted_iota(jnp.int32, (1, 128), 1)
    even_mask = jnp.where(lane < HEAD_DIM, 1.0, 0.0).astype(BF16)
    odd_mask = jnp.where(lane < HEAD_DIM, 0.0, 1.0).astype(BF16)
    wide = lambda cols: pl.BlockSpec((LENGTH, cols), lambda i: (i, 0))

    def attention_phase(layer):
        def body(item, poll, *refs):
            if layer == 0:
                x_blk, *refs = refs
            entry_blk, qkv_blk, probs_blk, attn_blk = refs
            here = pl.ds(pl.multiple_of(item * LENGTH, LENGTH), LENGTH)
            start = x_blk[...].astype(F32) if layer == 0 else stream[here]
            entry = start + shifts[pl.ds(layer * 8 + item, 1)]
            entry_blk[...] = entry
            stream[here] = entry
            hat, _ = normalize(entry)
            normed = (hat * norms[layer * 5 : layer * 5 + 1] + norms[layer * 5 + 1 : layer * 5 + 2]).astype(BF16)
            for slot in range(3):
                projected = nn(normed, weight(w.at[layer], slot)).astype(BF16)
                if slot == 0:
                    projected = projected * jnp.asarray(HEAD_DIM**-0.5, BF16)
                qkv_blk[:, slot * 512 : (slot + 1) * 512] = projected

            def scores(pair):
                query = qkv_blk[:, pair * 128 : (pair + 1) * 128]
                key = qkv_blk[:, 512 + pair * 128 : 512 + (pair + 1) * 128]
                return [nt(query * mask, key) for mask in (even_mask, odd_mask)]

            ahead = scores(0)
            for pair in range(4):
                both = ahead
                if pair < 3:
                    ahead = scores(pair + 1)
                span = slice(pair * 128, (pair + 1) * 128)
                value = qkv_blk[:, 1024 + pair * 128 : 1024 + (pair + 1) * 128]
                probs = []
                for side in range(2):
                    raised = jnp.exp(both[side] - jnp.max(both[side], -1, keepdims=True))
                    probs.append((raised * (1.0 / jnp.sum(raised, -1, keepdims=True))).astype(BF16))
                    probs_blk[0, pair * 2 + side] = probs[side]
                values = jnp.concatenate([value * even_mask, value * odd_mask], 0)
                joined = nn(jnp.concatenate(probs, 1), values).astype(BF16)
                attn_blk[:, span] = joined
                attn[here, span] = joined

        each_item(
            body, [(times.slot(ATTENTION),) for _ in range(items)], items,
            [wide(512)] if layer == 0 else [],
            [wide(512), wide(1536), pl.BlockSpec((1, 8, 256, 256), lambda i: (i, 0, 0, 0)), wide(512)],
            ([x_ref] if layer == 0 else [])
            + [entry_out.at[layer], qkv_out.at[layer], probs_out.at[layer], attn_out.at[layer]],
        )

    def middle_phase(layer):
        def body(item, poll, middle_blk):
            here = pl.ds(pl.multiple_of(item * LENGTH, LENGTH), LENGTH)
            middle = stream[here] + nt(attn[here], weight(w.at[layer], 3))
            middle_blk[...] = middle
            hat, _ = normalize(middle)
            normed = hat * norms[layer * 5 + 2 : layer * 5 + 3] + norms[layer * 5 + 3 : layer * 5 + 4]
            rounded[here] = normed.astype(BF16)
            stream[here] = middle + norms[layer * 5 + 4 : layer * 5 + 5]

        slots = [(times.slot(MIDDLE), []) for _ in range(items)]
        each_item(body, slots, items, [], [wide(512)], [middle_out.at[layer]])

    def feed_phase(layer, keep):
        def body(part, poll, hidden_blk, slope_blk):
            blocks = [slice(i * LENGTH, (i + 1) * LENGTH) for i in range(items)]
            up, down, shift = weight(w.at[layer], 4 + 2 * part), weight(w.at[layer], 5 + 2 * part), bias[layer, part]
            lift = lambda i: nn(rounded[blocks[i]], up) + shift[0:1]

            def lower(i, hidden):
                stream[blocks[i]] += nt(hidden, down)

            ahead, held = lift(0), None
            for i in range(items):
                pre = ahead
                if i + 1 < items:
                    ahead = lift(i + 1)
                hidden, slope = gelu_and_slope(pre)
                if held is not None:
                    lower(i - 1, held)
                held = hidden.astype(BF16)
                hidden_blk[blocks[i]] = held
                slope_blk[blocks[i]] = slope.astype(BF16)
            lower(items - 1, held)

        slots = []
        for part in range(4):
            entry = layer_pieces[layer][2 + part]
            slots.append((times.force((entry, 4)) + [(Start(keep[2 + part]), 0)], []))
            times.passed(FEED)
        tall = pl.BlockSpec((rows, 512), lambda i: (0, i))
        each_item(body, slots, 4, [], [tall, tall], [hidden_out.at[layer], slope_out.at[layer]])

    spread_times(0)
    keeps = []
    for layer in range(LAYERS):
        keep = [
            pltpu.make_async_copy(w.at[layer, pl.ds(*span)], w_out.at[layer, pl.ds(*span)], keep_sem.at[layer, i])
            for i, span in enumerate(spans)
        ]
        keeps += keep
        if layer > 0:
            play(times.force((time_pieces[layer], 4), (layer_pieces[layer][0], 4)))
            spread_times(layer)
        keep[0].start()
        attention_phase(layer)
        play(times.force((layer_pieces[layer][1], 4), (bias_piece, 4)))
        keep[1].start()
        if layer == 0:
            spread_bias()
        middle_phase(layer)
        feed_phase(layer, keep)

    def finish_rows(item, carry):
        here = pl.ds(pl.multiple_of(item * LENGTH, LENGTH), LENGTH)
        rounded[here] = stream[here].astype(BF16)
        return carry

    lax.fori_loop(0, items, finish_rows, 0)
    last = pltpu.make_async_copy(rounded, act_out, act_sem)
    last.start()
    for entry in pieces:
        entry.finish()
    for copy in keeps + [last]:
        copy.wait()


ATTENTION, MIDDLE, FEED = 2.2, 0.8, 2.4
FEED_BACK, ATTENTION_BACK, GRAD = 1.9, 2.7, 0.76


class Start:
    def __init__(self, copy):
        self.copy = copy

    def step(self, number):
        self.copy.start()


def forward_call(rep, rows, steps, x, qkv, out, up, down, time, norm, bias):
    items = rows // LENGTH
    hbm = pl.BlockSpec(memory_space=pl.ANY)
    vmem = pl.BlockSpec(memory_space=pltpu.VMEM)
    smem = pl.BlockSpec(memory_space=pltpu.SMEM)
    shape = jax.ShapeDtypeStruct
    return pl.pallas_call(
        functools.partial(forward_kernel, rep),
        name="forward",
        in_specs=[smem, hbm] + [vmem] * 7,
        out_shape=[
            shape((LAYERS, 12, 2, 4, 4, 32, 256), BF16),
            shape((16, 512), F32),
            shape((8, 512), F32),
            shape((LAYERS, rows, 512), F32),
            shape((LAYERS, rows, 512), F32),
            shape((LAYERS, rows, 1536), BF16),
            shape((LAYERS, items, 8, 256, 256), BF16),
            shape((LAYERS, rows, 512), BF16),
            shape((LAYERS, rows, 2048), BF16),
            shape((LAYERS, rows, 2048), BF16),
            shape((rows, 512), BF16),
        ],
        out_specs=[hbm, vmem, vmem] + [hbm] * 8,
        scratch_shapes=[
            pltpu.VMEM((LAYERS, 12, 2, 4, 4, 32, 256), BF16),
            pltpu.VMEM((LAYERS, 2, 4, 4, 16, 512), BF16),
            pltpu.VMEM((2, 2, 4, 4, 16, 128), F32),
            pltpu.VMEM((16, 512), F32),
            pltpu.VMEM((LAYERS, 4, 8, 512), F32),
            pltpu.VMEM((16, 512), F32),
            pltpu.VMEM((rows, 512), F32),
            pltpu.VMEM((rows, 512), BF16),
            pltpu.VMEM((rows, 512), BF16),
            pltpu.VMEM((2, 16, 128), F32),
            pltpu.SemaphoreType.DMA((GATHER_PIECES, 8)),
            pltpu.SemaphoreType.DMA((GATHER_PIECES, 8)),
            pltpu.SemaphoreType.DMA((LAYERS, 6)),
            pltpu.SemaphoreType.DMA,
        ],
        compiler_params=pltpu.CompilerParams(collective_id=1, has_side_effects=True, vmem_limit_bytes=56 << 20),
    )(steps, x, qkv, out, up, down, time, norm, bias)


class Scatter(Exchange):
    slots = 10

    def __init__(self, place, grads, received, total, groups, send, recv):
        self.place, self.grads, self.received, self.total = place, grads, received, total
        self.first, self.count = groups
        self.span = pl.ds(*groups)
        self.send, self.recv = send, recv

    def copy(self, slot):
        p, span = self.place, self.span
        core, diag_y, diag_x, col_x, col_y, along = self.received
        low, high = pl.ds(0, 2), pl.ds(2, 2)
        to_x, to_y = p.device(p.z, p.yx_x, p.t), p.device(p.z, p.yx_y, p.t)
        if slot == 0:
            src, dst, device = self.grads.at[span, 1 - p.t], core.at[span], p.device(p.z, p.yx, 1 - p.t)
        elif slot == 1:
            src, dst, device = self.grads.at[span, p.t, low, p.yx_d], diag_y.at[span], to_y
        elif slot == 2:
            src, dst, device = self.grads.at[span, p.t, high, p.yx_d], diag_x.at[span], to_x
        elif slot == 3:
            src, dst, device = self.grads.at[span, p.t, low, p.yx_x], col_x.at[span, low], to_x
        elif slot == 4:
            src, dst, device = self.grads.at[span, p.t, high, p.yx_y], col_y.at[span, high], to_y
        elif slot == 5:
            src, dst, device = self.grads.at[span, p.t, high, p.yx_x], col_x.at[span, high], to_x
        elif slot == 6:
            src, dst, device = self.grads.at[span, p.t, low, p.yx_y], col_y.at[span, low], to_y
        else:
            there = p.z_ahead(slot - 6)
            src, dst, device = self.grads.at[span, p.t, there, p.yx], along.at[slot - 7, span], p.device(there, p.yx, p.t)
        return self.remote(slot, src, dst, device)

    def add(self, where, terms):
        def one(group, carry):
            ref = self.grads.at[(group, self.place.t) + where]
            value = ref[...].astype(F32)
            for term in terms:
                value = value + term[group].astype(F32)
            ref[...] = value.astype(BF16)
            return carry

        lax.fori_loop(self.first, self.first + self.count, one, 0)

    def step(self, number):
        p = self.place
        core, diag_y, diag_x, col_x, col_y, along = self.received
        every = slice(None)
        if number == 0:
            self.start(0)
        elif number == 1:
            self.arrived(0)
            self.add((every, every), [core])
            for slot in (1, 2, 5, 6):
                self.start(slot)
        elif number == 2:
            self.arrived(1)
            self.add((pl.ds(0, 2), p.yx_x), [diag_y])
            self.start(3)
            self.arrived(2)
            self.add((pl.ds(2, 2), p.yx_y), [diag_x])
            self.start(4)
        elif number == 3:
            self.arrived(3, 4, 5, 6)
            self.add((every, p.yx), [col_x, col_y])
            for slot in (7, 8, 9):
                self.start(slot)
        elif number == 4:
            self.arrived(7, 8, 9)

            def one(group, carry):
                value = self.grads[group, p.t, p.z, p.yx].astype(F32)
                for k in range(3):
                    value = value + along[k, group].astype(F32)
                self.total[group] = value
                return carry

            lax.fori_loop(self.first, self.first + self.count, one, 0)


class SmallSum(Exchange):
    slots = 6

    def __init__(self, place, sums, received, total, send, recv):
        self.place, self.sums, self.received, self.total = place, sums, received, total
        self.send, self.recv = send, recv

    def copy(self, slot):
        p = self.place
        if slot == 0:
            device = p.device(p.z, p.yx, 1 - p.t)
        elif slot < 3:
            device = p.device(p.z, p.yx_x if slot == 1 else p.yx_y, p.t)
        else:
            device = p.device(p.z_ahead(slot - 2), p.yx, p.t)
        return self.remote(slot, self.sums.at[min(slot, 3)], self.received.at[slot], device)

    def step(self, number):
        if number > 0:
            slots = (3, 4, 5) if number == 4 else (number - 1,)
            value = self.sums[number - 1]
            self.arrived(*slots)
            for slot in slots:
                value = value + self.received[slot]
            if number < 4:
                self.sums[number] = value
            else:
                self.total[...] = value
        if number < 3:
            self.start(number)
        elif number == 3:
            for slot in (3, 4, 5):
                self.start(slot)


GRAD_GROUPS = 13
SCATTER_PIECES = ((4, 2), (6, 2), (8, 2), (10, 2), (3, 1), (0, 1), (1, 1), (2, 1), (12, 1))


def backward_kernel(
    rep,
    scale_ref, small_ref, feats_ref, cot_ref, w_in, entry_in, middle_in, qkv_in, probs_in, attn_in, hidden_in, slope_in,
    grad_out, total_out, sums_out, time_out,
    w, gx, dattn, du, hidden, attn, n1t, n2t, gdt, got, dqkv, grads, item_grad, acc, acc_bias,
    r_core, r_dy, r_dx, r_x, r_y, r_z, sums, r_sums, r_time,
    w_sem, in_sem, send, recv, small_send, small_recv, time_send, time_recv,
):
    place = Place(rep)
    t = place.t
    rows = gx.shape[0]
    items = rows // LENGTH
    wide = lambda cols: pl.BlockSpec((LENGTH, cols), lambda i: (i, 0))
    lane = lax.broadcasted_iota(jnp.int32, (1, 128), 1)
    even_mask = jnp.where(lane < HEAD_DIM, 1.0, 0.0).astype(BF16)
    odd_mask = jnp.where(lane < HEAD_DIM, 0.0, 1.0).astype(BF16)
    times = Timeline()

    def load_weights(layer):
        copies = []
        for number, (first, count) in enumerate(((3, 9), (0, 3))):
            copy = pltpu.make_async_copy(
                w_in.at[layer, pl.ds(first, count)], w.at[pl.ds(first, count)], w_sem.at[layer, number]
            )
            copies.append(copy)
        return copies

    def load_stash(layer):
        return [
            pltpu.make_async_copy(hidden_in.at[layer], hidden, in_sem.at[layer, 0]),
            pltpu.make_async_copy(attn_in.at[layer], attn, in_sem.at[layer, 1]),
        ]

    def norm_back(hat, inverse, dy, layer, row, here):
        acc[row] += fold_rows(dy * hat)
        acc[row + 1] += fold_rows(dy)
        scaled = dy * small_ref[layer * 5 + row : layer * 5 + row + 1]
        mean = jnp.mean(scaled, -1, keepdims=True)
        along = jnp.mean(scaled * hat, -1, keepdims=True)
        return inverse * (scaled - mean - hat * along)

    def feed_phase(layer):
        last = layer == LAYERS - 1

        def body(item, poll, middle_blk, slope_blk, *rest):
            here = pl.ds(pl.multiple_of(item * LENGTH, LENGTH), LENGTH)
            if last:
                grad = rest[0][...].astype(F32) * scale_ref[t * items + item]
            else:
                grad = gx[here]
            acc[4] += fold_rows(grad)
            low = grad.astype(BF16)
            gdt[:, here] = low.T
            lift = lambda part: nn(low, weight(w, 5 + 2 * part))
            lower = lambda part, value: nt(value, weight(w, 4 + 2 * part))
            back, ahead, held = jnp.zeros((LENGTH, 512), F32), lift(0), None
            for part in range(4):
                span = slice(part * 512, (part + 1) * 512)
                dh = ahead
                if part == 2:
                    poll(1)
                if part < 3:
                    ahead = lift(part + 1)
                pre_grad = (dh * slope_blk[:, span].astype(F32)).astype(BF16)
                du[here, span] = pre_grad
                acc_bias[part] += fold_rows(pre_grad.astype(F32))
                if held is not None:
                    back = back + lower(part - 1, held)
                held = pre_grad
            back = back + lower(3, held)
            hat, inverse = normalize(middle_blk[...])
            normed = hat * small_ref[layer * 5 + 2 : layer * 5 + 3] + small_ref[layer * 5 + 3 : layer * 5 + 4]
            n2t[:, here] = normed.astype(BF16).T
            grad = grad + norm_back(hat, inverse, back, layer, 2, here)
            gx[here] = grad
            low = grad.astype(BF16)
            got[:, here] = low.T
            dattn[here] = nn(low, weight(w, 3)).astype(BF16)

        each_item(
            body, [[times.slot(FEED_BACK / 2) for _ in range(2)] for _ in range(items)], items, [wide(512), wide(2048)] + ([wide(512)] if last else []), [],
            [middle_in.at[layer], slope_in.at[layer]] + ([cot_ref] if last else []),
        )

    def attention_phase(layer):
        def body(item, poll, entry_blk, qkv_blk, probs_blk, *rest):
            here = pl.ds(pl.multiple_of(item * LENGTH, LENGTH), LENGTH)
            def sides(pair):
                query = qkv_blk[:, pair * 128 : (pair + 1) * 128]
                key = qkv_blk[:, 512 + pair * 128 : 512 + (pair + 1) * 128]
                value = qkv_blk[:, 1024 + pair * 128 : 1024 + (pair + 1) * 128]
                back = dattn[here, pair * 128 : (pair + 1) * 128]
                split = lambda v: [v * even_mask, v * odd_mask]
                return split(query), split(key), value, split(back)

            def scores(pair):
                _, _, value, back = sides(pair)
                return [nt(side, value) for side in back]

            def products(pair, dscores):
                query, key, _, back = sides(pair)
                probs = [probs_blk[0, pair * 2 + side] for side in range(2)]
                tall = jnp.concatenate(dscores, 0)
                dq = nn(jnp.concatenate(dscores, 1), jnp.concatenate(key, 0)) * HEAD_DIM**-0.5
                dk = tn(tall, jnp.concatenate(query, 0))
                dv = tn(jnp.concatenate(probs, 0), jnp.concatenate(back, 0))
                for slot, value in enumerate((dq, dk, dv)):
                    dqkv[here, slot * 512 + pair * 128 : slot * 512 + (pair + 1) * 128] = value.astype(BF16)

            ahead, held = scores(0), None
            for pair in range(4):
                both = ahead
                if pair > 0:
                    poll(pair)
                if pair < 3:
                    ahead = scores(pair + 1)
                dscores = []
                for side in range(2):
                    probs = probs_blk[0, pair * 2 + side].astype(F32)
                    mixed = probs * both[side]
                    dscores.append((mixed - probs * jnp.sum(mixed, -1, keepdims=True)).astype(BF16))
                if held is not None:
                    products(pair - 1, held)
                held = dscores
            products(3, held)
            back = jnp.zeros((LENGTH, 512), F32)
            for slot in range(3):
                back = back + nt(dqkv[here, slot * 512 : (slot + 1) * 512], weight(w, slot))
            hat, inverse = normalize(entry_blk[...])
            normed = hat * small_ref[layer * 5 : layer * 5 + 1] + small_ref[layer * 5 + 1 : layer * 5 + 2]
            n1t[:, here] = normed.astype(BF16).T
            grad = gx[here] + norm_back(hat, inverse, back, layer, 0, here)
            item_grad[pl.ds(item, 1)] = jnp.sum(grad, 0, keepdims=True)
            if layer == 0:
                rest[0][...] = grad.astype(BF16)
            else:
                gx[here] = grad

        slots = [[times.slot(ATTENTION_BACK / 4) for _ in range(4)] for _ in range(items)]
        each_item(
            body, slots, items,
            [wide(512), wide(1536), pl.BlockSpec((1, 8, 256, 256), lambda i: (i, 0, 0, 0))],
            [wide(512)] if layer == 0 else [],
            [entry_in.at[layer], qkv_in.at[layer], probs_in.at[layer]] + ([grad_out] if layer == 0 else []),
        )

    def keep_grad(group, value):
        for half in range(2):
            grads[group, half] = value[:, half * 256 : (half + 1) * 256].astype(BF16).reshape(4, 4, 32, 256)

    def weight_grad(left, right, group, part):
        keep_grad(group, nn(left[...], right[:, part * 512 : (part + 1) * 512]))

    scatters, smalls = [], []
    for layer in range(LAYERS):
        received = [r.at[layer] for r in (r_core, r_dy, r_dx, r_x, r_y, r_z)]
        scatters.append(
            [
                Scatter(place, grads, received, total_out.at[layer], groups, send.at[layer, i], recv.at[layer, i])
                for i, groups in enumerate(SCATTER_PIECES)
            ]
        )
        smalls.append(
            SmallSum(place, sums.at[layer], r_sums.at[layer], sums_out.at[layer], small_send.at[layer], small_recv.at[layer])
        )

    order = [LAYERS - 1 - i for i in range(LAYERS)]
    weights = {order[0]: load_weights(order[0])}
    stash = {order[0]: load_stash(order[0])}
    for copy in weights[order[0]] + stash[order[0]]:
        copy.start()
    item_grad[...] = jnp.zeros(item_grad.shape, F32)
    place.greet()

    def clear(layer, piece):
        if layer != order[0]:
            before = scatters[order[order.index(layer) - 1]][scatters[layer].index(piece)]
            play(times.force((before, 4)))
            before.finish()

    def begin(piece):
        piece.step(0)
        times.scatter(piece, UNIT * piece.count)

    for turn, layer in enumerate(order):
        feed_pieces, late_pieces = scatters[layer][:5], scatters[layer][5:]
        acc[...] = jnp.zeros(acc.shape, F32)
        acc_bias[...] = jnp.zeros(acc_bias.shape, F32)
        weights[layer][0].wait()
        feed_phase(layer)
        stash[layer][0].wait()
        stash[layer][1].wait()
        weights[layer][1].wait()
        for part, piece in enumerate(feed_pieces):
            clear(layer, piece)
            if part < 4:
                weight_grad(n2t, du, 4 + 2 * part, part)
                weight_grad(gdt, hidden, 5 + 2 * part, part)
            else:
                weight_grad(got, attn, 3, 0)
            times.passed(GRAD * piece.count)
            begin(piece)
            play(times.slot(0.0))
        attention_phase(layer)
        if turn + 1 < LAYERS:
            after = order[turn + 1]
            weights[after] = load_weights(after)
            stash[after] = load_stash(after)
            for copy in weights[after] + stash[after]:
                copy.start()
        for piece in late_pieces:
            clear(layer, piece)
        spread = lax.dot_general(
            feats_ref[...], item_grad[...], (((0,), (0,)), ((), ())),
            precision=lax.Precision.HIGHEST, preferred_element_type=F32,
        )
        keep_grad(12, spread)
        begin(late_pieces[3])
        for row in range(5):
            sums[layer, 0, row : row + 1] = jnp.sum(acc[row], 0, keepdims=True)
        for part in range(4):
            sums[layer, 0, 5 + part : 6 + part] = jnp.sum(acc_bias[part], 0, keepdims=True)
        sums[layer, 0, 9:16] = jnp.zeros((7, 512), F32)
        smalls[layer].step(0)
        times.small(smalls[layer])
        for slot in range(3):
            weight_grad(n1t, dqkv, slot, slot)
            times.passed(GRAD)
            begin(late_pieces[slot])
            play(times.slot(0.0))
    play(times.force(*[(piece, 4) for layer in range(LAYERS) for piece in scatters[layer] + [smalls[layer]]]))

    swaps = []
    for layer in range(LAYERS):
        swap = pltpu.make_async_remote_copy(
            src_ref=total_out.at[layer, 12, pl.ds(pl.multiple_of((1 - t) * 16, 16), 16)],
            dst_ref=r_time.at[layer], send_sem=time_send.at[layer], recv_sem=time_recv.at[layer],
            device_id=place.device(place.z, place.yx, 1 - t), device_id_type=MESH,
        )
        swap.start()
        swaps.append(swap)
    for layer in range(LAYERS):
        swaps[layer].wait()
        time_out[layer, :, place.cols] = total_out[layer, 12, pl.ds(pl.multiple_of(t * 16, 16), 16)]
        time_out[layer, :, place.other_cols] = r_time[layer]
    for piece in scatters[order[-1]]:
        piece.finish()
    for piece in smalls:
        piece.finish()


def backward_call(rep, rows, scale, small, feats, cot, w, entry, middle, qkv, probs, attn, hidden, slope):
    items = rows // LENGTH
    hbm = pl.BlockSpec(memory_space=pl.ANY)
    vmem = pl.BlockSpec(memory_space=pltpu.VMEM)
    smem = pl.BlockSpec(memory_space=pltpu.SMEM)
    shape = jax.ShapeDtypeStruct
    pieces = len(SCATTER_PIECES)
    dma = pltpu.SemaphoreType.DMA
    return pl.pallas_call(
        functools.partial(backward_kernel, rep),
        name="backward",
        in_specs=[smem, vmem, vmem] + [hbm] * 9,
        out_shape=[
            shape((rows, 512), BF16),
            shape((LAYERS, GRAD_GROUPS, 32, 256), F32),
            shape((LAYERS, 16, 512), F32),
            shape((LAYERS, 16, 512), F32),
        ],
        out_specs=[hbm, vmem, vmem, vmem],
        scratch_shapes=[
            pltpu.VMEM((12, 2, 4, 4, 32, 256), BF16),
            pltpu.VMEM((rows, 512), F32),
            pltpu.VMEM((rows, 512), BF16),
            pltpu.VMEM((rows, 2048), BF16),
            pltpu.VMEM((rows, 2048), BF16),
            pltpu.VMEM((rows, 512), BF16),
            pltpu.VMEM((512, rows), BF16),
            pltpu.VMEM((512, rows), BF16),
            pltpu.VMEM((512, rows), BF16),
            pltpu.VMEM((512, rows), BF16),
            pltpu.VMEM((rows, 1536), BF16),
            pltpu.VMEM((GRAD_GROUPS, 2, 4, 4, 32, 256), BF16),
            pltpu.VMEM((8, 512), F32),
            pltpu.VMEM((5, 8, 512), F32),
            pltpu.VMEM((4, 8, 512), F32),
            pltpu.VMEM((LAYERS, GRAD_GROUPS, 4, 4, 32, 256), BF16),
            pltpu.VMEM((LAYERS, GRAD_GROUPS, 2, 32, 256), BF16),
            pltpu.VMEM((LAYERS, GRAD_GROUPS, 2, 32, 256), BF16),
            pltpu.VMEM((LAYERS, GRAD_GROUPS, 4, 32, 256), BF16),
            pltpu.VMEM((LAYERS, GRAD_GROUPS, 4, 32, 256), BF16),
            pltpu.VMEM((LAYERS, 3, GRAD_GROUPS, 32, 256), BF16),
            pltpu.VMEM((LAYERS, 4, 16, 512), F32),
            pltpu.VMEM((LAYERS, 6, 16, 512), F32),
            pltpu.VMEM((LAYERS, 16, 256), F32),
            dma((LAYERS, 2)),
            dma((LAYERS, 2)),
            dma((LAYERS, pieces, 10)),
            dma((LAYERS, pieces, 10)),
            dma((LAYERS, 6)),
            dma((LAYERS, 6)),
            dma((LAYERS,)),
            dma((LAYERS,)),
        ],
        compiler_params=pltpu.CompilerParams(collective_id=2, has_side_effects=True, vmem_limit_bytes=62 << 20),
    )(scale, small, feats, cot, w, entry, middle, qkv, probs, attn, hidden, slope)


def adamw(weight, gradient, first_moment, second_moment, rate):
    first_new = beta_first * first_moment + (1.0 - beta_first) * gradient
    second_new = beta_second * second_moment + (1.0 - beta_second) * gradient * gradient
    first_corr = first_new * (1.0 / (1.0 - beta_first**STEP))
    second_corr = second_new * (1.0 / (1.0 - beta_second**STEP))
    weight_new = weight - rate * (first_corr / (jnp.sqrt(second_corr) + adam_eps) + weight_decay * weight)
    return (weight_new, first_new, second_new)


def update_kernel(*refs):
    hbm, outs, ins = refs[:26], refs[26:50], refs[50:74]
    row, *passing, sems = refs[74:]
    copies = [pltpu.make_async_copy(src, dst, sems.at[i]) for i, (src, dst) in enumerate(zip(hbm[:24], ins))]
    copies += [pltpu.make_async_copy(hbm[24 + i], passing[i], sems.at[24 + i]) for i in range(2)]
    leaving = [pltpu.make_async_copy(passing[i], outs[i], sems.at[26 + i]) for i in range(2)]
    for copy in copies:
        copy.start()
    for copy in copies:
        copy.wait()
    for copy in leaving:
        copy.start()
    total, sums, time_grad, *ins = ins
    outs = outs[2:]
    qkv, out, up, bias, down, norm, time = [ins[i * 3 : i * 3 + 3] for i in range(7)]
    qkv_new, key_second, value_second = outs[0:2], outs[2], outs[3]
    out_new, up_new, bias_new, down_new, norm_new, time_new = [outs[4 + i * 3 : 7 + i * 3] for i in range(6)]
    dp, t = lax.axis_index("dp"), lax.axis_index("tensor")

    def one(old, new, where, gradient, rate):
        values = adamw(old[0][where], gradient, old[1][where], old[2][where], rate)
        for ref, value in zip(new, values):
            ref[where] = value
        return values

    for layer in range(LAYERS):
        for slot in range(3):
            values = adamw(qkv[0][layer, slot], total[layer, slot], qkv[1][layer, slot], qkv[2][layer, slot], learn_rate)
            for ref, value in zip(qkv_new, values):
                ref[layer, slot] = value
            if slot < 2:
                key_second[layer, :, slot] = values[2]
            else:
                value_second[layer] = values[2]
        one(out, out_new, (layer,), total[layer, 3], learn_rate)
        for part in range(4):
            where = (layer, slice(None), slice(part * 256, (part + 1) * 256))
            one(up, up_new, where, total[layer, 4 + 2 * part], learn_rate)
            one(down, down_new, where, total[layer, 5 + 2 * part], learn_rate)
        one(time, time_new, (layer,), time_grad[layer], learn_rate)

        width = norm[0].shape[2]
        start = (dp * 2 + t) * width
        tile = sums[layer, :, pl.ds(pl.multiple_of(start // 128 * 128, 128), 128)]
        mine = pltpu.roll(tile, (128 - start % 128) % 128, 1)[0:5, 0:width]
        one(norm, norm_new, (slice(None), layer), mine, norm_rate)
        for part in range(4):
            for half in range(2):
                span = pl.ds(pl.multiple_of(t * 256 + half * 128, 128), 128)
                row[part * 2 + half : part * 2 + half + 1] = sums[layer, 5 + part : 6 + part, span]
        width = bias[0].shape[2]
        mine = pltpu.roll(row[...], (128 - dp * width) % 128, 1)[:, 0:width]
        one(bias, bias_new, (layer,), mine, learn_rate)
    for copy in leaving:
        copy.wait()


def update_call(total, sums, time_grad, states, row_results):
    flat = [total, sums, time_grad] + [array for state in states for array in state]
    like = lambda array: jax.ShapeDtypeStruct(array.shape, array.dtype)
    rows = states[0][0].shape[2]
    shapes = [like(array) for array in list(row_results) + flat[3:]]
    shapes[4:5] = [
        jax.ShapeDtypeStruct((LAYERS, rows, 2, 256), F32),
        jax.ShapeDtypeStruct((LAYERS, rows, 256), F32),
    ]
    vmem = pl.BlockSpec(memory_space=pltpu.VMEM)
    hbm = pl.BlockSpec(memory_space=pl.ANY)
    return pl.pallas_call(
        update_kernel,
        name="update",
        in_specs=[hbm] * 26,
        out_shape=shapes,
        out_specs=[hbm] * 2 + [vmem] * 22,
        scratch_shapes=[pltpu.VMEM(array.shape, F32) for array in flat]
        + [pltpu.VMEM((8, 128), F32)]
        + [pltpu.VMEM(array.shape, array.dtype) for array in row_results]
        + [pltpu.SemaphoreType.DMA((28,))],
        compiler_params=pltpu.CompilerParams(vmem_limit_bytes=56 << 20),
    )(*flat, *row_results)


def per_device(
    rep,
    inputs, cotangent, timesteps, item_scale,
    qkv_weight, qkv_first, qkv_second,
    out_weight, out_first, out_second,
    up_weight, up_first, up_second,
    up_bias, bias_first, bias_second,
    down_weight, down_first, down_second,
    norm_params, norm_first, norm_second,
    time_weight, time_first, time_second,
):
    rows = inputs.shape[0]
    dp, t = lax.axis_index("dp"), lax.axis_index("tensor")
    qkv, out, up, down, bias = qkv_weight, out_weight, up_weight, down_weight, up_bias
    norm, time = norm_params, time_weight
    teams = None
    if rep > 1:
        size = GROUPS * rep
        teams = [[g * rep + j for j in range(rep)] for g in range(GROUPS)]
        pairs = [[g * rep * 2 + j for j in range(rep * 2)] for g in range(GROUPS)]
        join = lambda v, axis: lax.all_gather(v, "dp", axis=axis, axis_index_groups=teams, tiled=True)
        join_both = lambda v, axis: lax.all_gather(
            v, ("dp", "tensor"), axis=axis, axis_index_groups=pairs, tiled=True
        )
        qkv, out, up, down, bias = join(qkv, 1), join(out, 2), join(up, 1), join(down, 2), join(bias, 2)
        norm, time = join_both(norm, 2), join_both(time, 1)
        norm = lax.dynamic_slice_in_dim(norm, t * 16, 16, 2)
        time = lax.dynamic_slice_in_dim(time, t * 16, 16, 1)

    slots = lambda *arrays: [jnp.transpose(v, (0, 2, 1, 3)) for v in arrays]
    flip = lambda *arrays: [jnp.swapaxes(v, 1, 2) for v in arrays]
    front = lambda *arrays: [jnp.swapaxes(v, 0, 1) for v in arrays]
    w, small, feats, entry, middle, qkv_rows, probs, attn, hidden, slope, activations = forward_call(
        rep, rows, timesteps, inputs, *slots(qkv), *flip(out), up, *flip(down), time, *front(norm), bias
    )
    input_grad, total, sums, time_grad = backward_call(
        rep, rows, item_scale, small, feats, cotangent, w, entry, middle, qkv_rows, probs, attn, hidden, slope
    )

    if rep > 1:
        total = lax.psum_scatter(total, "dp", scatter_dimension=2, axis_index_groups=teams, tiled=True)
        sums, time_grad = lax.psum((sums, time_grad), "dp", axis_index_groups=teams)
        time_grad = lax.all_gather(time_grad, "tensor", axis=1, tiled=True)
        width = time_weight.shape[1]
        time_grad = lax.dynamic_slice_in_dim(time_grad, ((dp % rep) * 2 + t) * width, width, 1)

    activations, input_grad, *new = update_call(
        total, sums, time_grad,
        [
            slots(qkv_weight, qkv_first, qkv_second),
            flip(out_weight, out_first, out_second),
            [up_weight, up_first, up_second],
            [up_bias, bias_first, bias_second],
            flip(down_weight, down_first, down_second),
            front(norm_params, norm_first, norm_second),
            [time_weight, time_first, time_second],
        ],
        (activations, input_grad),
    )
    return (
        activations, input_grad,
        *slots(*new[0:2]), new[2], new[3],
        *flip(*new[4:7]), *new[7:10], *new[10:13], *flip(*new[13:16]), *front(*new[16:19]), *new[19:22],
    )


def solution(mesh):
    rep = mesh.shape["dp"] // GROUPS
    shard = P(None, "dp", None, "tensor")
    rows = P(("dp", "tensor"), None)
    trans = P(None, "tensor", "dp")
    flat = P(None, "dp", "tensor")
    norm = P(None, None, ("dp", "tensor"))
    time = P(None, ("dp", "tensor"), None)
    return jax.shard_map(
        functools.partial(per_device, rep),
        mesh=mesh,
        in_specs=(rows, rows, P("dp"), P("dp")) + (shard,) * 3 + (trans,) * 3 + (flat,) * 3 + (trans,) * 6 + (norm,) * 3 + (time,) * 3,
        out_specs=(rows, rows, shard, shard, shard, flat) + (trans,) * 3 + (flat,) * 3 + (trans,) * 6 + (norm,) * 3 + (time,) * 3,
        check_vma=False,
    )
```
